256 devices in a mesh: batch: 8 (over z), ctx: 32 (over x, y, core).
Axes of the slice: x: 4, y: 4, z: 8, core: 2. Of those that a mesh axis runs over, the one named last changes fastest.
Arguments:
- latent_cache: bfloat16 [64, 32768, 576], P('batch', 'ctx'), parts along dimension 0, may hold values from -8 to 8
- queries: bfloat16 [64, 4, 64, 576], P('batch', None, 'ctx'), parts along dimension 0, may hold values from -60 to 60
- lengths: int32 [64], P('batch'), parts along dimension 0, may hold values from 8192 to 32768, as said below
- positions: int32 [64], P('batch'), parts along dimension 0, may hold values from 0 to 32767
- value_up: bfloat16 [64, 512, 128], P('ctx'), may hold values from -0.25 to 0.25
- out_proj: bfloat16 [8192, 7168], P('ctx'), may hold values from -0.25 to 0.25
Outputs:
- attended: bfloat16 [64, 4, 7168], P('batch', None, 'ctx'), parts along dimension 0
The draws below stay inside these ranges and needn't reach their ends.
There are 8 independent parts, one for each index of `batch`. The reference program is written for one: setup_inputs(seed, part) draws one part's arguments, and reference() takes and returns one part's arrays. A program takes and returns all parts, laid end to end along the dimension named above; an argument that names none is the same for every part. Nothing has to cross between parts.
Inputs may be any that keep to these rules, and one draw needn't show every extreme that they name: `lengths`: one row of every part has the full length 32768.
All inputs are finite; a program needn't handle non-finite values.
Results may differ from the reference program's by a relative error of at most 0.018.
Values may be sent and summed in bfloat16 or wider, within the bound.
No kernel may reach another device: no remote copies, remote signals or barrier semaphores. Data moves between devices by JAX's collectives and lax.ppermute only.
A program may use at most 320 MiB of HBM per device.

```python
import jax
import jax.numpy as jnp
from jax import lax

D = 7168
H = 64
KVL = 512
ROPE = 64
NOPE = 128
VD = 128
ROWS = 8
NEW_TOK = 4
CTX_DEV = 1024
CONTEXT = 32768
N_CTX = 32


def shared_anchors(key):
    signs = jax.random.randint(jax.random.fold_in(key, 101), (ROWS, KVL + ROPE), 0, 2)
    first = (2 * signs - 1).astype(jnp.float32)
    column = jnp.arange(KVL + ROPE, dtype=jnp.int32)[None, :]
    shrink = jnp.where(column < KVL // 2, 63.0 / 64.0, 1.0)
    second = first * shrink
    return (first, second)


def draw_lengths_from(key):
    key = jax.random.fold_in(key, 11)
    values = jax.random.randint(key, (ROWS,), CONTEXT // 4, CONTEXT + 1)
    longest = jax.random.randint(jax.random.fold_in(key, 1), (), 0, ROWS)
    return jnp.where(jnp.arange(ROWS, dtype=jnp.int32) == longest, CONTEXT, values).astype(jnp.int32)


def draw_latent_cache(key, part):
    first, second = shared_anchors(key)
    row_lengths = draw_lengths_from(key)
    key = jax.random.fold_in(key, 3)
    shape = (ROWS, CONTEXT, KVL + ROPE)
    base = jnp.clip(jax.random.normal(key, shape, jnp.float32), -6.0, 6.0)
    visible_end = row_lengths - NEW_TOK + 1
    half_end = visible_end // 2
    spot_first = jax.random.randint(jax.random.fold_in(key, 7), (ROWS,), 0, half_end)
    spot_second = half_end + jax.random.randint(jax.random.fold_in(key, 8), (ROWS,), 0, half_end)
    place = jnp.arange(CONTEXT, dtype=jnp.int32)[None, :]
    base = jnp.where((place == spot_first[:, None])[..., None], first[:, None, :], base)
    base = jnp.where((place == spot_second[:, None])[..., None], second[:, None, :], base)
    return base.astype(jnp.bfloat16)


def draw_queries(key, part):
    first, second = shared_anchors(key)
    key = jax.random.fold_in(key, 5)
    shape = (ROWS, NEW_TOK, H, KVL + ROPE)
    base = jnp.clip(1.5 * jax.random.normal(key, shape, jnp.float32), -9.0, 9.0)
    head_pick = jax.random.randint(jax.random.fold_in(key, 9), (ROWS,), 0, H)
    target = 130.0 + 200.0 * jnp.arange(ROWS, dtype=jnp.float32) / max(ROWS - 1, 1)
    strength = target * (NOPE + ROPE) ** 0.5 / KVL
    column = jnp.arange(KVL + ROPE, dtype=jnp.int32)[None, :]
    aligned = jnp.where(column < KVL, strength[:, None] * first, 0.0)
    chosen = jnp.arange(H, dtype=jnp.int32)[None, :] == head_pick[:, None]
    base = jnp.where(chosen[:, None, :, None], aligned[:, None, None, :], base)
    return base.astype(jnp.bfloat16)


def draw_lengths(key, part):
    return draw_lengths_from(key)


def with_ends(values, key, least, high):
    longest = values.shape.index(max(values.shape))
    spots = []
    for shift in (0, 1):
        where = [jax.random.randint(jax.random.fold_in(key, axis), (), 0, length) for axis, length in enumerate(values.shape)]
        where[longest] = (where[longest] + shift) % values.shape[longest]
        spots.append(tuple(where))
    return values.at[spots[0]].set(least).at[spots[1]].set(high)


def levels(key, shape, pieces, smallest, high):
    level, own = 1.0, jax.random.fold_in(key, 6)
    for axis_at, parts in pieces:
        steps = jnp.exp(jax.random.uniform(jax.random.fold_in(own, axis_at), (parts,), jnp.float32, smallest / len(pieces), high / len(pieces)))
        level = level * jnp.repeat(steps, shape[axis_at] // parts).reshape([-1 if axis == axis_at else 1 for axis in range(len(shape))])
    return level


def gaussian(stream_key, shape, width, bound, shards=(), held_as=jnp.bfloat16):
    values = width * jax.random.normal(stream_key, shape, jnp.float32)
    if shards:
        values = values * levels(stream_key, shape, shards, -0.22, 0.18)
    return jnp.clip(values, -bound, bound).astype(held_as)


def setup_inputs(seed: int = 0, part: int = 0) -> dict:
    arg_keys = jax.random.split(jax.random.key(seed), 7)
    part_keys = jax.random.split(jax.random.fold_in(arg_keys[6], part), 7)
    return {
        "latent_cache": draw_latent_cache(jax.random.fold_in(jax.random.fold_in(arg_keys[6], part), 71), part),
        "queries": draw_queries(jax.random.fold_in(jax.random.fold_in(arg_keys[6], part), 71), part),
        "lengths": draw_lengths(jax.random.fold_in(jax.random.fold_in(arg_keys[6], part), 71), part),
        "positions": with_ends(jax.random.randint(part_keys[3], (ROWS,), 0, CONTEXT), jax.random.fold_in(part_keys[3], 1), 0, CONTEXT - 1).astype(jnp.int32),
        "value_up": gaussian(arg_keys[4], (H, KVL, VD), KVL ** -0.5, 0.25, ((0, 32),)),
        "out_proj": gaussian(arg_keys[5], (H * VD, D), (H * VD // 16) ** -0.5, 0.25, ((0, 32),)),
    }


def rotate(queries, positions, latent_width):
    half_rope = (queries.shape[-1] - latent_width) // 2
    new_count = queries.shape[1]
    exponent = jnp.arange(half_rope, dtype=jnp.float32) * (-2.0 / (2 * half_rope))
    frequency = jnp.power(jnp.float32(50000.0), exponent)
    token_place = positions[:, None] + jnp.arange(new_count, dtype=jnp.int32)[None, :]
    angles = token_place.astype(jnp.float32)[:, :, None, None] * frequency
    cosine = jnp.cos(angles)
    sine_term = jnp.sin(angles)
    latent = queries[..., :latent_width].astype(jnp.float32)
    first_half = queries[..., latent_width:latent_width + half_rope].astype(jnp.float32)
    second_half = queries[..., latent_width + half_rope:].astype(jnp.float32)
    turned = jnp.concatenate([latent, first_half * cosine - second_half * sine_term,
                              second_half * cosine + first_half * sine_term], axis=-1)
    return turned.astype(jnp.bfloat16)


def visibility(lengths, first_index, span, new_count):
    token_index = first_index + jnp.arange(span, dtype=jnp.int32)
    limit = lengths[:, None] - new_count + 1 + jnp.arange(new_count, dtype=jnp.int32)[None, :]
    return (token_index[None, None, :] < limit[:, :, None])[:, :, None, :]


def block_terms(turned, latent_cache, lengths, block_index):
    start = (block_index * CTX_DEV).astype(jnp.int32)
    cache_block = lax.dynamic_slice_in_dim(latent_cache, start, CTX_DEV, 1)
    visible = visibility(lengths, start, CTX_DEV, NEW_TOK)
    score_scale = (NOPE + ROPE) ** -0.5
    scores = jnp.einsum('bqhc,btc->bqht', turned.astype(jnp.float32), cache_block.astype(jnp.float32)) * score_scale
    scores = jnp.where(visible, scores, -1e30)
    block_max = jnp.max(scores, axis=-1)
    weights = jnp.where(visible, jnp.exp(scores - block_max[..., None]), 0.0)
    block_sum = jnp.sum(weights, axis=-1)
    rounded = weights.astype(jnp.bfloat16)
    block_out = jnp.einsum('bqht,btc->bqhc', rounded.astype(jnp.float32),
                           cache_block[:, :, :KVL].astype(jnp.float32))
    return block_max, block_sum, block_out


def reference(latent_cache, queries, lengths, positions, value_up, out_proj):
    turned = rotate(queries, positions, KVL)
    maxima, totals, outputs = lax.map(lambda index: block_terms(turned, latent_cache, lengths, index),
                                      jnp.arange(N_CTX, dtype=jnp.int32))
    top = jnp.max(maxima, axis=0)
    factor = jnp.exp(maxima - top[None])
    total = jnp.sum(factor * totals, axis=0)
    summed = jnp.sum(factor[..., None] * outputs, axis=0)
    latent_heads = (summed / total[..., None]).astype(jnp.bfloat16)
    head_values = jnp.einsum('bqhc,hcv->bqhv', latent_heads.astype(jnp.float32),
                             value_up.astype(jnp.float32)).astype(jnp.bfloat16)
    flat = head_values.reshape(ROWS * NEW_TOK, H * VD)
    attended = jnp.dot(flat, out_proj, preferred_element_type=jnp.float32).astype(jnp.bfloat16)
    return attended.reshape(ROWS, NEW_TOK, D)
```

```python
import functools
import math

import jax
import jax.numpy as jnp
from jax import lax
from jax.experimental import pallas as pl
from jax.experimental.pallas import tpu as pltpu
from jax.sharding import PartitionSpec as P

ROPE = 64
NOPE = 128
LANES = 128
POWER = math.log2(math.e) / math.sqrt(NOPE + ROPE)
HIDDEN = -1e30
LEAST = -1e29


def angle_terms(positions, new_count, repeats):
    half_rope = ROPE // 2
    exponent = jnp.arange(half_rope, dtype=jnp.float32) * (-2.0 / ROPE)
    frequency = jnp.power(jnp.float32(50000.0), exponent)
    token_place = positions[:, None] + jnp.arange(new_count, dtype=jnp.int32)[None, :]
    angles = token_place.astype(jnp.float32)[:, :, None] * frequency
    cosine, sine = jnp.cos(angles), jnp.sin(angles)
    cosines = jnp.concatenate([cosine, cosine], axis=-1)
    sines = jnp.concatenate([-sine, sine], axis=-1)
    return jnp.tile(cosines, (1, repeats, 1)), jnp.tile(sines, (1, repeats, 1))


def split_stat(value, lane):
    high = value.astype(jnp.bfloat16).astype(jnp.float32)
    rest = value - high
    middle = rest.astype(jnp.bfloat16).astype(jnp.float32)
    low = rest - middle
    spot = lane % (LANES // 2)
    return jnp.where(spot == 0, high, jnp.where(spot == 1, middle, low))


def join_stat(tile, pair):
    at = pair * (LANES // 2)
    return tile[..., at : at + 1] + tile[..., at + 1 : at + 2] + tile[..., at + 2 : at + 3]


def attend_kernel(half_ref, first_ref, lengths_ref, cache_ref, query_ref, cos_ref, sin_ref, out_ref, *, new_count):
    pair = pl.program_id(0)
    peers, sixteen, full = query_ref.shape
    group = sixteen // 2
    latent = full - ROPE
    count = peers * group
    context = cache_ref.shape[1]
    column_groups = latent // LANES
    gathered = query_ref[...].astype(jnp.float32)
    place = first_ref[0] + lax.broadcasted_iota(jnp.int32, (count, context), 1)
    token = lax.broadcasted_iota(jnp.int32, (count, context), 0) % new_count
    outs, stats = [], []
    for row in range(2):
        query = gathered[:, row * group : (row + 1) * group, :]
        rope = query[:, :, latent:]
        swapped = jnp.concatenate([rope[:, :, ROPE // 2 :], rope[:, :, : ROPE // 2]], axis=-1)
        turned = rope * cos_ref[row][None] + swapped * sin_ref[row][None]
        query = jnp.concatenate([query[:, :, :latent], turned], axis=-1)
        query = query.reshape(count, full).astype(jnp.bfloat16)
        keys = cache_ref[row]
        scores = lax.dot_general(query, keys, (((1,), (1,)), ((), ())), preferred_element_type=jnp.float32)
        length = lengths_ref[half_ref[0] * 4 + pair * 2 + row]
        scores = jnp.where(place < length - new_count + 1 + token, scores, HIDDEN)
        top = jnp.maximum(jnp.max(scores, axis=-1, keepdims=True), LEAST)
        weights = jnp.exp2((scores - top) * POWER)
        total = jnp.sum(weights, axis=-1, keepdims=True)
        out = jnp.dot(weights.astype(jnp.bfloat16), keys[:, :latent], preferred_element_type=jnp.float32)
        seen = total > 0.0
        safe = jnp.where(seen, total, 1.0)
        out = out * (1.0 / safe)
        stat = jnp.where(seen, top * POWER + jnp.log2(safe), HIDDEN)
        outs.append(out.reshape(peers, group, latent))
        stats.append(jnp.broadcast_to(stat, (count, LANES)).reshape(peers, group, LANES))
    both = jnp.concatenate(outs, axis=1).astype(jnp.bfloat16)
    for g in range(column_groups):
        at = pl.multiple_of(g * 2 * sixteen + pair * sixteen, sixteen)
        out_ref[:, pl.ds(at, sixteen), :] = both[:, :, g * LANES : (g + 1) * LANES]
    stat = jnp.concatenate(stats, axis=1)
    lane = lax.broadcasted_iota(jnp.int32, stat.shape, 2)
    packed = split_stat(stat, lane).astype(jnp.bfloat16)
    at = column_groups * 2 * sixteen

    @pl.when(pair == 0)
    def _():
        out_ref[:, at : at + sixteen, :] = packed

    @pl.when(pair == 1)
    def _():
        out_ref[:, at : at + sixteen, :] = jnp.where(
            lane < LANES // 2, out_ref[:, at : at + sixteen, :].astype(jnp.float32), packed.astype(jnp.float32)
        ).astype(jnp.bfloat16)


def attend(half, first, lengths, cache, query, cosines, sines, new_count):
    peers, depth, full = query.shape
    sixteen = depth // 2
    context = cache.shape[1]
    group = sixteen // 2
    latent = full - ROPE
    rows_out = latent // LANES * depth + sixteen
    count = peers * group
    return pl.pallas_call(
        functools.partial(attend_kernel, new_count=new_count),
        out_shape=jax.ShapeDtypeStruct((peers, rows_out, LANES), jnp.bfloat16),
        grid_spec=pltpu.PrefetchScalarGridSpec(
            num_scalar_prefetch=3,
            grid=(2,),
            in_specs=[
                pl.BlockSpec((2, context, full), lambda p, half, *_: (half[0] * 2 + p, 0, 0)),
                pl.BlockSpec((peers, sixteen, full), lambda p, *_: (0, p, 0)),
                pl.BlockSpec((2, group, ROPE), lambda p, half, *_: (half[0] * 2 + p, 0, 0)),
                pl.BlockSpec((2, group, ROPE), lambda p, half, *_: (half[0] * 2 + p, 0, 0)),
            ],
            out_specs=pl.BlockSpec((peers, rows_out, LANES), lambda p, *_: (0, 0, 0)),
        ),
        compiler_params=pltpu.CompilerParams(vmem_limit_bytes=40 * 1024 * 1024),
        cost_estimate=pl.CostEstimate(
            flops=4 * count * context * (full + latent) * 2,
            bytes_accessed=4 * context * full * 2 + 4 * peers * rows_out * LANES,
            transcendentals=4 * count * context,
        ),
        name="attend",
    )(half, first, lengths, cache, query, cosines, sines)


def merge_kernel(left_ref, right_ref, out_ref):
    rows_out = out_ref.shape[1]
    sixteen = 16
    groups = (rows_out - sixteen) // (2 * sixteen)
    at = rows_out - sixteen
    left_stat = left_ref[:, at:, :].astype(jnp.float32)
    right_stat = right_ref[:, at:, :].astype(jnp.float32)
    lane = lax.broadcasted_iota(jnp.int32, left_stat.shape, 2)
    packed = []
    for pair in range(2):
        left, right = join_stat(left_stat, pair), join_stat(right_stat, pair)
        top = jnp.maximum(left, right)
        left_weight, right_weight = jnp.exp2(left - top), jnp.exp2(right - top)
        total = left_weight + right_weight
        packed.append(split_stat(jnp.broadcast_to(top + jnp.log2(total), left_stat.shape), lane))
        scale = 1.0 / total
        left_weight, right_weight = left_weight * scale, right_weight * scale
        for g in range(groups):
            rows = slice(g * 2 * sixteen + pair * sixteen, g * 2 * sixteen + pair * sixteen + sixteen)
            out_ref[:, rows, :] = (
                left_ref[:, rows, :].astype(jnp.float32) * left_weight
                + right_ref[:, rows, :].astype(jnp.float32) * right_weight
            ).astype(jnp.bfloat16)
    out_ref[:, at:, :] = jnp.where(lane < LANES // 2, packed[0], packed[1]).astype(jnp.bfloat16)


def merge(left, right):
    peers, rows_out, lanes = left.shape
    step = peers // 4
    spec = pl.BlockSpec((step, rows_out, lanes), lambda i: (i, 0, 0))
    return pl.pallas_call(
        merge_kernel,
        out_shape=jax.ShapeDtypeStruct(left.shape, left.dtype),
        grid=(4,),
        in_specs=[spec, spec],
        out_specs=spec,
        compiler_params=pltpu.CompilerParams(vmem_limit_bytes=16 * 1024 * 1024),
        name="merge",
    )(left, right)


def project_kernel(parts_ref, up_ref, proj_ref, out_ref, flat_ref, *, new_count):
    sixteen = 16
    peers, rows_out, lanes = parts_ref.shape
    at = rows_out - sixteen
    groups = at // (2 * sixteen)
    heads, _, width = up_ref.shape

    @pl.when(pl.program_id(0) == 0)
    def _():
        blocks = []
        for half in range(2):
            chosen = [2 * k + 1 - half for k in range(peers // 2)]
            stat_tiles = [parts_ref[k, at:, :].astype(jnp.float32) for k in chosen]
            for pair in range(2):
                stats = [join_stat(tile, pair) for tile in stat_tiles]
                top = functools.reduce(jnp.maximum, stats)
                weights = [jnp.exp2(stat - top) for stat in stats]
                scale = 1.0 / functools.reduce(jnp.add, weights)
                sums = []
                for g in range(groups):
                    start = g * 2 * sixteen + pair * sixteen
                    acc = None
                    for k, weight in zip(chosen, weights):
                        term = parts_ref[k, start : start + sixteen, :].astype(jnp.float32) * weight
                        acc = term if acc is None else acc + term
                    sums.append(acc * scale)
                blocks.append(jnp.concatenate(sums, axis=-1))
        latent = jnp.concatenate(blocks, axis=0).astype(jnp.bfloat16)
        count = latent.shape[0]
        out_row = lax.broadcasted_iota(jnp.int32, (count // heads, count), 0)
        in_row = lax.broadcasted_iota(jnp.int32, (count // heads, count), 1)
        base = (out_row // new_count) * (new_count * heads) + out_row % new_count
        for head in range(heads):
            pick = jnp.where(in_row == base + head * new_count, 1.0, 0.0).astype(jnp.bfloat16)
            own = jnp.dot(pick, latent, preferred_element_type=jnp.float32).astype(jnp.bfloat16)
            values = jnp.dot(own, up_ref[head], preferred_element_type=jnp.float32)
            flat_ref[:, head * width : (head + 1) * width] = values.astype(jnp.bfloat16)

    out_ref[...] = jnp.dot(flat_ref[...], proj_ref[...], preferred_element_type=jnp.float32).astype(jnp.bfloat16)


def project(parts, value_up, out_proj, new_count):
    peers, rows_out, lanes = parts.shape
    heads, latent, width = value_up.shape
    depth, columns = out_proj.shape
    tokens = 32
    steps = 4
    block = columns // steps
    return pl.pallas_call(
        functools.partial(project_kernel, new_count=new_count),
        out_shape=jax.ShapeDtypeStruct((tokens, columns), jnp.bfloat16),
        grid=(steps,),
        in_specs=[
            pl.BlockSpec((peers, rows_out, lanes), lambda i: (0, 0, 0)),
            pl.BlockSpec((heads, latent, width), lambda i: (0, 0, 0)),
            pl.BlockSpec((depth, block), lambda i: (0, i)),
        ],
        out_specs=pl.BlockSpec((tokens, block), lambda i: (0, i)),
        scratch_shapes=[pltpu.VMEM((tokens, depth), jnp.bfloat16)],
        compiler_params=pltpu.CompilerParams(vmem_limit_bytes=24 * 1024 * 1024),
        name="project",
    )(parts, value_up, out_proj)


def body(latent_cache, queries, lengths, positions, value_up, out_proj):
    row_count, context_dev, full = latent_cache.shape
    new_count, heads_dev = queries.shape[1], queries.shape[2]
    shard = lax.axis_index("ctx")
    peers = lax.axis_size("ctx")
    core = shard % 2
    partners = [(i, i ^ 1) for i in range(peers)]
    depth = row_count // 2 * new_count * heads_dev
    own = queries.transpose(0, 2, 1, 3).reshape(1, 2, depth, full)
    own = jnp.broadcast_to(own, (peers // 2, 2, depth, full)).reshape(peers, depth, full)
    here = lax.all_to_all(own, "ctx", 0, 0, tiled=True)
    there = lax.ppermute(here, "ctx", partners)
    cosines, sines = angle_terms(positions, new_count, heads_dev)
    first = (shard * context_dev).astype(jnp.int32).reshape(1)
    core = core.astype(jnp.int32).reshape(1)
    sent = attend(core, first, lengths, latent_cache, here, cosines, sines, new_count)
    came = lax.ppermute(sent, "ctx", partners)
    kept = attend(1 - core, first, lengths, latent_cache, there, cosines, sines, new_count)
    merged = merge(kept, came)
    parts = lax.all_to_all(merged, "ctx", 0, 0, tiled=True)
    terms = project(parts, value_up, out_proj, new_count)
    width = out_proj.shape[1] // peers
    terms = terms.reshape(row_count * new_count, peers, width).transpose(1, 0, 2)
    terms = lax.all_to_all(terms, "ctx", 0, 0, tiled=True)
    result = jnp.sum(terms.astype(jnp.float32), axis=0).astype(jnp.bfloat16)
    return result.reshape(row_count, new_count, width)


def solution(mesh):
    in_specs = (
        P("batch", "ctx", None),
        P("batch", None, "ctx", None),
        P("batch"),
        P("batch"),
        P("ctx", None, None),
        P("ctx", None),
    )
    out_specs = P("batch", None, "ctx")
    return jax.shard_map(body, mesh=mesh, in_specs=in_specs, out_specs=out_specs, check_vma=False)
```

```python
import functools
import math

import jax
import jax.numpy as jnp
from jax import lax
from jax.experimental import pallas as pl
from jax.experimental.pallas import tpu as pltpu
from jax.sharding import PartitionSpec as P

ROPE = 64
NOPE = 128
LANES = 128
POWER = math.log2(math.e) / math.sqrt(NOPE + ROPE)
HIDDEN = -1e30
VMEM_LIMIT = 24 * 1024 * 1024
LEAST = -1e29


def angle_terms(positions, new_count, repeats):
    half_rope = ROPE // 2
    exponent = jnp.arange(half_rope, dtype=jnp.float32) * (-2.0 / ROPE)
    frequency = jnp.power(jnp.float32(50000.0), exponent)
    token_place = positions[:, None] + jnp.arange(new_count, dtype=jnp.int32)[None, :]
    angles = token_place.astype(jnp.float32)[:, :, None] * frequency
    cosine, sine = jnp.cos(angles), jnp.sin(angles)
    cosines = jnp.concatenate([cosine, cosine], axis=-1)
    sines = jnp.concatenate([-sine, sine], axis=-1)
    return jnp.tile(cosines, (1, repeats, 1)), jnp.tile(sines, (1, repeats, 1))


def split_stat(value, lane):
    high = value.astype(jnp.bfloat16).astype(jnp.float32)
    rest = value - high
    middle = rest.astype(jnp.bfloat16).astype(jnp.float32)
    low = rest - middle
    spot = lane % (LANES // 2)
    return jnp.where(spot == 0, high, jnp.where(spot == 1, middle, low))


def join_stat(tile, pair):
    at = pair * (LANES // 2)
    return tile[..., at : at + 1] + tile[..., at + 1 : at + 2] + tile[..., at + 2 : at + 3]


def attend_kernel(scalars_ref, lengths_ref, own_ref, came_ref, query_ref, cos_ref, sin_ref, out_ref, kept_ref, *, new_count):
    row = pl.program_id(0)
    peers, sixteen, full = query_ref.shape
    group = sixteen // 2
    latent = full - ROPE
    count = peers * group
    context = own_ref.shape[2]
    column_groups = latent // LANES
    odd = lax.rem(row, 2) == 1
    gathered = query_ref[...].astype(jnp.float32)
    query = jnp.where(odd, gathered[:, group:, :], gathered[:, :group, :])
    rope = query[:, :, latent:]
    swapped = jnp.concatenate([rope[:, :, ROPE // 2 :], rope[:, :, : ROPE // 2]], axis=-1)
    turned = rope * cos_ref[0][None] + swapped * sin_ref[0][None]
    query = jnp.concatenate([query[:, :, :latent], turned], axis=-1)
    query = query.reshape(count, full).astype(jnp.bfloat16)
    limit = lengths_ref[scalars_ref[0] * 4 + row] - new_count + 1
    token = lax.broadcasted_iota(jnp.int32, (count, 1), 0) % new_count
    terms = []
    for block, first in ((own_ref, scalars_ref[1]), (came_ref, scalars_ref[2])):
        keys = block[0]
        scores = jnp.dot(query, keys, preferred_element_type=jnp.float32)
        place = lax.broadcasted_iota(jnp.int32, (count, context), 1)
        scores = jnp.where(place < limit - first + token, scores, HIDDEN)
        top = jnp.maximum(jnp.max(scores, axis=-1, keepdims=True), LEAST)
        weights = jnp.exp2((scores - top) * POWER)
        total = jnp.sum(weights, axis=-1, keepdims=True)
        out = lax.dot_general(
            weights.astype(jnp.bfloat16),
            keys[:latent],
            (((1,), (1,)), ((), ())),
            preferred_element_type=jnp.float32,
        )
        terms.append((top, total, out))
    (top_a, total_a, out_a), (top_b, total_b, out_b) = terms
    top = jnp.maximum(top_a, top_b)
    scale_a, scale_b = jnp.exp2((top_a - top) * POWER), jnp.exp2((top_b - top) * POWER)
    total = total_a * scale_a + total_b * scale_b
    seen = total > 0.0
    safe = jnp.where(seen, total, 1.0)
    inverse = 1.0 / safe
    out = out_a * (scale_a * inverse) + out_b * (scale_b * inverse)
    stat = jnp.where(seen, top * POWER + jnp.log2(safe), HIDDEN)
    out = out.reshape(peers, group, latent)
    stat = jnp.broadcast_to(stat, (count, LANES)).reshape(peers, group, LANES)

    @pl.when(jnp.logical_not(odd))
    def _():
        kept_ref[:, :, :latent] = out
        kept_ref[:, :, latent:] = stat

    @pl.when(odd)
    def _():
        pair = row // 2
        both = jnp.concatenate([kept_ref[:, :, :latent], out], axis=1).astype(jnp.bfloat16)
        for g in range(column_groups):
            at = pl.multiple_of(g * 2 * sixteen + pair * sixteen, sixteen)
            out_ref[:, pl.ds(at, sixteen), :] = both[:, :, g * LANES : (g + 1) * LANES]
        stats = jnp.concatenate([kept_ref[:, :, latent:], stat], axis=1)
        lane = lax.broadcasted_iota(jnp.int32, stats.shape, 2)
        packed = split_stat(stats, lane)
        at = column_groups * 2 * sixteen

        @pl.when(pair == 0)
        def _():
            out_ref[:, at : at + sixteen, :] = packed.astype(jnp.bfloat16)

        @pl.when(pair == 1)
        def _():
            before = out_ref[:, at : at + sixteen, :].astype(jnp.float32)
            out_ref[:, at : at + sixteen, :] = jnp.where(lane < LANES // 2, before, packed).astype(jnp.bfloat16)


def attend(scalars, lengths, own, came, query, cosines, sines, new_count):
    peers, depth, full = query.shape
    sixteen = depth // 2
    context = own.shape[2]
    group = sixteen // 2
    latent = full - ROPE
    rows_out = latent // LANES * depth + sixteen
    count = peers * group
    return pl.pallas_call(
        functools.partial(attend_kernel, new_count=new_count),
        out_shape=jax.ShapeDtypeStruct((peers, rows_out, LANES), jnp.bfloat16),
        grid_spec=pltpu.PrefetchScalarGridSpec(
            num_scalar_prefetch=2,
            grid=(4,),
            in_specs=[
                pl.BlockSpec((1, full, context), lambda r, scalars, _: (scalars[0] * 4 + r, 0, 0)),
                pl.BlockSpec((1, full, context), lambda r, *_: (r, 0, 0)),
                pl.BlockSpec((peers, sixteen, full), lambda r, *_: (0, r // 2, 0)),
                pl.BlockSpec((1, group, ROPE), lambda r, scalars, _: (scalars[0] * 4 + r, 0, 0)),
                pl.BlockSpec((1, group, ROPE), lambda r, scalars, _: (scalars[0] * 4 + r, 0, 0)),
            ],
            out_specs=pl.BlockSpec((peers, rows_out, LANES), lambda r, *_: (0, 0, 0)),
            scratch_shapes=[pltpu.VMEM((peers, group, latent + LANES), jnp.float32)],
        ),
        compiler_params=pltpu.CompilerParams(vmem_limit_bytes=VMEM_LIMIT),
        cost_estimate=pl.CostEstimate(
            flops=4 * count * context * (full + latent) * 4,
            bytes_accessed=8 * context * full * 2 + 4 * peers * rows_out * LANES,
            transcendentals=8 * count * context,
        ),
        name="attend",
    )(scalars, lengths, own, came, query, cosines, sines)


def project_kernel(parts_ref, up_ref, proj_ref, out_ref, flat_ref, *, new_count):
    sixteen = 16
    peers, rows_out, lanes = parts_ref.shape
    at = rows_out - sixteen
    groups = at // (2 * sixteen)
    heads, _, width = up_ref.shape

    @pl.when(pl.program_id(0) == 0)
    def _():
        blocks = []
        for half in range(2):
            chosen = [2 * k + half for k in range(peers // 2)]
            stat_tiles = [parts_ref[k, at:, :].astype(jnp.float32) for k in chosen]
            for pair in range(2):
                stats = [join_stat(tile, pair) for tile in stat_tiles]
                top = functools.reduce(jnp.maximum, stats)
                weights = [jnp.exp2(stat - top) for stat in stats]
                scale = 1.0 / functools.reduce(jnp.add, weights)
                sums = []
                for g in range(groups):
                    start = g * 2 * sixteen + pair * sixteen
                    acc = None
                    for k, weight in zip(chosen, weights):
                        term = parts_ref[k, start : start + sixteen, :].astype(jnp.float32) * weight
                        acc = term if acc is None else acc + term
                    sums.append(acc * scale)
                blocks.append(jnp.concatenate(sums, axis=-1))
        latent = jnp.concatenate(blocks, axis=0).astype(jnp.bfloat16)
        count = latent.shape[0]
        out_row = lax.broadcasted_iota(jnp.int32, (count // heads, count), 0)
        in_row = lax.broadcasted_iota(jnp.int32, (count // heads, count), 1)
        base = (out_row // new_count) * (new_count * heads) + out_row % new_count
        for head in range(heads):
            pick = jnp.where(in_row == base + head * new_count, 1.0, 0.0).astype(jnp.bfloat16)
            own = jnp.dot(pick, latent, preferred_element_type=jnp.float32).astype(jnp.bfloat16)
            values = jnp.dot(own, up_ref[head], preferred_element_type=jnp.float32)
            flat_ref[:, head * width : (head + 1) * width] = values.astype(jnp.bfloat16)

    terms = jnp.dot(flat_ref[...], proj_ref[...], preferred_element_type=jnp.float32)
    width = out_ref.shape[2]
    for k in range(out_ref.shape[0]):
        out_ref[k] = terms[:, k * width : (k + 1) * width].astype(jnp.bfloat16)


def project(parts, value_up, out_proj, new_count):
    peers, rows_out, lanes = parts.shape
    heads, latent, width = value_up.shape
    depth, columns = out_proj.shape
    tokens = (rows_out - 16) // (latent // lanes) * 2 // heads
    steps = 4
    block = columns // steps
    return pl.pallas_call(
        functools.partial(project_kernel, new_count=new_count),
        out_shape=jax.ShapeDtypeStruct((peers, tokens, columns // peers), jnp.bfloat16),
        grid=(steps,),
        in_specs=[
            pl.BlockSpec((peers, rows_out, lanes), lambda i: (0, 0, 0)),
            pl.BlockSpec((heads, latent, width), lambda i: (0, 0, 0)),
            pl.BlockSpec((depth, block), lambda i: (0, i)),
        ],
        out_specs=pl.BlockSpec((peers // steps, tokens, columns // peers), lambda i: (i, 0, 0)),
        scratch_shapes=[pltpu.VMEM((tokens, depth), jnp.bfloat16)],
        compiler_params=pltpu.CompilerParams(vmem_limit_bytes=16 * 1024 * 1024),
        name="project",
    )(parts, value_up, out_proj)


def total_kernel(terms_ref, out_ref):
    total = jnp.sum(terms_ref[...].astype(jnp.float32), axis=0).astype(jnp.bfloat16)
    new_count = out_ref.shape[1]
    for row in range(out_ref.shape[0]):
        out_ref[row] = total[row * new_count : (row + 1) * new_count]


def total(terms, rows, new_count):
    return pl.pallas_call(
        total_kernel,
        out_shape=jax.ShapeDtypeStruct((rows, new_count, terms.shape[2]), jnp.bfloat16),
        compiler_params=pltpu.CompilerParams(vmem_limit_bytes=8 * 1024 * 1024),
        name="total",
    )(terms)


def body(latent_cache, queries, lengths, positions, value_up, out_proj):
    row_count, context_dev, full = latent_cache.shape
    new_count, heads_dev = queries.shape[1], queries.shape[2]
    shard = lax.axis_index("ctx")
    peers = lax.axis_size("ctx")
    core = shard % 2
    partners = [(i, i ^ 1) for i in range(peers)]
    depth = row_count // 2 * new_count * heads_dev
    own = queries.transpose(0, 2, 1, 3).reshape(1, 2, depth, full)
    own = jnp.broadcast_to(own, (peers // 2, 2, depth, full)).reshape(peers, depth, full)
    here = lax.all_to_all(own, "ctx", 0, 0, tiled=True)
    cache = jnp.swapaxes(latent_cache, 1, 2)
    half = row_count // 2
    lost = lax.dynamic_slice_in_dim(cache, (1 - core) * half, half, 0)
    came = lax.ppermute(lost, "ctx", partners)
    cosines, sines = angle_terms(positions, new_count, heads_dev)
    scalars = jnp.stack([core, shard * context_dev, (shard ^ 1) * context_dev]).astype(jnp.int32)
    mine = attend(scalars, lengths, cache, came, here, cosines, sines, new_count)
    parts = lax.all_to_all(mine, "ctx", 0, 0, tiled=True)
    terms = project(parts, value_up, out_proj, new_count)
    terms = lax.all_to_all(terms, "ctx", 0, 0, tiled=True)
    return total(terms, row_count, new_count)


def solution(mesh):
    in_specs = (
        P("batch", "ctx", None),
        P("batch", None, "ctx", None),
        P("batch"),
        P("batch"),
        P("ctx", None, None),
        P("ctx", None),
    )
    out_specs = P("batch", None, "ctx")
    return jax.shard_map(body, mesh=mesh, in_specs=in_specs, out_specs=out_specs, check_vma=False)
```

```python
import functools
import math

import jax
import jax.numpy as jnp
from jax import lax
from jax.experimental import pallas as pl
from jax.experimental.pallas import tpu as pltpu
from jax.sharding import PartitionSpec as P

ROPE = 64
NOPE = 128
LANES = 128
POWER = math.log2(math.e) / math.sqrt(NOPE + ROPE)
HIDDEN = -1e30
VMEM_LIMIT = 24 * 1024 * 1024
LEAST = -1e29


def angle_terms(positions, new_count, repeats):
    half_rope = ROPE // 2
    exponent = jnp.arange(half_rope, dtype=jnp.float32) * (-2.0 / ROPE)
    frequency = jnp.power(jnp.float32(50000.0), exponent)
    token_place = positions[:, None] + jnp.arange(new_count, dtype=jnp.int32)[None, :]
    angles = token_place.astype(jnp.float32)[:, :, None] * frequency
    cosine, sine = jnp.cos(angles), jnp.sin(angles)
    cosines = jnp.concatenate([cosine, cosine], axis=-1)
    sines = jnp.concatenate([-sine, sine], axis=-1)
    return jnp.tile(cosines, (1, repeats, 1)), jnp.tile(sines, (1, repeats, 1))


def split_stat(value, lane):
    high = value.astype(jnp.bfloat16).astype(jnp.float32)
    rest = value - high
    middle = rest.astype(jnp.bfloat16).astype(jnp.float32)
    low = rest - middle
    spot = lane % (LANES // 2)
    return jnp.where(spot == 0, high, jnp.where(spot == 1, middle, low))


def join_stat(tile, pair):
    at = pair * (LANES // 2)
    return tile[..., at : at + 1] + tile[..., at + 1 : at + 2] + tile[..., at + 2 : at + 3]


def attend_kernel(scalars_ref, lengths_ref, own_ref, came_ref, query_ref, cos_ref, sin_ref, out_ref, keys_ref, arrived, *, new_count):
    peers, depth, full = query_ref.shape
    rows = keys_ref.shape[0] // 2
    group = depth // rows
    latent = full - ROPE
    count = peers * group
    context = keys_ref.shape[2]
    column_groups = latent // LANES
    base = scalars_ref[0] * rows
    copies = []
    for row in range(rows):
        for side, ref in enumerate((own_ref, came_ref)):
            slot = row * 2 + side
            copies.append(pltpu.make_async_copy(ref.at[base + row], keys_ref.at[slot], arrived.at[slot]))
    for copy in copies:
        copy.start()
    token = lax.broadcasted_iota(jnp.int32, (count, 1), 0) % new_count
    queries = []
    for row in range(rows):
        query = query_ref[:, row // 2 * 2 * group : (row // 2 + 1) * 2 * group, :].astype(jnp.float32)
        query = query[:, row % 2 * group : (row % 2 + 1) * group, :]
        rope = query[:, :, latent:]
        swapped = jnp.concatenate([rope[:, :, ROPE // 2 :], rope[:, :, : ROPE // 2]], axis=-1)
        turned = rope * cos_ref[base + row][None] + swapped * sin_ref[base + row][None]
        query = jnp.concatenate([query[:, :, :latent], turned], axis=-1)
        queries.append(query.reshape(count, full).astype(jnp.bfloat16))

    def scores_of(slot):
        copies[slot].wait()
        return jnp.dot(queries[slot // 2], keys_ref[slot], preferred_element_type=jnp.float32)

    def terms_of(slot, scores):
        row, side = slot // 2, slot % 2
        limit = lengths_ref[base + row] - new_count + 1 - scalars_ref[1 + side]
        place = lax.broadcasted_iota(jnp.int32, (count, context), 1)
        scores = jnp.where(place < limit + token, scores, HIDDEN)
        top = jnp.maximum(jnp.max(scores, axis=-1, keepdims=True), LEAST)
        weights = jnp.exp2((scores - top) * POWER)
        total = jnp.sum(weights, axis=-1, keepdims=True)
        out = lax.dot_general(
            weights.astype(jnp.bfloat16),
            keys_ref[slot, :latent],
            (((1,), (1,)), ((), ())),
            preferred_element_type=jnp.float32,
        )
        return top, total, out

    def close(row, first, second):
        (top_a, total_a, out_a), (top_b, total_b, out_b) = first, second
        top = jnp.maximum(top_a, top_b)
        scale_a, scale_b = jnp.exp2((top_a - top) * POWER), jnp.exp2((top_b - top) * POWER)
        total = total_a * scale_a + total_b * scale_b
        seen = total > 0.0
        safe = jnp.where(seen, total, 1.0)
        inverse = 1.0 / safe
        out = out_a * (scale_a * inverse) + out_b * (scale_b * inverse)
        stat = jnp.where(seen, top * POWER + jnp.log2(safe), HIDDEN)
        return out.reshape(peers, group, latent), jnp.broadcast_to(stat, (count, LANES)).reshape(peers, group, LANES)

    sixteen = 2 * group
    at = column_groups * depth
    slots = 2 * rows
    ahead = scores_of(0)
    terms, closed, packed = [], [], []
    for slot in range(slots):
        scores = ahead
        if slot + 1 < slots:
            ahead = scores_of(slot + 1)
        terms.append(terms_of(slot, scores))
        if slot % 2 == 1:
            closed.append(close(slot // 2, *terms[-2:]))
        if slot % 4 == 3:
            pair = slot // 4
            (out_a, stat_a), (out_b, stat_b) = closed[-2:]
            both = jnp.concatenate([out_a, out_b], axis=1).astype(jnp.bfloat16)
            for g in range(column_groups):
                start = g * depth + pair * sixteen
                out_ref[:, start : start + sixteen, :] = both[:, :, g * LANES : (g + 1) * LANES]
            stats = jnp.concatenate([stat_a, stat_b], axis=1)
            lane = lax.broadcasted_iota(jnp.int32, stats.shape, 2)
            packed.append(split_stat(stats, lane))
    lane = lax.broadcasted_iota(jnp.int32, packed[0].shape, 2)
    out_ref[:, at : at + sixteen, :] = jnp.where(lane < LANES // 2, packed[0], packed[1]).astype(jnp.bfloat16)


def attend(scalars, lengths, own, came, query, cosines, sines, new_count):
    peers, depth, full = query.shape
    rows = own.shape[0] // 2
    context = own.shape[2]
    latent = full - ROPE
    rows_out = latent // LANES * depth + depth // rows * 2
    count = peers * depth // rows
    smem, vmem, anywhere = (pl.BlockSpec(memory_space=s) for s in (pltpu.SMEM, pltpu.VMEM, pl.ANY))
    own = pltpu.with_memory_space_constraint(own, pltpu.HBM)
    return pl.pallas_call(
        functools.partial(attend_kernel, new_count=new_count),
        out_shape=pltpu.VMEM((peers, rows_out, LANES), jnp.bfloat16),
        in_specs=[smem, smem, anywhere, anywhere, vmem, vmem, vmem],
        out_specs=vmem,
        scratch_shapes=[
            pltpu.VMEM((2 * rows, full, context), jnp.bfloat16),
            pltpu.SemaphoreType.DMA((2 * rows,)),
        ],
        compiler_params=pltpu.CompilerParams(vmem_limit_bytes=VMEM_LIMIT),
        cost_estimate=pl.CostEstimate(
            flops=4 * count * context * (full + latent) * rows,
            bytes_accessed=2 * rows * context * full * 2 + 2 * peers * rows_out * LANES,
            transcendentals=2 * rows * count * context,
        ),
        name="attend",
    )(scalars, lengths, own, came, query, cosines, sines)


def project_kernel(parts_ref, up_ref, proj_ref, out_ref, flat_ref, *, new_count):
    sixteen = 16
    peers, rows_out, lanes = parts_ref.shape
    at = rows_out - sixteen
    groups = at // (2 * sixteen)
    heads, _, width = up_ref.shape

    @pl.when(pl.program_id(0) == 0)
    def _():
        blocks = []
        for half in range(2):
            chosen = [2 * k + half for k in range(peers // 2)]
            stat_tiles = [parts_ref[k, at:, :].astype(jnp.float32) for k in chosen]
            for pair in range(2):
                stats = [join_stat(tile, pair) for tile in stat_tiles]
                top = functools.reduce(jnp.maximum, stats)
                weights = [jnp.exp2(stat - top) for stat in stats]
                scale = 1.0 / functools.reduce(jnp.add, weights)
                sums = []
                for g in range(groups):
                    start = g * 2 * sixteen + pair * sixteen
                    acc = None
                    for k, weight in zip(chosen, weights):
                        term = parts_ref[k, start : start + sixteen, :].astype(jnp.float32) * weight
                        acc = term if acc is None else acc + term
                    sums.append(acc * scale)
                blocks.append(jnp.concatenate(sums, axis=-1))
        latent = jnp.concatenate(blocks, axis=0).astype(jnp.bfloat16)
        count = latent.shape[0]
        out_row = lax.broadcasted_iota(jnp.int32, (count // heads, count), 0)
        in_row = lax.broadcasted_iota(jnp.int32, (count // heads, count), 1)
        base = (out_row // new_count) * (new_count * heads) + out_row % new_count
        for head in range(heads):
            pick = jnp.where(in_row == base + head * new_count, 1.0, 0.0).astype(jnp.bfloat16)
            own = jnp.dot(pick, latent, preferred_element_type=jnp.float32).astype(jnp.bfloat16)
            values = jnp.dot(own, up_ref[head], preferred_element_type=jnp.float32)
            flat_ref[:, head * width : (head + 1) * width] = values.astype(jnp.bfloat16)

    terms = jnp.dot(flat_ref[...], proj_ref[...], preferred_element_type=jnp.float32)
    width = out_ref.shape[2]
    for k in range(out_ref.shape[0]):
        out_ref[k] = terms[:, k * width : (k + 1) * width].astype(jnp.bfloat16)


def project(parts, value_up, out_proj, new_count):
    peers, rows_out, lanes = parts.shape
    heads, latent, width = value_up.shape
    depth, columns = out_proj.shape
    tokens = (rows_out - 16) // (latent // lanes) * 2 // heads
    steps = 4
    block = columns // steps
    return pl.pallas_call(
        functools.partial(project_kernel, new_count=new_count),
        out_shape=jax.ShapeDtypeStruct((peers, tokens, columns // peers), jnp.bfloat16),
        grid=(steps,),
        in_specs=[
            pl.BlockSpec((peers, rows_out, lanes), lambda i: (0, 0, 0)),
            pl.BlockSpec((heads, latent, width), lambda i: (0, 0, 0)),
            pl.BlockSpec((depth, block), lambda i: (0, i)),
        ],
        out_specs=pl.BlockSpec((peers // steps, tokens, columns // peers), lambda i: (i, 0, 0)),
        scratch_shapes=[pltpu.VMEM((tokens, depth), jnp.bfloat16)],
        compiler_params=pltpu.CompilerParams(vmem_limit_bytes=16 * 1024 * 1024),
        name="project",
    )(parts, value_up, out_proj)


def total_kernel(terms_ref, out_ref):
    total = jnp.sum(terms_ref[...].astype(jnp.float32), axis=0).astype(jnp.bfloat16)
    new_count = out_ref.shape[1]
    for row in range(out_ref.shape[0]):
        out_ref[row] = total[row * new_count : (row + 1) * new_count]


def total(terms, rows, new_count):
    return pl.pallas_call(
        total_kernel,
        out_shape=jax.ShapeDtypeStruct((rows, new_count, terms.shape[2]), jnp.bfloat16),
        compiler_params=pltpu.CompilerParams(vmem_limit_bytes=8 * 1024 * 1024),
        name="total",
    )(terms)


def body(latent_cache, queries, lengths, positions, value_up, out_proj):
    row_count, context_dev, full = latent_cache.shape
    new_count, heads_dev = queries.shape[1], queries.shape[2]
    shard = lax.axis_index("ctx")
    peers = lax.axis_size("ctx")
    core = shard % 2
    partners = [(i, i ^ 1) for i in range(peers)]
    depth = row_count // 2 * new_count * heads_dev
    own = queries.transpose(0, 2, 1, 3).reshape(1, 2, depth, full)
    own = jnp.broadcast_to(own, (peers // 2, 2, depth, full)).reshape(peers, depth, full)
    here = lax.all_to_all(own, "ctx", 0, 0, tiled=True)
    cache = jnp.swapaxes(latent_cache, 1, 2)
    came = lax.ppermute(cache, "ctx", partners)
    cosines, sines = angle_terms(positions, new_count, heads_dev)
    scalars = jnp.stack([core, shard * context_dev, (shard ^ 1) * context_dev]).astype(jnp.int32)
    mine = attend(scalars, lengths, cache, came, here, cosines, sines, new_count)
    parts = lax.all_to_all(mine, "ctx", 0, 0, tiled=True)
    terms = project(parts, value_up, out_proj, new_count)
    terms = lax.all_to_all(terms, "ctx", 0, 0, tiled=True)
    return total(terms, row_count, new_count)


def solution(mesh):
    in_specs = (
        P("batch", "ctx", None),
        P("batch", None, "ctx", None),
        P("batch"),
        P("batch"),
        P("ctx", None, None),
        P("ctx", None),
    )
    out_specs = P("batch", None, "ctx")
    return jax.shard_map(body, mesh=mesh, in_specs=in_specs, out_specs=out_specs, check_vma=False)
```

```python
import functools
import math

import jax
import jax.numpy as jnp
from jax import lax
from jax.experimental import pallas as pl
from jax.experimental.pallas import tpu as pltpu
from jax.sharding import Mesh
from jax.sharding import PartitionSpec as P

ROPE = 64
NOPE = 128
LANES = 128
POWER = math.log2(math.e) / math.sqrt(NOPE + ROPE)
HIDDEN = -1e30
VMEM_LIMIT = 24 * 1024 * 1024
LEAST = -1e29


def angle_terms(positions, new_count, repeats):
    half_rope = ROPE // 2
    exponent = jnp.arange(half_rope, dtype=jnp.float32) * (-2.0 / ROPE)
    frequency = jnp.power(jnp.float32(50000.0), exponent)
    token_place = positions[:, None] + jnp.arange(new_count, dtype=jnp.int32)[None, :]
    angles = token_place.astype(jnp.float32)[:, :, None] * frequency
    cosine, sine = jnp.cos(angles), jnp.sin(angles)
    cosines = jnp.concatenate([cosine, cosine], axis=-1)
    sines = jnp.concatenate([-sine, sine], axis=-1)
    return jnp.repeat(cosines, repeats, axis=1), jnp.repeat(sines, repeats, axis=1)


def split_stat(value, lane):
    high = value.astype(jnp.bfloat16).astype(jnp.float32)
    rest = value - high
    middle = rest.astype(jnp.bfloat16).astype(jnp.float32)
    low = rest - middle
    spot = lane % (LANES // 2)
    return jnp.where(spot == 0, high, jnp.where(spot == 1, middle, low))


def join_stat(tile, pair):
    at = pair * (LANES // 2)
    return tile[..., at : at + 1] + tile[..., at + 1 : at + 2] + tile[..., at + 2 : at + 3]


def spread_kernel(query_ref, out_ref, flat_ref):
    rows, new_count, heads, _ = query_ref.shape
    for row in range(rows):
        for token in range(new_count):
            at = (row * new_count + token) * heads
            flat_ref[at : at + heads, :] = query_ref[row, token].astype(jnp.float32)
    flat = flat_ref[...].astype(jnp.bfloat16)
    depth = out_ref.shape[1]
    for peer in range(out_ref.shape[0]):
        at = peer % 2 * depth
        out_ref[peer] = flat[at : at + depth]


def spread(queries, peers):
    rows, new_count, heads, full = queries.shape
    count = rows * new_count * heads
    vmem = pl.BlockSpec(memory_space=pltpu.VMEM)
    return pl.pallas_call(
        spread_kernel,
        out_shape=pltpu.VMEM((peers, count // 2, full), jnp.bfloat16),
        in_specs=[vmem],
        out_specs=vmem,
        scratch_shapes=[pltpu.VMEM((count, full), jnp.float32)],
        compiler_params=pltpu.CompilerParams(vmem_limit_bytes=8 * 1024 * 1024),
        name="spread",
    )(queries)


def attend_kernel(scalars_ref, lengths_ref, own_ref, came_ref, query_ref, cos_ref, sin_ref, out_ref, keys_ref, arrived, *, new_count):
    peers, depth, full = query_ref.shape
    slots, wide, context = keys_ref.shape
    rows = slots // 2
    group = depth // rows
    latent = full - ROPE
    count = peers * group
    column_groups = latent // LANES
    base = scalars_ref[0] * rows
    copies = []
    for row in range(rows):
        for side, ref in enumerate((own_ref, came_ref)):
            slot = row * 2 + side
            copies.append(pltpu.make_async_copy(ref.at[base + row], keys_ref.at[slot, pl.ds(0, full)], arrived.at[slot]))
    for copy in copies:
        copy.start()
    spare = wide - full
    heads = group // new_count
    column = lax.broadcasted_iota(jnp.int32, (peers, group, spare), 2)
    member = lax.broadcasted_iota(jnp.int32, (peers, group, spare), 1)
    flags = jnp.where(column == member // heads, 1.0, 0.0)
    place = lax.broadcasted_iota(jnp.int32, (spare, context), 1)
    token = lax.broadcasted_iota(jnp.int32, (spare, context), 0)
    for slot in range(slots):
        limit = lengths_ref[base + slot // 2] - new_count + 1 - scalars_ref[1 + slot % 2]
        hidden = (token < new_count) & (place >= limit + token)
        keys_ref[slot, full:, :] = jnp.where(hidden, HIDDEN, 0.0).astype(jnp.bfloat16)
    queries = []
    for row in range(rows):
        query = query_ref[:, row // 2 * 2 * group : (row // 2 + 1) * 2 * group, :].astype(jnp.float32)
        query = query[:, row % 2 * group : (row % 2 + 1) * group, :]
        rope = query[:, :, latent:]
        swapped = jnp.concatenate([rope[:, :, ROPE // 2 :], rope[:, :, : ROPE // 2]], axis=-1)
        turned = rope * cos_ref[base + row][None] + swapped * sin_ref[base + row][None]
        query = jnp.concatenate([query[:, :, :latent], turned, flags], axis=-1)
        queries.append(query.reshape(count, wide).astype(jnp.bfloat16))

    def score(slot):
        copies[slot].wait()
        scores = jnp.dot(queries[slot // 2], keys_ref[slot], preferred_element_type=jnp.float32)
        return scores, jnp.maximum(jnp.max(scores, axis=-1, keepdims=True), LEAST)

    def close(first, second):
        (top_a, total_a, out_a), (top_b, total_b, out_b) = first, second
        top = jnp.maximum(top_a, top_b)
        scale_a, scale_b = jnp.exp2((top_a - top) * POWER), jnp.exp2((top_b - top) * POWER)
        total = total_a * scale_a + total_b * scale_b
        seen = total > 0.0
        safe = jnp.where(seen, total, 1.0)
        inverse = 1.0 / safe
        out = out_a * (scale_a * inverse) + out_b * (scale_b * inverse)
        stat = jnp.where(seen, top * POWER + jnp.log2(safe), HIDDEN)
        return out.reshape(peers, group, latent), jnp.broadcast_to(stat, (count, LANES)).reshape(peers, group, LANES)

    sixteen = 2 * group
    at = column_groups * depth
    terms, closed, packed = [], [], []
    ahead = score(0)
    for slot in range(slots):
        scores, top = ahead
        if slot + 1 < slots:
            ahead = score(slot + 1)
        weights = jnp.exp2((scores - top) * POWER)
        total = jnp.sum(weights, axis=-1, keepdims=True)
        out = lax.dot_general(
            weights.astype(jnp.bfloat16),
            keys_ref[slot, :latent],
            (((1,), (1,)), ((), ())),
            preferred_element_type=jnp.float32,
        )
        terms.append((top, total, out))
        if slot % 2 == 1:
            closed.append(close(*terms[-2:]))
        if slot % 4 == 3:
            pair = slot // 4
            (out_a, stat_a), (out_b, stat_b) = closed[-2:]
            both = jnp.concatenate([out_a, out_b], axis=1).astype(jnp.bfloat16)
            for g in range(column_groups):
                start = g * depth + pair * sixteen
                out_ref[:, start : start + sixteen, :] = both[:, :, g * LANES : (g + 1) * LANES]
            stats = jnp.concatenate([stat_a, stat_b], axis=1)
            lane = lax.broadcasted_iota(jnp.int32, stats.shape, 2)
            packed.append(split_stat(stats, lane))
    lane = lax.broadcasted_iota(jnp.int32, packed[0].shape, 2)
    out_ref[:, at : at + sixteen, :] = jnp.where(lane < LANES // 2, packed[0], packed[1]).astype(jnp.bfloat16)


def attend(scalars, lengths, own, came, query, cosines, sines, new_count):
    peers, depth, full = query.shape
    rows = own.shape[0] // 2
    context = own.shape[2]
    latent = full - ROPE
    rows_out = latent // LANES * depth + depth // rows * 2
    count = peers * depth // rows
    smem, vmem, anywhere = (pl.BlockSpec(memory_space=s) for s in (pltpu.SMEM, pltpu.VMEM, pl.ANY))
    own = pltpu.with_memory_space_constraint(own, pltpu.HBM)
    return pl.pallas_call(
        functools.partial(attend_kernel, new_count=new_count),
        out_shape=pltpu.VMEM((peers, rows_out, LANES), jnp.bfloat16),
        in_specs=[smem, smem, anywhere, anywhere, vmem, vmem, vmem],
        out_specs=vmem,
        scratch_shapes=[
            pltpu.VMEM((2 * rows, -(-full // LANES) * LANES, context), jnp.bfloat16),
            pltpu.SemaphoreType.DMA((2 * rows,)),
        ],
        compiler_params=pltpu.CompilerParams(vmem_limit_bytes=VMEM_LIMIT),
        cost_estimate=pl.CostEstimate(
            flops=4 * count * context * (full + latent) * rows,
            bytes_accessed=2 * rows * context * full * 2 + 2 * peers * rows_out * LANES,
            transcendentals=2 * rows * count * context,
        ),
        name="attend",
    )(scalars, lengths, own, came, query, cosines, sines)


def project_kernel(core_ref, parts_ref, own_up_ref, came_up_ref, own_proj_ref, came_proj_ref, out_ref):
    sixteen = 16
    peers, rows_out, _ = parts_ref.shape
    at = rows_out - sixteen
    groups = at // (2 * sixteen)
    flats = []
    for side, up_ref in enumerate((own_up_ref, came_up_ref)):
        heads = up_ref.shape[0]
        member = core_ref[0] if side == 0 else 1 - core_ref[0]
        blocks = []
        stat_tiles = [parts_ref[2 * k + member, at:, :].astype(jnp.float32) for k in range(peers // 2)]
        for pair in range(2):
            stats = [join_stat(tile, pair) for tile in stat_tiles]
            top = functools.reduce(jnp.maximum, stats)
            weights = [jnp.exp2(stat - top) for stat in stats]
            scale = 1.0 / functools.reduce(jnp.add, weights)
            sums = []
            for g in range(groups):
                start = g * 2 * sixteen + pair * sixteen
                terms = [
                    parts_ref[2 * k + member, start : start + sixteen, :].astype(jnp.float32) * weight
                    for k, weight in enumerate(weights)
                ]
                sums.append(functools.reduce(jnp.add, terms) * scale)
            blocks.append(jnp.concatenate(sums, axis=-1))
        latent = jnp.concatenate(blocks, axis=0).astype(jnp.bfloat16)
        count = latent.shape[0]
        out_row = lax.broadcasted_iota(jnp.int32, (count // heads, count), 0)
        in_row = lax.broadcasted_iota(jnp.int32, (count // heads, count), 1)
        values = []
        for head in range(heads):
            pick = jnp.where(in_row == out_row * heads + head, 1.0, 0.0).astype(jnp.bfloat16)
            chosen = jnp.dot(pick, latent, preferred_element_type=jnp.float32).astype(jnp.bfloat16)
            values.append(jnp.dot(chosen, up_ref[head], preferred_element_type=jnp.float32).astype(jnp.bfloat16))
        flats.append(jnp.concatenate(values, axis=-1))
    width = out_ref.shape[2]
    step = 4
    for first in range(0, out_ref.shape[0], step):
        columns = slice(first * width, (first + step) * width)
        terms = jnp.dot(flats[0], own_proj_ref[:, columns], preferred_element_type=jnp.float32)
        terms += jnp.dot(flats[1], came_proj_ref[:, columns], preferred_element_type=jnp.float32)
        for k in range(step):
            out_ref[first + k] = terms[:, k * width : (k + 1) * width].astype(jnp.bfloat16)


def project(core, parts, own_up, came_up, own_proj, came_proj):
    peers, rows_out, lanes = parts.shape
    heads, latent, _ = own_up.shape
    columns = own_proj.shape[1]
    tokens = (rows_out - 16) // (latent // lanes) // heads
    smem, vmem = (pl.BlockSpec(memory_space=space) for space in (pltpu.SMEM, pltpu.VMEM))
    return pl.pallas_call(
        project_kernel,
        out_shape=pltpu.VMEM((peers, tokens, columns // peers), jnp.bfloat16),
        in_specs=[smem] + [vmem] * 5,
        out_specs=vmem,
        compiler_params=pltpu.CompilerParams(vmem_limit_bytes=16 * 1024 * 1024),
        name="project",
    )(core, parts, own_up, came_up, own_proj, came_proj)


def total_kernel(terms_ref, out_ref):
    rows, new_count, _ = out_ref.shape
    half = rows // 2
    for core in range(2):
        terms = [terms_ref[k].astype(jnp.float32) for k in range(core, terms_ref.shape[0], 2)]
        result = functools.reduce(jnp.add, terms).astype(jnp.bfloat16)
        for row in range(half):
            out_ref[core * half + row] = result[row * new_count : (row + 1) * new_count]


def total(terms, rows, new_count):
    vmem = pl.BlockSpec(memory_space=pltpu.VMEM)
    return pl.pallas_call(
        total_kernel,
        out_shape=jax.ShapeDtypeStruct((rows, new_count, terms.shape[2]), jnp.bfloat16),
        in_specs=[vmem],
        out_specs=vmem,
        compiler_params=pltpu.CompilerParams(vmem_limit_bytes=8 * 1024 * 1024),
        name="total",
    )(terms)


def body(latent_cache, queries, lengths, positions, value_up, out_proj):
    row_count, context_dev, full = latent_cache.shape
    new_count, heads_dev = queries.shape[1], queries.shape[2]
    core = lax.axis_index("core")
    shard = lax.axis_index("chip") * 2 + core
    peers = lax.axis_size("chip") * 2
    both = ("chip", "core")
    swap = [(0, 1), (1, 0)]
    cache = jnp.swapaxes(latent_cache, 1, 2)
    came = lax.ppermute(cache, "core", swap)
    query = lax.all_to_all(spread(queries, peers), both, 0, 0, tiled=True)
    cosines, sines = angle_terms(positions, new_count, heads_dev)
    scalars = jnp.stack([core, shard * context_dev, (shard ^ 1) * context_dev]).astype(jnp.int32)
    mine = attend(scalars, lengths, cache, came, query, cosines, sines, new_count)
    query, value_up, out_proj = lax.optimization_barrier((query, value_up, out_proj))
    came_up = lax.ppermute(value_up, "core", swap)
    came_proj = lax.ppermute(out_proj, "core", swap)
    parts = lax.all_to_all(mine, "chip", 0, 0, tiled=True)
    terms = project(scalars[:1], parts, value_up, came_up, out_proj, came_proj)
    terms = lax.all_to_all(terms, both, 0, 0, tiled=True)
    return total(terms, row_count, new_count)


def solution(mesh):
    batch, ctx = mesh.devices.shape
    mesh = Mesh(mesh.devices.reshape(batch, ctx // 2, 2), ("batch", "chip", "core"))
    ctx = ("chip", "core")
    in_specs = (
        P("batch", ctx, None),
        P("batch", None, ctx, None),
        P("batch"),
        P("batch"),
        P(ctx, None, None),
        P(ctx, None),
    )
    out_specs = P("batch", None, ctx)
    return jax.shard_map(body, mesh=mesh, in_specs=in_specs, out_specs=out_specs, check_vma=False)
```

```python
import functools
import math

import jax
import jax.numpy as jnp
from jax import lax
from jax.experimental import pallas as pl
from jax.experimental.pallas import tpu as pltpu
from jax.sharding import Mesh
from jax.sharding import PartitionSpec as P

ROPE = 64
NOPE = 128
LANES = 128
POWER = math.log2(math.e) / math.sqrt(NOPE + ROPE)
HIDDEN = -1e30
VMEM_LIMIT = 24 * 1024 * 1024
LEAST = -1e29


def angle_terms(positions, new_count, repeats):
    half_rope = ROPE // 2
    exponent = jnp.arange(half_rope, dtype=jnp.float32) * (-2.0 / ROPE)
    frequency = jnp.power(jnp.float32(50000.0), exponent)
    token_place = positions[:, None] + jnp.arange(new_count, dtype=jnp.int32)[None, :]
    angles = token_place.astype(jnp.float32)[:, :, None] * frequency
    cosine, sine = jnp.cos(angles), jnp.sin(angles)
    cosines = jnp.concatenate([cosine, cosine], axis=-1)
    sines = jnp.concatenate([-sine, sine], axis=-1)
    return jnp.repeat(cosines, repeats, axis=1), jnp.repeat(sines, repeats, axis=1)


def split_stat(value, lane):
    high = value.astype(jnp.bfloat16).astype(jnp.float32)
    rest = value - high
    middle = rest.astype(jnp.bfloat16).astype(jnp.float32)
    low = rest - middle
    spot = lane % (LANES // 2)
    return jnp.where(spot == 0, high, jnp.where(spot == 1, middle, low))


def join_stat(tile, pair):
    at = pair * (LANES // 2)
    return tile[..., at : at + 1] + tile[..., at + 1 : at + 2] + tile[..., at + 2 : at + 3]


def spread_kernel(query_ref, out_ref, flat_ref):
    rows, new_count, heads, _ = query_ref.shape
    for row in range(rows):
        for token in range(new_count):
            at = (row * new_count + token) * heads
            flat_ref[at : at + heads, :] = query_ref[row, token].astype(jnp.float32)
    flat = flat_ref[...].astype(jnp.bfloat16)
    depth = out_ref.shape[1]
    for peer in range(out_ref.shape[0]):
        at = peer % 2 * depth
        out_ref[peer] = flat[at : at + depth]


def spread(queries, peers):
    rows, new_count, heads, full = queries.shape
    count = rows * new_count * heads
    vmem = pl.BlockSpec(memory_space=pltpu.VMEM)
    return pl.pallas_call(
        spread_kernel,
        out_shape=pltpu.VMEM((peers, count // 2, full), jnp.bfloat16),
        in_specs=[vmem],
        out_specs=vmem,
        scratch_shapes=[pltpu.VMEM((count, full), jnp.float32)],
        compiler_params=pltpu.CompilerParams(vmem_limit_bytes=8 * 1024 * 1024),
        name="spread",
    )(queries)


def attend_kernel(scalars_ref, lengths_ref, own_ref, came_ref, query_ref, cos_ref, sin_ref, out_ref, keys_ref, arrived, *, new_count):
    peers, depth, full = query_ref.shape
    slots, wide, context = keys_ref.shape
    rows = slots // 2
    group = depth // rows
    latent = full - ROPE
    count = peers * group
    column_groups = latent // LANES
    base = scalars_ref[0] * rows
    copies = []
    for row in range(rows):
        for side, ref in enumerate((own_ref, came_ref)):
            slot = row * 2 + side
            copies.append(pltpu.make_async_copy(ref.at[base + row], keys_ref.at[slot, pl.ds(0, full)], arrived.at[slot]))
    for copy in copies:
        copy.start()
    spare = wide - full
    heads = group // new_count
    column = lax.broadcasted_iota(jnp.int32, (peers, group, spare), 2)
    member = lax.broadcasted_iota(jnp.int32, (peers, group, spare), 1)
    flags = jnp.where(column == member // heads, 1.0, 0.0)
    place = lax.broadcasted_iota(jnp.int32, (spare, context), 1)
    token = lax.broadcasted_iota(jnp.int32, (spare, context), 0)
    for slot in range(slots):
        limit = lengths_ref[base + slot // 2] - new_count + 1 - scalars_ref[1 + slot % 2]
        hidden = (token < new_count) & (place >= limit + token)
        keys_ref[slot, full:, :] = jnp.where(hidden, HIDDEN, 0.0).astype(jnp.bfloat16)
    queries = []
    for row in range(rows):
        query = query_ref[:, row // 2 * 2 * group : (row // 2 + 1) * 2 * group, :].astype(jnp.float32)
        query = query[:, row % 2 * group : (row % 2 + 1) * group, :]
        rope = query[:, :, latent:]
        swapped = jnp.concatenate([rope[:, :, ROPE // 2 :], rope[:, :, : ROPE // 2]], axis=-1)
        turned = rope * cos_ref[base + row][None] + swapped * sin_ref[base + row][None]
        query = jnp.concatenate([query[:, :, :latent], turned, flags], axis=-1)
        queries.append(query.reshape(count, wide).astype(jnp.bfloat16))

    def score(slot):
        copies[slot].wait()
        scores = jnp.dot(queries[slot // 2], keys_ref[slot], preferred_element_type=jnp.float32)
        return scores, jnp.maximum(jnp.max(scores, axis=-1, keepdims=True), LEAST)

    def close(first, second):
        (top_a, total_a, out_a), (top_b, total_b, out_b) = first, second
        top = jnp.maximum(top_a, top_b)
        scale_a, scale_b = jnp.exp2((top_a - top) * POWER), jnp.exp2((top_b - top) * POWER)
        total = total_a * scale_a + total_b * scale_b
        seen = total > 0.0
        safe = jnp.where(seen, total, 1.0)
        inverse = 1.0 / safe
        out = out_a * (scale_a * inverse) + out_b * (scale_b * inverse)
        stat = jnp.where(seen, top * POWER + jnp.log2(safe), HIDDEN)
        return out.reshape(peers, group, latent), jnp.broadcast_to(stat, (count, LANES)).reshape(peers, group, LANES)

    sixteen = 2 * group
    at = column_groups * depth
    terms, closed, packed = [], [], []
    ahead = score(0)
    for slot in range(slots):
        scores, top = ahead
        if slot + 1 < slots:
            ahead = score(slot + 1)
        weights = jnp.exp2((scores - top) * POWER)
        total = jnp.sum(weights, axis=-1, keepdims=True)
        out = lax.dot_general(
            weights.astype(jnp.bfloat16),
            keys_ref[slot, :latent],
            (((1,), (1,)), ((), ())),
            preferred_element_type=jnp.float32,
        )
        terms.append((top, total, out))
        if slot % 2 == 1:
            closed.append(close(*terms[-2:]))
        if slot % 4 == 3:
            pair = slot // 4
            (out_a, stat_a), (out_b, stat_b) = closed[-2:]
            both = jnp.concatenate([out_a, out_b], axis=1).astype(jnp.bfloat16)
            for g in range(column_groups):
                start = g * depth + pair * sixteen
                out_ref[:, start : start + sixteen, :] = both[:, :, g * LANES : (g + 1) * LANES]
            stats = jnp.concatenate([stat_a, stat_b], axis=1)
            lane = lax.broadcasted_iota(jnp.int32, stats.shape, 2)
            packed.append(split_stat(stats, lane))
    lane = lax.broadcasted_iota(jnp.int32, packed[0].shape, 2)
    out_ref[:, at : at + sixteen, :] = jnp.where(lane < LANES // 2, packed[0], packed[1]).astype(jnp.bfloat16)


def attend(scalars, lengths, own, came, query, cosines, sines, new_count):
    peers, depth, full = query.shape
    rows = own.shape[0] // 2
    context = own.shape[2]
    latent = full - ROPE
    rows_out = latent // LANES * depth + depth // rows * 2
    count = peers * depth // rows
    smem, vmem, anywhere = (pl.BlockSpec(memory_space=s) for s in (pltpu.SMEM, pltpu.VMEM, pl.ANY))
    own = pltpu.with_memory_space_constraint(own, pltpu.HBM)
    return pl.pallas_call(
        functools.partial(attend_kernel, new_count=new_count),
        out_shape=pltpu.VMEM((peers, rows_out, LANES), jnp.bfloat16),
        in_specs=[smem, smem, anywhere, anywhere, vmem, vmem, vmem],
        out_specs=vmem,
        scratch_shapes=[
            pltpu.VMEM((2 * rows, -(-full // LANES) * LANES, context), jnp.bfloat16),
            pltpu.SemaphoreType.DMA((2 * rows,)),
        ],
        compiler_params=pltpu.CompilerParams(vmem_limit_bytes=VMEM_LIMIT),
        cost_estimate=pl.CostEstimate(
            flops=4 * count * context * (full + latent) * rows,
            bytes_accessed=2 * rows * context * full * 2 + 2 * peers * rows_out * LANES,
            transcendentals=2 * rows * count * context,
        ),
        name="attend",
    )(scalars, lengths, own, came, query, cosines, sines)


def project_kernel(parts_ref, up_ref, proj_ref, out_ref):
    sixteen = 16
    peers, rows_out, _ = parts_ref.shape
    at = rows_out - sixteen
    groups = at // (2 * sixteen)
    heads = up_ref.shape[0]
    blocks = []
    for half in range(2):
        chosen = range(half, peers, 2)
        stat_tiles = [parts_ref[k, at:, :].astype(jnp.float32) for k in chosen]
        for pair in range(2):
            stats = [join_stat(tile, pair) for tile in stat_tiles]
            top = functools.reduce(jnp.maximum, stats)
            weights = [jnp.exp2(stat - top) for stat in stats]
            scale = 1.0 / functools.reduce(jnp.add, weights)
            sums = []
            for g in range(groups):
                start = g * 2 * sixteen + pair * sixteen
                terms = [
                    parts_ref[k, start : start + sixteen, :].astype(jnp.float32) * weight
                    for k, weight in zip(chosen, weights)
                ]
                sums.append(functools.reduce(jnp.add, terms) * scale)
            blocks.append(jnp.concatenate(sums, axis=-1))
    latent = jnp.concatenate(blocks, axis=0).astype(jnp.bfloat16)
    count = latent.shape[0]
    out_row = lax.broadcasted_iota(jnp.int32, (count // heads, count), 0)
    in_row = lax.broadcasted_iota(jnp.int32, (count // heads, count), 1)
    values = []
    for head in range(heads):
        pick = jnp.where(in_row == out_row * heads + head, 1.0, 0.0).astype(jnp.bfloat16)
        own = jnp.dot(pick, latent, preferred_element_type=jnp.float32).astype(jnp.bfloat16)
        values.append(jnp.dot(own, up_ref[head], preferred_element_type=jnp.float32).astype(jnp.bfloat16))
    flat = jnp.concatenate(values, axis=-1)
    width = out_ref.shape[2]
    step = 4
    for first in range(0, out_ref.shape[0], step):
        columns = slice(first * width, (first + step) * width)
        terms = jnp.dot(flat, proj_ref[:, columns], preferred_element_type=jnp.float32)
        for k in range(step):
            out_ref[first + k] = terms[:, k * width : (k + 1) * width].astype(jnp.bfloat16)


def project(parts, value_up, out_proj):
    peers, rows_out, lanes = parts.shape
    heads, latent, _ = value_up.shape
    columns = out_proj.shape[1]
    tokens = (rows_out - 16) // (latent // lanes) * 2 // heads
    vmem = pl.BlockSpec(memory_space=pltpu.VMEM)
    return pl.pallas_call(
        project_kernel,
        out_shape=pltpu.VMEM((peers, tokens, columns // peers), jnp.bfloat16),
        in_specs=[vmem] * 3,
        out_specs=vmem,
        compiler_params=pltpu.CompilerParams(vmem_limit_bytes=16 * 1024 * 1024),
        name="project",
    )(parts, value_up, out_proj)


def total_kernel(terms_ref, out_ref):
    rows, new_count, _ = out_ref.shape
    terms = [terms_ref[k].astype(jnp.float32) for k in range(terms_ref.shape[0])]
    result = functools.reduce(jnp.add, terms).astype(jnp.bfloat16)
    for row in range(rows):
        out_ref[row] = result[row * new_count : (row + 1) * new_count]


def total(terms, rows, new_count):
    vmem = pl.BlockSpec(memory_space=pltpu.VMEM)
    return pl.pallas_call(
        total_kernel,
        out_shape=jax.ShapeDtypeStruct((rows, new_count, terms.shape[2]), jnp.bfloat16),
        in_specs=[vmem],
        out_specs=vmem,
        compiler_params=pltpu.CompilerParams(vmem_limit_bytes=8 * 1024 * 1024),
        name="total",
    )(terms)


def body(latent_cache, queries, lengths, positions, value_up, out_proj):
    row_count, context_dev, full = latent_cache.shape
    new_count, heads_dev = queries.shape[1], queries.shape[2]
    core = lax.axis_index("core")
    shard = lax.axis_index("chip") * 2 + core
    peers = lax.axis_size("chip") * 2
    both = ("chip", "core")
    swap = [(0, 1), (1, 0)]
    cache = jnp.swapaxes(latent_cache, 1, 2)
    came = lax.ppermute(cache, "core", swap)
    query = lax.all_to_all(spread(queries, peers), both, 0, 0, tiled=True)
    cosines, sines = angle_terms(positions, new_count, heads_dev)
    scalars = jnp.stack([core, shard * context_dev, (shard ^ 1) * context_dev]).astype(jnp.int32)
    mine = attend(scalars, lengths, cache, came, query, cosines, sines, new_count)
    parts = lax.all_to_all(mine, both, 0, 0, tiled=True)
    terms = project(parts, value_up, out_proj)
    terms = lax.all_to_all(terms, both, 0, 0, tiled=True)
    return total(terms, row_count, new_count)


def solution(mesh):
    batch, ctx = mesh.devices.shape
    mesh = Mesh(mesh.devices.reshape(batch, ctx // 2, 2), ("batch", "chip", "core"))
    ctx = ("chip", "core")
    in_specs = (
        P("batch", ctx, None),
        P("batch", None, ctx, None),
        P("batch"),
        P("batch"),
        P(ctx, None, None),
        P(ctx, None),
    )
    out_specs = P("batch", None, ctx)
    return jax.shard_map(body, mesh=mesh, in_specs=in_specs, out_specs=out_specs, check_vma=False)
```

```python
import functools
import math

import jax
import jax.numpy as jnp
from jax import lax
from jax.experimental import pallas as pl
from jax.experimental.pallas import tpu as pltpu
from jax.sharding import Mesh
from jax.sharding import PartitionSpec as P

ROPE = 64
NOPE = 128
LANES = 128
POWER = math.log2(math.e) / math.sqrt(NOPE + ROPE)
HIDDEN = -1e30
VMEM_LIMIT = 24 * 1024 * 1024
LEAST = -1e29


def angle_terms(positions, new_count, repeats):
    half_rope = ROPE // 2
    exponent = jnp.arange(half_rope, dtype=jnp.float32) * (-2.0 / ROPE)
    frequency = jnp.power(jnp.float32(50000.0), exponent)
    token_place = positions[:, None] + jnp.arange(new_count, dtype=jnp.int32)[None, :]
    angles = token_place.astype(jnp.float32)[:, :, None] * frequency
    cosine, sine = jnp.cos(angles), jnp.sin(angles)
    cosines = jnp.concatenate([cosine, cosine], axis=-1)
    sines = jnp.concatenate([-sine, sine], axis=-1)
    return jnp.repeat(cosines, repeats, axis=1), jnp.repeat(sines, repeats, axis=1)


def split_stat(value, lane):
    high = value.astype(jnp.bfloat16).astype(jnp.float32)
    rest = value - high
    middle = rest.astype(jnp.bfloat16).astype(jnp.float32)
    low = rest - middle
    spot = lane % (LANES // 2)
    return jnp.where(spot == 0, high, jnp.where(spot == 1, middle, low))


def join_stat(tile, pair):
    at = pair * (LANES // 2)
    return tile[..., at : at + 1] + tile[..., at + 1 : at + 2] + tile[..., at + 2 : at + 3]


def spread_kernel(query_ref, cos_ref, sin_ref, out_ref, flat_ref):
    rows, new_count, heads, full = query_ref.shape
    latent = full - ROPE
    for row in range(rows):
        for token in range(new_count):
            at = (row * new_count + token) * heads
            flat_ref[at : at + heads, :] = query_ref[row, token].astype(jnp.float32)
    flat = flat_ref[...]
    rope = flat[:, latent:]
    swapped = jnp.concatenate([rope[:, ROPE // 2 :], rope[:, : ROPE // 2]], axis=-1)
    turned = rope * cos_ref[...].reshape(rope.shape) + swapped * sin_ref[...].reshape(rope.shape)
    flat = jnp.concatenate([flat[:, :latent], turned], axis=-1).astype(jnp.bfloat16)
    depth = out_ref.shape[1]
    for peer in range(out_ref.shape[0]):
        at = peer % 2 * depth
        out_ref[peer] = flat[at : at + depth]


def spread(queries, cosines, sines, peers):
    rows, new_count, heads, full = queries.shape
    count = rows * new_count * heads
    vmem = pl.BlockSpec(memory_space=pltpu.VMEM)
    return pl.pallas_call(
        spread_kernel,
        out_shape=pltpu.VMEM((peers, count // 2, full), jnp.bfloat16),
        in_specs=[vmem] * 3,
        out_specs=vmem,
        scratch_shapes=[pltpu.VMEM((count, full), jnp.float32)],
        compiler_params=pltpu.CompilerParams(vmem_limit_bytes=8 * 1024 * 1024),
        name="spread",
    )(queries, cosines, sines)


def attend_kernel(scalars_ref, lengths_ref, own_ref, came_ref, query_ref, out_ref, keys_ref, arrived, *, new_count, mode=0):
    peers, depth, full = query_ref.shape
    rows, wide, context = keys_ref.shape
    span = context // 2
    group = depth // rows
    heads = group // new_count
    latent = full - ROPE
    count = peers * group
    column_groups = latent // LANES
    base = scalars_ref[0] * rows
    copies = []
    for row in range(rows):
        for side, ref in enumerate((own_ref, came_ref)):
            target = keys_ref.at[row, pl.ds(0, full), pl.ds(side * span, span)]
            copies.append(pltpu.make_async_copy(ref.at[base + row], target, arrived.at[row * 2 + side]))
    for copy in copies:
        copy.start()
    spare = wide - full
    column = lax.broadcasted_iota(jnp.int32, (peers, group, spare), 2)
    member = lax.broadcasted_iota(jnp.int32, (peers, group, spare), 1)
    flags = jnp.where(column == member // heads, 1.0, 0.0)
    place = lax.broadcasted_iota(jnp.int32, (spare, span), 1)
    token = lax.broadcasted_iota(jnp.int32, (spare, span), 0)
    queries = []
    for row in range(rows):
        for side in range(2):
            limit = lengths_ref[base + row] - new_count + 1 - scalars_ref[1 + side]
            hidden = (token < new_count) & (place >= limit + token)
            keys_ref[row, full:, side * span : (side + 1) * span] = jnp.where(hidden, HIDDEN, 0.0).astype(jnp.bfloat16)
        query = query_ref[:, row // 2 * 2 * group : (row // 2 + 1) * 2 * group, :].astype(jnp.float32)
        query = jnp.concatenate([query[:, row % 2 * group : (row % 2 + 1) * group, :], flags], axis=-1)
        queries.append(query.reshape(count, wide).astype(jnp.bfloat16))

    def score(row):
        copies[2 * row].wait()
        copies[2 * row + 1].wait()
        scores = jnp.dot(queries[row], keys_ref[row], preferred_element_type=jnp.float32)
        return scores, jnp.maximum(jnp.max(scores, axis=-1, keepdims=True), LEAST)

    sixteen = 2 * group
    at = column_groups * depth
    closed, packed = [], []
    ahead = score(0)
    for row in range(rows):
        scores, top = ahead
        if row + 1 < rows:
            ahead = score(row + 1)
        weights = jnp.exp2((scores - top) * POWER)
        total = jnp.sum(weights, axis=-1, keepdims=True)
        out = lax.dot_general(
            weights.astype(jnp.bfloat16),
            keys_ref[row, :latent],
            (((1,), (1,)), ((), ())),
            preferred_element_type=jnp.float32,
        )
        seen = total > 0.0
        safe = jnp.where(seen, total, 1.0)
        out = out * (1.0 / safe)
        stat = jnp.where(seen, top * POWER + jnp.log2(safe), HIDDEN)
        stat = jnp.broadcast_to(stat, (count, LANES)).reshape(peers, group, LANES)
        closed.append((out.reshape(peers, group, latent), stat))
        if row % 2 == 1:
            pair = row // 2
            (out_a, stat_a), (out_b, stat_b) = closed[-2:]
            both = jnp.concatenate([out_a, out_b], axis=1).astype(jnp.bfloat16)
            for g in range(column_groups):
                start = g * depth + pair * sixteen
                out_ref[:, start : start + sixteen, :] = both[:, :, g * LANES : (g + 1) * LANES]
            stats = jnp.concatenate([stat_a, stat_b], axis=1)
            lane = lax.broadcasted_iota(jnp.int32, stats.shape, 2)
            packed.append(split_stat(stats, lane))
    lane = lax.broadcasted_iota(jnp.int32, packed[0].shape, 2)
    out_ref[:, at : at + sixteen, :] = jnp.where(lane < LANES // 2, packed[0], packed[1]).astype(jnp.bfloat16)


def attend(scalars, lengths, own, came, query, new_count):
    peers, depth, full = query.shape
    rows = own.shape[0] // 2
    context = own.shape[2]
    latent = full - ROPE
    rows_out = latent // LANES * depth + depth // rows * 2
    count = peers * depth // rows
    smem, vmem, anywhere = (pl.BlockSpec(memory_space=s) for s in (pltpu.SMEM, pltpu.VMEM, pl.ANY))
    own = pltpu.with_memory_space_constraint(own, pltpu.HBM)
    return pl.pallas_call(
        functools.partial(attend_kernel, new_count=new_count),
        out_shape=pltpu.VMEM((peers, rows_out, LANES), jnp.bfloat16),
        in_specs=[smem, smem, anywhere, anywhere, vmem],
        out_specs=vmem,
        scratch_shapes=[
            pltpu.VMEM((rows, -(-full // LANES) * LANES, 2 * context), jnp.bfloat16),
            pltpu.SemaphoreType.DMA((2 * rows,)),
        ],
        compiler_params=pltpu.CompilerParams(vmem_limit_bytes=VMEM_LIMIT),
        cost_estimate=pl.CostEstimate(
            flops=4 * count * context * (full + latent) * rows,
            bytes_accessed=2 * rows * context * full * 2 + 2 * peers * rows_out * LANES,
            transcendentals=2 * rows * count * context,
        ),
        name="attend",
    )(scalars, lengths, own, came, query)


def project_kernel(parts_ref, up_ref, proj_ref, out_ref):
    sixteen = 16
    peers, rows_out, _ = parts_ref.shape
    at = rows_out - sixteen
    groups = at // (2 * sixteen)
    heads = up_ref.shape[0]
    blocks = []
    for half in range(2):
        chosen = range(half, peers, 2)
        stat_tiles = [parts_ref[k, at:, :].astype(jnp.float32) for k in chosen]
        for pair in range(2):
            stats = [join_stat(tile, pair) for tile in stat_tiles]
            top = functools.reduce(jnp.maximum, stats)
            weights = [jnp.exp2(stat - top) for stat in stats]
            scale = 1.0 / functools.reduce(jnp.add, weights)
            sums = []
            for g in range(groups):
                start = g * 2 * sixteen + pair * sixteen
                terms = [
                    parts_ref[k, start : start + sixteen, :].astype(jnp.float32) * weight
                    for k, weight in zip(chosen, weights)
                ]
                sums.append(functools.reduce(jnp.add, terms) * scale)
            blocks.append(jnp.concatenate(sums, axis=-1))
    latent = jnp.concatenate(blocks, axis=0).astype(jnp.bfloat16)
    count = latent.shape[0]
    out_row = lax.broadcasted_iota(jnp.int32, (count // heads, count), 0)
    in_row = lax.broadcasted_iota(jnp.int32, (count // heads, count), 1)
    values = []
    for head in range(heads):
        pick = jnp.where(in_row == out_row * heads + head, 1.0, 0.0).astype(jnp.bfloat16)
        own = jnp.dot(pick, latent, preferred_element_type=jnp.float32).astype(jnp.bfloat16)
        values.append(jnp.dot(own, up_ref[head], preferred_element_type=jnp.float32).astype(jnp.bfloat16))
    flat = jnp.concatenate(values, axis=-1)
    width = out_ref.shape[2]
    step = 4
    for first in range(0, out_ref.shape[0], step):
        columns = slice(first * width, (first + step) * width)
        terms = jnp.dot(flat, proj_ref[:, columns], preferred_element_type=jnp.float32)
        for k in range(step):
            out_ref[first + k] = terms[:, k * width : (k + 1) * width].astype(jnp.bfloat16)


def project(parts, value_up, out_proj):
    peers, rows_out, lanes = parts.shape
    heads, latent, _ = value_up.shape
    columns = out_proj.shape[1]
    tokens = (rows_out - 16) // (latent // lanes) * 2 // heads
    vmem = pl.BlockSpec(memory_space=pltpu.VMEM)
    return pl.pallas_call(
        project_kernel,
        out_shape=pltpu.VMEM((peers, tokens, columns // peers), jnp.bfloat16),
        in_specs=[vmem] * 3,
        out_specs=vmem,
        compiler_params=pltpu.CompilerParams(vmem_limit_bytes=16 * 1024 * 1024),
        name="project",
    )(parts, value_up, out_proj)


def total_kernel(terms_ref, out_ref):
    rows, new_count, _ = out_ref.shape
    terms = [terms_ref[k].astype(jnp.float32) for k in range(terms_ref.shape[0])]
    result = functools.reduce(jnp.add, terms).astype(jnp.bfloat16)
    for row in range(rows):
        out_ref[row] = result[row * new_count : (row + 1) * new_count]


def total(terms, rows, new_count):
    vmem = pl.BlockSpec(memory_space=pltpu.VMEM)
    return pl.pallas_call(
        total_kernel,
        out_shape=jax.ShapeDtypeStruct((rows, new_count, terms.shape[2]), jnp.bfloat16),
        in_specs=[vmem],
        out_specs=vmem,
        compiler_params=pltpu.CompilerParams(vmem_limit_bytes=8 * 1024 * 1024),
        name="total",
    )(terms)


def body(latent_cache, queries, lengths, positions, value_up, out_proj):
    row_count, context_dev, full = latent_cache.shape
    new_count, heads_dev = queries.shape[1], queries.shape[2]
    core = lax.axis_index("core")
    shard = lax.axis_index("chip") * 2 + core
    peers = lax.axis_size("chip") * 2
    both = ("chip", "core")
    swap = [(0, 1), (1, 0)]
    cache = jnp.swapaxes(latent_cache, 1, 2)
    came = lax.ppermute(cache, "core", swap)
    cosines, sines = angle_terms(positions, new_count, heads_dev)
    query = lax.all_to_all(spread(queries, cosines, sines, peers), both, 0, 0, tiled=True)
    scalars = jnp.stack([core, shard * context_dev, (shard ^ 1) * context_dev]).astype(jnp.int32)
    mine = attend(scalars, lengths, cache, came, query, new_count)
    parts = lax.all_to_all(mine, both, 0, 0, tiled=True)
    terms = project(parts, value_up, out_proj)
    terms = lax.all_to_all(terms, both, 0, 0, tiled=True)
    return total(terms, row_count, new_count)


def solution(mesh):
    batch, ctx = mesh.devices.shape
    mesh = Mesh(mesh.devices.reshape(batch, ctx // 2, 2), ("batch", "chip", "core"))
    ctx = ("chip", "core")
    in_specs = (
        P("batch", ctx, None),
        P("batch", None, ctx, None),
        P("batch"),
        P("batch"),
        P(ctx, None, None),
        P(ctx, None),
    )
    out_specs = P("batch", None, ctx)
    return jax.shard_map(body, mesh=mesh, in_specs=in_specs, out_specs=out_specs, check_vma=False)
```

```python
import functools
import math

import jax
import jax.numpy as jnp
import numpy as np
from jax import lax
from jax.experimental import pallas as pl
from jax.experimental.pallas import tpu as pltpu
from jax.sharding import Mesh
from jax.sharding import PartitionSpec as P

ROPE = 64
NOPE = 128
LANES = 128
POWER = math.log2(math.e) / math.sqrt(NOPE + ROPE)
HIDDEN = -1e30
VMEM_LIMIT = 24 * 1024 * 1024
LEAST = -1e29


def angles(positions, new_count, repeats):
    half_rope = ROPE // 2
    shape = (new_count * repeats, ROPE)
    lane = lax.broadcasted_iota(jnp.int32, shape, 1)
    frequency = jnp.zeros(shape, jnp.float32)
    for i in range(half_rope):
        value = float(np.float32(50000.0 ** (-2.0 * i / ROPE)))
        frequency = jnp.where(lane % half_rope == i, value, frequency)
    token = lax.broadcasted_iota(jnp.int32, shape, 0) // repeats
    terms = []
    for position in positions:
        angle = (position + token).astype(jnp.float32) * frequency
        sine = jnp.sin(angle)
        terms.append((jnp.cos(angle), jnp.where(lane < half_rope, -sine, sine)))
    return terms


def split_stat(value, lane):
    high = value.astype(jnp.bfloat16).astype(jnp.float32)
    rest = value - high
    middle = rest.astype(jnp.bfloat16).astype(jnp.float32)
    low = rest - middle
    spot = lane % (LANES // 2)
    return jnp.where(spot == 0, high, jnp.where(spot == 1, middle, low))


def join_stat(tile, pair):
    at = pair * (LANES // 2)
    return tile[..., at : at + 1] + tile[..., at + 1 : at + 2] + tile[..., at + 2 : at + 3]


def spread_kernel(query_ref, out_ref, flat_ref):
    rows, new_count, heads, _ = query_ref.shape
    for row in range(rows):
        for token in range(new_count):
            at = (row * new_count + token) * heads
            flat_ref[at : at + heads, :] = query_ref[row, token].astype(jnp.float32)
    flat = flat_ref[...].astype(jnp.bfloat16)
    depth = out_ref.shape[1]
    for peer in range(out_ref.shape[0]):
        at = peer % 2 * depth
        out_ref[peer] = flat[at : at + depth]


def spread(queries, peers):
    rows, new_count, heads, full = queries.shape
    count = rows * new_count * heads
    vmem = pl.BlockSpec(memory_space=pltpu.VMEM)
    return pl.pallas_call(
        spread_kernel,
        out_shape=pltpu.VMEM((peers, count // 2, full), jnp.bfloat16),
        in_specs=[vmem],
        out_specs=vmem,
        scratch_shapes=[pltpu.VMEM((count, full), jnp.float32)],
        compiler_params=pltpu.CompilerParams(vmem_limit_bytes=8 * 1024 * 1024),
        name="spread",
    )(queries)


def attend_kernel(lengths_ref, positions_ref, own_ref, came_ref, query_ref, out_ref, keys_ref, arrived, *, new_count):
    peers, depth, full = query_ref.shape
    rows, wide, context = keys_ref.shape
    span = context // 2
    group = depth // rows
    heads = group // new_count
    latent = full - ROPE
    count = peers * group
    column_groups = latent // LANES
    core = lax.axis_index("core")
    base = core * rows
    starts = [(lax.axis_index("chip") * 2 + place) * span for place in (core, 1 - core)]
    copies = []
    for row in range(rows):
        for side, ref in enumerate((own_ref, came_ref)):
            target = keys_ref.at[row, pl.ds(0, full), pl.ds(side * span, span)]
            copies.append(pltpu.make_async_copy(ref.at[base + row], target, arrived.at[row * 2 + side]))
    for copy in copies:
        copy.start()
    spare = wide - full
    column = lax.broadcasted_iota(jnp.int32, (peers, group, spare), 2)
    member = lax.broadcasted_iota(jnp.int32, (peers, group, spare), 1)
    flags = jnp.where(column == member // heads, 1.0, 0.0)
    place = lax.broadcasted_iota(jnp.int32, (spare, span), 1)
    token = lax.broadcasted_iota(jnp.int32, (spare, span), 0)
    turns = angles([positions_ref[base + row] for row in range(rows)], new_count, heads)
    queries = []
    for row in range(rows):
        for side in range(2):
            limit = lengths_ref[base + row] - new_count + 1 - starts[side]
            hidden = (token < new_count) & (place >= limit + token)
            keys_ref[row, full:, side * span : (side + 1) * span] = jnp.where(hidden, HIDDEN, 0.0).astype(jnp.bfloat16)
        query = query_ref[:, row // 2 * 2 * group : (row // 2 + 1) * 2 * group, :].astype(jnp.float32)
        query = query[:, row % 2 * group : (row % 2 + 1) * group, :]
        rope = query[:, :, latent:]
        swapped = jnp.concatenate([rope[:, :, ROPE // 2 :], rope[:, :, : ROPE // 2]], axis=-1)
        turned = rope * turns[row][0][None] + swapped * turns[row][1][None]
        query = jnp.concatenate([query[:, :, :latent], turned, flags], axis=-1)
        queries.append(query.reshape(count, wide).astype(jnp.bfloat16))

    def score(row):
        halves = []
        for side in range(2):
            copies[2 * row + side].wait()
            keys = keys_ref[row, :, side * span : (side + 1) * span]
            halves.append(jnp.dot(queries[row], keys, preferred_element_type=jnp.float32))
        scores = jnp.concatenate(halves, axis=-1)
        return scores, jnp.maximum(jnp.max(scores, axis=-1, keepdims=True), LEAST)

    sixteen = 2 * group
    at = column_groups * depth
    closed, packed = [], []
    ahead = score(0)
    for row in range(rows):
        scores, top = ahead
        if row + 1 < rows:
            ahead = score(row + 1)
        weights = jnp.exp2((scores - top) * POWER)
        total = jnp.sum(weights, axis=-1, keepdims=True)
        out = lax.dot_general(
            weights.astype(jnp.bfloat16),
            keys_ref[row, :latent],
            (((1,), (1,)), ((), ())),
            preferred_element_type=jnp.float32,
        )
        seen = total > 0.0
        safe = jnp.where(seen, total, 1.0)
        out = out * (1.0 / safe)
        stat = jnp.where(seen, top * POWER + jnp.log2(safe), HIDDEN)
        stat = jnp.broadcast_to(stat, (count, LANES)).reshape(peers, group, LANES)
        closed.append((out.reshape(peers, group, latent), stat))
        if row % 2 == 1:
            pair = row // 2
            (out_a, stat_a), (out_b, stat_b) = closed[-2:]
            both = jnp.concatenate([out_a, out_b], axis=1).astype(jnp.bfloat16)
            for g in range(column_groups):
                start = g * depth + pair * sixteen
                out_ref[:, start : start + sixteen, :] = both[:, :, g * LANES : (g + 1) * LANES]
            stats = jnp.concatenate([stat_a, stat_b], axis=1)
            lane = lax.broadcasted_iota(jnp.int32, stats.shape, 2)
            packed.append(split_stat(stats, lane))
    lane = lax.broadcasted_iota(jnp.int32, packed[0].shape, 2)
    out_ref[:, at : at + sixteen, :] = jnp.where(lane < LANES // 2, packed[0], packed[1]).astype(jnp.bfloat16)


def attend(lengths, positions, own, came, query, new_count):
    peers, depth, full = query.shape
    rows = own.shape[0] // 2
    context = own.shape[2]
    latent = full - ROPE
    rows_out = latent // LANES * depth + depth // rows * 2
    count = peers * depth // rows
    smem, vmem, anywhere = (pl.BlockSpec(memory_space=s) for s in (pltpu.SMEM, pltpu.VMEM, pl.ANY))
    own = pltpu.with_memory_space_constraint(own, pltpu.HBM)
    return pl.pallas_call(
        functools.partial(attend_kernel, new_count=new_count),
        out_shape=pltpu.VMEM((peers, rows_out, LANES), jnp.bfloat16),
        in_specs=[smem, smem, anywhere, anywhere, vmem],
        out_specs=vmem,
        scratch_shapes=[
            pltpu.VMEM((rows, -(-full // LANES) * LANES, 2 * context), jnp.bfloat16),
            pltpu.SemaphoreType.DMA((2 * rows,)),
        ],
        compiler_params=pltpu.CompilerParams(vmem_limit_bytes=VMEM_LIMIT),
        cost_estimate=pl.CostEstimate(
            flops=4 * count * context * (full + latent) * rows,
            bytes_accessed=2 * rows * context * full * 2 + 2 * peers * rows_out * LANES,
            transcendentals=2 * rows * count * context,
        ),
        name="attend",
    )(lengths, positions, own, came, query)


def project_kernel(parts_ref, up_ref, proj_ref, out_ref):
    sixteen = 16
    peers, rows_out, _ = parts_ref.shape
    at = rows_out - sixteen
    groups = at // (2 * sixteen)
    heads = up_ref.shape[0]
    blocks = []
    for half in range(2):
        chosen = range(half, peers, 2)
        stat_tiles = [parts_ref[k, at:, :].astype(jnp.float32) for k in chosen]
        for pair in range(2):
            stats = [join_stat(tile, pair) for tile in stat_tiles]
            top = functools.reduce(jnp.maximum, stats)
            weights = [jnp.exp2(stat - top) for stat in stats]
            scale = 1.0 / functools.reduce(jnp.add, weights)
            sums = []
            for g in range(groups):
                start = g * 2 * sixteen + pair * sixteen
                terms = [
                    parts_ref[k, start : start + sixteen, :].astype(jnp.float32) * weight
                    for k, weight in zip(chosen, weights)
                ]
                sums.append(functools.reduce(jnp.add, terms) * scale)
            blocks.append(jnp.concatenate(sums, axis=-1))
    latent = jnp.concatenate(blocks, axis=0).astype(jnp.bfloat16)
    count = latent.shape[0]
    out_row = lax.broadcasted_iota(jnp.int32, (count // heads, count), 0)
    in_row = lax.broadcasted_iota(jnp.int32, (count // heads, count), 1)
    values = []
    for head in range(heads):
        pick = jnp.where(in_row == out_row * heads + head, 1.0, 0.0).astype(jnp.bfloat16)
        own = jnp.dot(pick, latent, preferred_element_type=jnp.float32).astype(jnp.bfloat16)
        values.append(jnp.dot(own, up_ref[head], preferred_element_type=jnp.float32).astype(jnp.bfloat16))
    flat = jnp.concatenate(values, axis=-1)
    width = out_ref.shape[2]
    step = 4
    for first in range(0, out_ref.shape[0], step):
        columns = slice(first * width, (first + step) * width)
        terms = jnp.dot(flat, proj_ref[:, columns], preferred_element_type=jnp.float32)
        for k in range(step):
            out_ref[first + k] = terms[:, k * width : (k + 1) * width].astype(jnp.bfloat16)


def project(parts, value_up, out_proj):
    peers, rows_out, lanes = parts.shape
    heads, latent, _ = value_up.shape
    columns = out_proj.shape[1]
    tokens = (rows_out - 16) // (latent // lanes) * 2 // heads
    vmem = pl.BlockSpec(memory_space=pltpu.VMEM)
    return pl.pallas_call(
        project_kernel,
        out_shape=pltpu.VMEM((peers, tokens, columns // peers), jnp.bfloat16),
        in_specs=[vmem] * 3,
        out_specs=vmem,
        compiler_params=pltpu.CompilerParams(vmem_limit_bytes=16 * 1024 * 1024),
        name="project",
    )(parts, value_up, out_proj)


def total_kernel(terms_ref, out_ref):
    rows, new_count, _ = out_ref.shape
    terms = [terms_ref[k].astype(jnp.float32) for k in range(terms_ref.shape[0])]
    result = functools.reduce(jnp.add, terms).astype(jnp.bfloat16)
    for row in range(rows):
        out_ref[row] = result[row * new_count : (row + 1) * new_count]


def total(terms, rows, new_count):
    vmem = pl.BlockSpec(memory_space=pltpu.VMEM)
    return pl.pallas_call(
        total_kernel,
        out_shape=jax.ShapeDtypeStruct((rows, new_count, terms.shape[2]), jnp.bfloat16),
        in_specs=[vmem],
        out_specs=vmem,
        compiler_params=pltpu.CompilerParams(vmem_limit_bytes=8 * 1024 * 1024),
        name="total",
    )(terms)


def body(latent_cache, queries, lengths, positions, value_up, out_proj):
    row_count, new_count = queries.shape[:2]
    peers = lax.axis_size("chip") * 2
    both = ("chip", "core")
    swap = [(0, 1), (1, 0)]
    cache = jnp.swapaxes(latent_cache, 1, 2)
    came = lax.ppermute(cache, "core", swap)
    query = lax.all_to_all(spread(queries, peers), both, 0, 0, tiled=True)
    mine = attend(lengths, positions, cache, came, query, new_count)
    parts = lax.all_to_all(mine, both, 0, 0, tiled=True)
    terms = project(parts, value_up, out_proj)
    terms = lax.all_to_all(terms, both, 0, 0, tiled=True)
    return total(terms, row_count, new_count)


def solution(mesh):
    batch, ctx = mesh.devices.shape
    mesh = Mesh(mesh.devices.reshape(batch, ctx // 2, 2), ("batch", "chip", "core"))
    ctx = ("chip", "core")
    in_specs = (
        P("batch", ctx, None),
        P("batch", None, ctx, None),
        P("batch"),
        P("batch"),
        P(ctx, None, None),
        P(ctx, None),
    )
    out_specs = P("batch", None, ctx)
    return jax.shard_map(body, mesh=mesh, in_specs=in_specs, out_specs=out_specs, check_vma=False)
```

```python
import functools
import math

import jax
import jax.numpy as jnp
import numpy as np
from jax import lax
from jax.experimental import pallas as pl
from jax.experimental.pallas import tpu as pltpu
from jax.sharding import Mesh
from jax.sharding import PartitionSpec as P

ROPE = 64
NOPE = 128
LANES = 128
POWER = math.log2(math.e) / math.sqrt(NOPE + ROPE)
HIDDEN = -1e30
STRIP = 16
VMEM_LIMIT = 24 * 1024 * 1024
LEAST = -1e29


def angles(positions, new_count, repeats):
    half_rope = ROPE // 2
    shape = (new_count * repeats, ROPE)
    lane = lax.broadcasted_iota(jnp.int32, shape, 1)
    frequency = jnp.zeros(shape, jnp.float32)
    for i in range(half_rope):
        value = float(np.float32(50000.0 ** (-2.0 * i / ROPE)))
        frequency = jnp.where(lane % half_rope == i, value, frequency)
    token = lax.broadcasted_iota(jnp.int32, shape, 0) // repeats
    terms = []
    for position in positions:
        angle = (position + token).astype(jnp.float32) * frequency
        sine = jnp.sin(angle)
        terms.append((jnp.cos(angle), jnp.where(lane < half_rope, -sine, sine)))
    return terms


def split_stat(value, lane):
    high = value.astype(jnp.bfloat16).astype(jnp.float32)
    rest = value - high
    middle = rest.astype(jnp.bfloat16).astype(jnp.float32)
    low = rest - middle
    spot = lane % (LANES // 2)
    return jnp.where(spot == 0, high, jnp.where(spot == 1, middle, low))


def join_stat(tile, pair):
    at = pair * (LANES // 2)
    return tile[..., at : at + 1] + tile[..., at + 1 : at + 2] + tile[..., at + 2 : at + 3]


def spread_kernel(query_ref, out_ref, flat_ref):
    rows, new_count, heads, _ = query_ref.shape
    for row in range(rows):
        for token in range(new_count):
            at = (row * new_count + token) * heads
            flat_ref[at : at + heads, :] = query_ref[row, token].astype(jnp.float32)
    flat = flat_ref[...].astype(jnp.bfloat16)
    depth = out_ref.shape[1]
    for peer in range(out_ref.shape[0]):
        at = peer % 2 * depth
        out_ref[peer] = flat[at : at + depth]


def spread(queries, peers):
    rows, new_count, heads, full = queries.shape
    count = rows * new_count * heads
    vmem = pl.BlockSpec(memory_space=pltpu.VMEM)
    return pl.pallas_call(
        spread_kernel,
        out_shape=pltpu.VMEM((peers, count // 2, full), jnp.bfloat16),
        in_specs=[vmem],
        out_specs=vmem,
        scratch_shapes=[pltpu.VMEM((count, full), jnp.float32)],
        compiler_params=pltpu.CompilerParams(vmem_limit_bytes=8 * 1024 * 1024),
        name="spread",
    )(queries)


def attend_kernel(lengths_ref, positions_ref, own_ref, came_ref, query_ref, out_ref, keys_ref, arrived, *, new_count):
    peers, depth, full = query_ref.shape
    rows, wide, context = keys_ref.shape
    span = context // 2
    group = depth // rows
    heads = group // new_count
    latent = full - ROPE
    count = peers * group
    column_groups = latent // LANES
    core = lax.axis_index("core")
    base = core * rows
    starts = [(lax.axis_index("chip") * 2 + place) * span for place in (core, 1 - core)]
    copies = []
    for row in range(rows):
        for side, ref in enumerate((own_ref, came_ref)):
            target = keys_ref.at[row, pl.ds(0, full), pl.ds(side * span, span)]
            copies.append(pltpu.make_async_copy(ref.at[base + row], target, arrived.at[row * 2 + side]))
    for copy in copies:
        copy.start()
    spare = wide - full
    column = lax.broadcasted_iota(jnp.int32, (peers, group, spare), 2)
    member = lax.broadcasted_iota(jnp.int32, (peers, group, spare), 1)
    flags = jnp.where(column == member // heads, 1.0, 0.0)
    place = lax.broadcasted_iota(jnp.int32, (spare, span), 1)
    token = lax.broadcasted_iota(jnp.int32, (spare, span), 0)
    turns = angles([positions_ref[base + row] for row in range(rows)], new_count, heads)
    queries = []
    for row in range(rows):
        for side in range(2):
            limit = lengths_ref[base + row] - new_count + 1 - starts[side]
            hidden = (token < new_count) & (place >= limit + token)
            keys_ref[row, full:, side * span : (side + 1) * span] = jnp.where(hidden, HIDDEN, 0.0).astype(jnp.bfloat16)
        query = query_ref[:, row // 2 * 2 * group : (row // 2 + 1) * 2 * group, :].astype(jnp.float32)
        query = query[:, row % 2 * group : (row % 2 + 1) * group, :]
        rope = query[:, :, latent:]
        swapped = jnp.concatenate([rope[:, :, ROPE // 2 :], rope[:, :, : ROPE // 2]], axis=-1)
        turned = rope * turns[row][0][None] + swapped * turns[row][1][None]
        query = jnp.concatenate([query[:, :, :latent], turned, flags], axis=-1)
        queries.append(query.reshape(count, wide).astype(jnp.bfloat16))

    def score(row):
        copies[2 * row].wait()
        copies[2 * row + 1].wait()
        scores = jnp.dot(queries[row], keys_ref[row], preferred_element_type=jnp.float32)
        return scores

    sixteen = 2 * group
    at = column_groups * depth
    closed, packed = [], []
    ahead = score(0)
    for row in range(rows):
        scores = ahead
        if row + 1 < rows:
            ahead = score(row + 1)
        tops, totals, strips = [], [], []
        for first in range(0, count, STRIP):
            strip = scores[first : first + STRIP]
            tops.append(jnp.maximum(jnp.max(strip, axis=-1, keepdims=True), LEAST))
            strip = jnp.exp2((strip - tops[-1]) * POWER)
            totals.append(jnp.sum(strip, axis=-1, keepdims=True))
            strips.append(strip.astype(jnp.bfloat16))
        top, total = jnp.concatenate(tops, axis=0), jnp.concatenate(totals, axis=0)
        out = lax.dot_general(
            jnp.concatenate(strips, axis=0),
            keys_ref[row, :latent],
            (((1,), (1,)), ((), ())),
            preferred_element_type=jnp.float32,
        )
        seen = total > 0.0
        safe = jnp.where(seen, total, 1.0)
        out = out * (1.0 / safe)
        stat = jnp.where(seen, top * POWER + jnp.log2(safe), HIDDEN)
        stat = jnp.broadcast_to(stat, (count, LANES)).reshape(peers, group, LANES)
        closed.append((out.reshape(peers, group, latent), stat))
        if row % 2 == 1:
            pair = row // 2
            (out_a, stat_a), (out_b, stat_b) = closed[-2:]
            both = jnp.concatenate([out_a, out_b], axis=1).astype(jnp.bfloat16)
            for g in range(column_groups):
                start = g * depth + pair * sixteen
                out_ref[:, start : start + sixteen, :] = both[:, :, g * LANES : (g + 1) * LANES]
            stats = jnp.concatenate([stat_a, stat_b], axis=1)
            lane = lax.broadcasted_iota(jnp.int32, stats.shape, 2)
            packed.append(split_stat(stats, lane))
    lane = lax.broadcasted_iota(jnp.int32, packed[0].shape, 2)
    out_ref[:, at : at + sixteen, :] = jnp.where(lane < LANES // 2, packed[0], packed[1]).astype(jnp.bfloat16)


def attend(lengths, positions, own, came, query, new_count):
    peers, depth, full = query.shape
    rows = own.shape[0] // 2
    context = own.shape[2]
    latent = full - ROPE
    rows_out = latent // LANES * depth + depth // rows * 2
    count = peers * depth // rows
    smem, vmem, anywhere = (pl.BlockSpec(memory_space=s) for s in (pltpu.SMEM, pltpu.VMEM, pl.ANY))
    own = pltpu.with_memory_space_constraint(own, pltpu.HBM)
    return pl.pallas_call(
        functools.partial(attend_kernel, new_count=new_count),
        out_shape=pltpu.VMEM((peers, rows_out, LANES), jnp.bfloat16),
        in_specs=[smem, smem, anywhere, anywhere, vmem],
        out_specs=vmem,
        scratch_shapes=[
            pltpu.VMEM((rows, -(-full // LANES) * LANES, 2 * context), jnp.bfloat16),
            pltpu.SemaphoreType.DMA((2 * rows,)),
        ],
        compiler_params=pltpu.CompilerParams(vmem_limit_bytes=VMEM_LIMIT),
        cost_estimate=pl.CostEstimate(
            flops=4 * count * context * (full + latent) * rows,
            bytes_accessed=2 * rows * context * full * 2 + 2 * peers * rows_out * LANES,
            transcendentals=2 * rows * count * context,
        ),
        name="attend",
    )(lengths, positions, own, came, query)


def project_kernel(parts_ref, up_ref, proj_ref, out_ref):
    sixteen = 16
    peers, rows_out, _ = parts_ref.shape
    at = rows_out - sixteen
    groups = at // (2 * sixteen)
    heads = up_ref.shape[0]
    blocks = []
    for half in range(2):
        chosen = range(half, peers, 2)
        stat_tiles = [parts_ref[k, at:, :].astype(jnp.float32) for k in chosen]
        for pair in range(2):
            stats = [join_stat(tile, pair) for tile in stat_tiles]
            top = functools.reduce(jnp.maximum, stats)
            weights = [jnp.exp2(stat - top) for stat in stats]
            scale = 1.0 / functools.reduce(jnp.add, weights)
            sums = []
            for g in range(groups):
                start = g * 2 * sixteen + pair * sixteen
                terms = [
                    parts_ref[k, start : start + sixteen, :].astype(jnp.float32) * weight
                    for k, weight in zip(chosen, weights)
                ]
                sums.append(functools.reduce(jnp.add, terms) * scale)
            blocks.append(jnp.concatenate(sums, axis=-1))
    latent = jnp.concatenate(blocks, axis=0).astype(jnp.bfloat16)
    count = latent.shape[0]
    out_row = lax.broadcasted_iota(jnp.int32, (count // heads, count), 0)
    in_row = lax.broadcasted_iota(jnp.int32, (count // heads, count), 1)
    values = []
    for head in range(heads):
        pick = jnp.where(in_row == out_row * heads + head, 1.0, 0.0).astype(jnp.bfloat16)
        own = jnp.dot(pick, latent, preferred_element_type=jnp.float32).astype(jnp.bfloat16)
        values.append(jnp.dot(own, up_ref[head], preferred_element_type=jnp.float32).astype(jnp.bfloat16))
    flat = jnp.concatenate(values, axis=-1)
    width = out_ref.shape[2]
    step = 4
    for first in range(0, out_ref.shape[0], step):
        columns = slice(first * width, (first + step) * width)
        terms = jnp.dot(flat, proj_ref[:, columns], preferred_element_type=jnp.float32)
        for k in range(step):
            out_ref[first + k] = terms[:, k * width : (k + 1) * width].astype(jnp.bfloat16)


def project(parts, value_up, out_proj):
    peers, rows_out, lanes = parts.shape
    heads, latent, _ = value_up.shape
    columns = out_proj.shape[1]
    tokens = (rows_out - 16) // (latent // lanes) * 2 // heads
    vmem = pl.BlockSpec(memory_space=pltpu.VMEM)
    return pl.pallas_call(
        project_kernel,
        out_shape=pltpu.VMEM((peers, tokens, columns // peers), jnp.bfloat16),
        in_specs=[vmem] * 3,
        out_specs=vmem,
        compiler_params=pltpu.CompilerParams(vmem_limit_bytes=16 * 1024 * 1024),
        name="project",
    )(parts, value_up, out_proj)


def total_kernel(terms_ref, out_ref):
    rows, new_count, _ = out_ref.shape
    terms = [terms_ref[k].astype(jnp.float32) for k in range(terms_ref.shape[0])]
    result = functools.reduce(jnp.add, terms).astype(jnp.bfloat16)
    for row in range(rows):
        out_ref[row] = result[row * new_count : (row + 1) * new_count]


def total(terms, rows, new_count):
    vmem = pl.BlockSpec(memory_space=pltpu.VMEM)
    return pl.pallas_call(
        total_kernel,
        out_shape=jax.ShapeDtypeStruct((rows, new_count, terms.shape[2]), jnp.bfloat16),
        in_specs=[vmem],
        out_specs=vmem,
        compiler_params=pltpu.CompilerParams(vmem_limit_bytes=8 * 1024 * 1024),
        name="total",
    )(terms)


def body(latent_cache, queries, lengths, positions, value_up, out_proj):
    row_count, new_count = queries.shape[:2]
    peers = lax.axis_size("chip") * 2
    both = ("chip", "core")
    swap = [(0, 1), (1, 0)]
    cache = jnp.swapaxes(latent_cache, 1, 2)
    came = lax.ppermute(cache, "core", swap)
    query = lax.all_to_all(spread(queries, peers), both, 0, 0, tiled=True)
    mine = attend(lengths, positions, cache, came, query, new_count)
    mine, value_up, out_proj = lax.optimization_barrier((mine, value_up, out_proj))
    parts = lax.all_to_all(mine, both, 0, 0, tiled=True)
    terms = project(parts, value_up, out_proj)
    terms = lax.all_to_all(terms, both, 0, 0, tiled=True)
    return total(terms, row_count, new_count)


def solution(mesh):
    batch, ctx = mesh.devices.shape
    mesh = Mesh(mesh.devices.reshape(batch, ctx // 2, 2), ("batch", "chip", "core"))
    ctx = ("chip", "core")
    in_specs = (
        P("batch", ctx, None),
        P("batch", None, ctx, None),
        P("batch"),
        P("batch"),
        P(ctx, None, None),
        P(ctx, None),
    )
    out_specs = P("batch", None, ctx)
    return jax.shard_map(body, mesh=mesh, in_specs=in_specs, out_specs=out_specs, check_vma=False)
```

```python
import functools
import math

import jax
import jax.numpy as jnp
import numpy as np
from jax import lax
from jax.experimental import pallas as pl
from jax.experimental.pallas import tpu as pltpu
from jax.sharding import Mesh
from jax.sharding import PartitionSpec as P

ROPE = 64
NOPE = 128
LANES = 128
STAT_LANES = 32
POWER = math.log2(math.e) / math.sqrt(NOPE + ROPE)
HIDDEN = -1e30
STRIP = 16
VMEM_LIMIT = 24 * 1024 * 1024
LEAST = -1e29


def angles(positions, new_count, repeats):
    half_rope = ROPE // 2
    shape = (new_count * repeats, ROPE)
    lane = lax.broadcasted_iota(jnp.int32, shape, 1)
    frequency = jnp.zeros(shape, jnp.float32)
    for i in range(half_rope):
        value = float(np.float32(50000.0 ** (-2.0 * i / ROPE)))
        frequency = jnp.where(lane % half_rope == i, value, frequency)
    token = lax.broadcasted_iota(jnp.int32, shape, 0) // repeats
    terms = []
    for position in positions:
        angle = (position + token).astype(jnp.float32) * frequency
        sine = jnp.sin(angle)
        terms.append((jnp.cos(angle), jnp.where(lane < half_rope, -sine, sine)))
    return terms


def split_stat(value, lane):
    high = value.astype(jnp.bfloat16).astype(jnp.float32)
    rest = value - high
    middle = rest.astype(jnp.bfloat16).astype(jnp.float32)
    low = rest - middle
    spot = lane % STAT_LANES
    return jnp.where(spot == 0, high, jnp.where(spot == 1, middle, low))


def join_stat(tile, row):
    at = row * STAT_LANES
    return tile[..., at : at + 1] + tile[..., at + 1 : at + 2] + tile[..., at + 2 : at + 3]


def spread_kernel(query_ref, out_ref, flat_ref):
    rows, new_count, heads, full = query_ref.shape
    latent = full - ROPE
    for row in range(rows):
        for token in range(new_count):
            at = (row * new_count + token) * heads
            flat_ref[at : at + heads, :] = query_ref[row, token].astype(jnp.float32)
    flat = flat_ref[...]
    depth = flat.shape[0] // 2
    for half in range(2):
        mine = flat[half * depth : (half + 1) * depth]
        pieces = [mine[:, g : g + LANES] for g in range(0, latent, LANES)]
        pieces.append(jnp.concatenate([mine[: depth // 2, latent:], mine[depth // 2 :, latent:]], axis=-1))
        block = jnp.concatenate(pieces, axis=0).astype(jnp.bfloat16)
        for peer in range(half, out_ref.shape[0], 2):
            out_ref[peer] = block


def spread(queries, peers):
    rows, new_count, heads, full = queries.shape
    count = rows * new_count * heads
    vmem = pl.BlockSpec(memory_space=pltpu.VMEM)
    return pl.pallas_call(
        spread_kernel,
        out_shape=pltpu.VMEM((peers, count // 2 * full // LANES, LANES), jnp.bfloat16),
        in_specs=[vmem],
        out_specs=vmem,
        scratch_shapes=[pltpu.VMEM((count, full), jnp.float32)],
        compiler_params=pltpu.CompilerParams(vmem_limit_bytes=8 * 1024 * 1024),
        name="spread",
    )(queries)


def attend_kernel(lengths_ref, positions_ref, own_ref, came_ref, query_ref, out_ref, keys_ref, arrived, *, new_count):
    peers = query_ref.shape[0]
    full = own_ref.shape[1]
    rows, wide, context = keys_ref.shape
    span = context // 2
    latent = full - ROPE
    column_groups = latent // LANES
    depth = query_ref.shape[1] * LANES // full
    group = depth // rows
    heads = group // new_count
    count = peers * group
    core = lax.axis_index("core")
    base = core * rows
    starts = [(lax.axis_index("chip") * 2 + place) * span for place in (core, 1 - core)]
    copies = []
    for row in range(rows):
        for side, ref in enumerate((own_ref, came_ref)):
            target = keys_ref.at[row, pl.ds(0, full), pl.ds(side * span, span)]
            copies.append(pltpu.make_async_copy(ref.at[base + row], target, arrived.at[row * 2 + side]))
    for copy in copies:
        copy.start()
    spare = wide - full
    column = lax.broadcasted_iota(jnp.int32, (peers, group, spare), 2)
    member = lax.broadcasted_iota(jnp.int32, (peers, group, spare), 1)
    flags = jnp.where(column == member // heads, 1.0, 0.0)
    place = lax.broadcasted_iota(jnp.int32, (spare, span), 1)
    token = lax.broadcasted_iota(jnp.int32, (spare, span), 0)
    turns = angles([positions_ref[base + row] for row in range(rows)], new_count, heads)
    queries = []
    for row in range(rows):
        for side in range(2):
            limit = lengths_ref[base + row] - new_count + 1 - starts[side]
            hidden = (token < new_count) & (place >= limit + token)
            keys_ref[row, full:, side * span : (side + 1) * span] = jnp.where(hidden, HIDDEN, 0.0).astype(jnp.bfloat16)
        tile, upper = row // 2 * 2 * group, slice(row % 2 * group, (row % 2 + 1) * group)
        pieces = []
        for g in range(column_groups):
            piece = query_ref[:, g * depth + tile : g * depth + tile + 2 * group, :].astype(jnp.float32)
            pieces.append(piece[:, upper])
        rope = query_ref[:, column_groups * depth :, :].astype(jnp.float32)
        rope = rope[:, upper, row // 2 * ROPE : (row // 2 + 1) * ROPE]
        swapped = jnp.concatenate([rope[:, :, ROPE // 2 :], rope[:, :, : ROPE // 2]], axis=-1)
        turned = rope * turns[row][0][None] + swapped * turns[row][1][None]
        query = jnp.concatenate([*pieces, turned, flags], axis=-1)
        queries.append(query.reshape(count, wide).astype(jnp.bfloat16))

    def score(row):
        copies[2 * row].wait()
        copies[2 * row + 1].wait()
        scores = jnp.dot(queries[row], keys_ref[row], preferred_element_type=jnp.float32)
        return scores

    sixteen = 2 * group
    at = column_groups * depth
    closed, packed = [], None
    lane = lax.broadcasted_iota(jnp.int32, (peers, group, LANES), 2)
    ahead = score(0)
    for row in range(rows):
        scores = ahead
        if row + 1 < rows:
            ahead = score(row + 1)
        tops, totals, strips = [], [], []
        for first in range(0, count, STRIP):
            strip = scores[first : first + STRIP]
            tops.append(jnp.maximum(jnp.max(strip, axis=-1, keepdims=True), LEAST))
            strip = jnp.exp2((strip - tops[-1]) * POWER)
            totals.append(jnp.sum(strip, axis=-1, keepdims=True))
            strips.append(strip.astype(jnp.bfloat16))
        top, total = jnp.concatenate(tops, axis=0), jnp.concatenate(totals, axis=0)
        out = lax.dot_general(
            jnp.concatenate(strips, axis=0),
            keys_ref[row, :latent],
            (((1,), (1,)), ((), ())),
            preferred_element_type=jnp.float32,
        )
        seen = total > 0.0
        safe = jnp.where(seen, total, 1.0)
        out = out * (1.0 / safe)
        stat = jnp.where(seen, top * POWER + jnp.log2(safe), HIDDEN)
        stat = jnp.broadcast_to(stat, (count, LANES)).reshape(peers, group, LANES)
        closed.append(out.reshape(peers, group, latent))
        stat = split_stat(stat, lane)
        packed = stat if packed is None else jnp.where(lane < row * STAT_LANES, packed, stat)
        if row % 2 == 1:
            both = jnp.concatenate(closed[-2:], axis=1).astype(jnp.bfloat16)
            for g in range(column_groups):
                start = g * depth + row // 2 * sixteen
                out_ref[:, start : start + sixteen, :] = both[:, :, g * LANES : (g + 1) * LANES]
    out_ref[:, at:, :] = packed.astype(jnp.bfloat16)


def attend(lengths, positions, own, came, query, new_count):
    peers = query.shape[0]
    rows = own.shape[0] // 2
    full, context = own.shape[1:]
    latent = full - ROPE
    depth = query.shape[1] * LANES // full
    group = depth // rows
    rows_out = latent // LANES * depth + group
    count = peers * group
    smem, vmem, anywhere = (pl.BlockSpec(memory_space=s) for s in (pltpu.SMEM, pltpu.VMEM, pl.ANY))
    own = pltpu.with_memory_space_constraint(own, pltpu.HBM)
    return pl.pallas_call(
        functools.partial(attend_kernel, new_count=new_count),
        out_shape=pltpu.VMEM((peers, rows_out, LANES), jnp.bfloat16),
        in_specs=[smem, smem, anywhere, anywhere, vmem],
        out_specs=vmem,
        scratch_shapes=[
            pltpu.VMEM((rows, -(-full // LANES) * LANES, 2 * context), jnp.bfloat16),
            pltpu.SemaphoreType.DMA((2 * rows,)),
        ],
        compiler_params=pltpu.CompilerParams(vmem_limit_bytes=VMEM_LIMIT),
        cost_estimate=pl.CostEstimate(
            flops=4 * count * context * (full + latent) * rows,
            bytes_accessed=2 * rows * context * full * 2 + 2 * peers * rows_out * LANES,
            transcendentals=2 * rows * count * context,
        ),
        name="attend",
    )(lengths, positions, own, came, query)


def project_kernel(parts_ref, up_ref, proj_ref, out_ref):
    sixteen = 16
    peers, rows_out, _ = parts_ref.shape
    heads, wide, _ = up_ref.shape
    groups = wide // LANES
    at = rows_out - rows_out % sixteen
    depth = at // groups
    blocks = []
    for half in range(2):
        chosen = range(half, peers, 2)
        stat_tiles = [parts_ref[k, at:, :].astype(jnp.float32) for k in chosen]
        for pair in range(2):
            stats = [
                jnp.concatenate([join_stat(tile, 2 * pair), join_stat(tile, 2 * pair + 1)], axis=0)
                for tile in stat_tiles
            ]
            top = functools.reduce(jnp.maximum, stats)
            weights = [jnp.exp2(stat - top) for stat in stats]
            scale = 1.0 / functools.reduce(jnp.add, weights)
            sums = []
            for g in range(groups):
                start = g * depth + pair * sixteen
                terms = [
                    parts_ref[k, start : start + sixteen, :].astype(jnp.float32) * weight
                    for k, weight in zip(chosen, weights)
                ]
                sums.append(functools.reduce(jnp.add, terms) * scale)
            blocks.append(jnp.concatenate(sums, axis=-1))
    latent = jnp.concatenate(blocks, axis=0).astype(jnp.bfloat16)
    count = latent.shape[0]
    out_row = lax.broadcasted_iota(jnp.int32, (count // heads, count), 0)
    in_row = lax.broadcasted_iota(jnp.int32, (count // heads, count), 1)
    values = []
    for head in range(heads):
        pick = jnp.where(in_row == out_row * heads + head, 1.0, 0.0).astype(jnp.bfloat16)
        own = jnp.dot(pick, latent, preferred_element_type=jnp.float32).astype(jnp.bfloat16)
        values.append(jnp.dot(own, up_ref[head], preferred_element_type=jnp.float32).astype(jnp.bfloat16))
    flat = jnp.concatenate(values, axis=-1)
    width = proj_ref.shape[1] // peers
    step = 4
    for first in range(0, peers, step):
        columns = slice(first * width, (first + step) * width)
        terms = jnp.dot(flat, proj_ref[:, columns], preferred_element_type=jnp.float32)
        for k in range(step):
            out_ref[first + k] = fold(terms[:, k * width : (k + 1) * width]).astype(jnp.bfloat16)


def fold(block):
    lines, width = block.shape
    part = lines // 4
    thin = LANES // 4
    pieces = [block[:, :LANES]]
    for at in range(LANES, width, thin):
        pieces.append(
            jnp.concatenate([block[m * part : (m + 1) * part, at : at + thin] for m in range(4)], axis=-1)
        )
    return jnp.concatenate(pieces, axis=0)


def unfold(block, lines):
    part = lines // 4
    thin = LANES // 4
    pieces = [block[:lines]]
    for at in range(lines, block.shape[0], part):
        pieces.append(
            jnp.concatenate([block[at : at + part, m * thin : (m + 1) * thin] for m in range(4)], axis=0)
        )
    return jnp.concatenate(pieces, axis=-1)


def project(parts, value_up, out_proj):
    peers, rows_out, _ = parts.shape
    heads, latent, _ = value_up.shape
    columns = out_proj.shape[1]
    tokens = rows_out // 16 * 16 // (latent // LANES) * 2 // heads
    lines = tokens * (columns // peers) // LANES
    vmem = pl.BlockSpec(memory_space=pltpu.VMEM)
    return pl.pallas_call(
        project_kernel,
        out_shape=pltpu.VMEM((peers, lines, LANES), jnp.bfloat16),
        in_specs=[vmem] * 3,
        out_specs=vmem,
        compiler_params=pltpu.CompilerParams(vmem_limit_bytes=16 * 1024 * 1024),
        name="project",
    )(parts, value_up, out_proj)


def total_kernel(terms_ref, out_ref):
    rows, new_count, _ = out_ref.shape
    terms = [terms_ref[k].astype(jnp.float32) for k in range(terms_ref.shape[0])]
    result = unfold(functools.reduce(jnp.add, terms), rows * new_count).astype(jnp.bfloat16)
    for row in range(rows):
        out_ref[row] = result[row * new_count : (row + 1) * new_count]


def total(terms, rows, new_count):
    peers, lines, _ = terms.shape
    vmem = pl.BlockSpec(memory_space=pltpu.VMEM)
    return pl.pallas_call(
        total_kernel,
        out_shape=jax.ShapeDtypeStruct((rows, new_count, lines * LANES // (rows * new_count)), jnp.bfloat16),
        in_specs=[vmem],
        out_specs=vmem,
        compiler_params=pltpu.CompilerParams(vmem_limit_bytes=8 * 1024 * 1024),
        name="total",
    )(terms)


def body(latent_cache, queries, lengths, positions, value_up, out_proj):
    row_count, new_count = queries.shape[:2]
    peers = lax.axis_size("chip") * 2
    both = ("chip", "core")
    swap = [(0, 1), (1, 0)]
    cache = jnp.swapaxes(latent_cache, 1, 2)
    came = lax.ppermute(cache, "core", swap)
    query = lax.all_to_all(spread(queries, peers), both, 0, 0, tiled=True)
    mine = attend(lengths, positions, cache, came, query, new_count)
    mine, value_up, out_proj = lax.optimization_barrier((mine, value_up, out_proj))
    parts = lax.all_to_all(mine, both, 0, 0, tiled=True)
    terms = project(parts, value_up, out_proj)
    terms = lax.all_to_all(terms, both, 0, 0, tiled=True)
    return total(terms, row_count, new_count)


def solution(mesh):
    batch, ctx = mesh.devices.shape
    mesh = Mesh(mesh.devices.reshape(batch, ctx // 2, 2), ("batch", "chip", "core"))
    ctx = ("chip", "core")
    in_specs = (
        P("batch", ctx, None),
        P("batch", None, ctx, None),
        P("batch"),
        P("batch"),
        P(ctx, None, None),
        P(ctx, None),
    )
    out_specs = P("batch", None, ctx)
    return jax.shard_map(body, mesh=mesh, in_specs=in_specs, out_specs=out_specs, check_vma=False)
```

```python
import functools
import math

import jax
import jax.numpy as jnp
import numpy as np
from jax import lax
from jax.experimental import pallas as pl
from jax.experimental.pallas import tpu as pltpu
from jax.sharding import Mesh
from jax.sharding import PartitionSpec as P

ROPE = 64
NOPE = 128
LANES = 128
STAT_LANES = 32
POWER = math.log2(math.e) / math.sqrt(NOPE + ROPE)
HIDDEN = -1e30
STRIP = 16
VMEM_LIMIT = 24 * 1024 * 1024
LEAST = -1e29


def angles(positions, new_count, repeats):
    half_rope = ROPE // 2
    shape = (new_count * repeats, ROPE)
    lane = lax.broadcasted_iota(jnp.int32, shape, 1)
    frequency = jnp.zeros(shape, jnp.float32)
    for i in range(half_rope):
        value = float(np.float32(50000.0 ** (-2.0 * i / ROPE)))
        frequency = jnp.where(lane % half_rope == i, value, frequency)
    token = lax.broadcasted_iota(jnp.int32, shape, 0) // repeats
    terms = []
    for position in positions:
        angle = (position + token).astype(jnp.float32) * frequency
        sine = jnp.sin(angle)
        terms.append((jnp.cos(angle), jnp.where(lane < half_rope, -sine, sine)))
    return terms


def split_stat(value, lane):
    high = value.astype(jnp.bfloat16).astype(jnp.float32)
    rest = value - high
    middle = rest.astype(jnp.bfloat16).astype(jnp.float32)
    low = rest - middle
    spot = lane % STAT_LANES
    return jnp.where(spot == 0, high, jnp.where(spot == 1, middle, low))


def join_stat(tile, row):
    at = row * STAT_LANES
    return tile[..., at : at + 1] + tile[..., at + 1 : at + 2] + tile[..., at + 2 : at + 3]


def spread_kernel(own_ref, came_ref, out_ref, flat_ref):
    rows, new_count, heads, full = own_ref.shape
    latent = full - ROPE
    depth = flat_ref.shape[1] // 2
    core = lax.axis_index("core")
    for side, ref in enumerate((own_ref, came_ref)):
        for row in range(rows):
            for token in range(new_count):
                at = (row * new_count + token) * heads
                flat_ref[side, at : at + heads, :] = ref[row, token].astype(jnp.float32)
        mine = flat_ref[side, pl.ds(pl.multiple_of(core * depth, depth), depth), :]
        pieces = [mine[:, g : g + LANES] for g in range(0, latent, LANES)]
        pieces.append(jnp.concatenate([mine[: depth // 2, latent:], mine[depth // 2 :, latent:]], axis=-1))
        block = jnp.concatenate(pieces, axis=0).astype(jnp.bfloat16)
        member = core if side == 0 else 1 - core
        for chip in range(out_ref.shape[0] // 2):
            out_ref[2 * chip + member] = block


def spread(own, came, peers):
    rows, new_count, heads, full = own.shape
    count = rows * new_count * heads
    vmem = pl.BlockSpec(memory_space=pltpu.VMEM)
    return pl.pallas_call(
        spread_kernel,
        out_shape=pltpu.VMEM((peers, count // 2 * full // LANES, LANES), jnp.bfloat16),
        in_specs=[vmem] * 2,
        out_specs=vmem,
        scratch_shapes=[pltpu.VMEM((2, count, full), jnp.float32)],
        compiler_params=pltpu.CompilerParams(vmem_limit_bytes=8 * 1024 * 1024),
        name="spread",
    )(own, came)


def attend_kernel(lengths_ref, positions_ref, own_ref, came_ref, query_ref, out_ref, keys_ref, arrived, *, new_count):
    peers = query_ref.shape[0]
    full = own_ref.shape[1]
    rows, wide, context = keys_ref.shape
    span = context // 2
    latent = full - ROPE
    column_groups = latent // LANES
    depth = query_ref.shape[1] * LANES // full
    group = depth // rows
    heads = group // new_count
    count = peers * group
    core = lax.axis_index("core")
    base = core * rows
    starts = [(lax.axis_index("chip") * 2 + place) * span for place in (core, 1 - core)]
    copies = []
    for row in range(rows):
        for side, ref in enumerate((own_ref, came_ref)):
            target = keys_ref.at[row, pl.ds(0, full), pl.ds(side * span, span)]
            copies.append(pltpu.make_async_copy(ref.at[base + row], target, arrived.at[row * 2 + side]))
    for copy in copies:
        copy.start()
    spare = wide - full
    column = lax.broadcasted_iota(jnp.int32, (peers, group, spare), 2)
    member = lax.broadcasted_iota(jnp.int32, (peers, group, spare), 1)
    flags = jnp.where(column == member // heads, 1.0, 0.0)
    place = lax.broadcasted_iota(jnp.int32, (spare, span), 1)
    token = lax.broadcasted_iota(jnp.int32, (spare, span), 0)
    turns = angles([positions_ref[base + row] for row in range(rows)], new_count, heads)
    queries = []
    for row in range(rows):
        for side in range(2):
            limit = lengths_ref[base + row] - new_count + 1 - starts[side]
            hidden = (token < new_count) & (place >= limit + token)
            keys_ref[row, full:, side * span : (side + 1) * span] = jnp.where(hidden, HIDDEN, 0.0).astype(jnp.bfloat16)
        tile, upper = row // 2 * 2 * group, slice(row % 2 * group, (row % 2 + 1) * group)
        pieces = []
        for g in range(column_groups):
            piece = query_ref[:, g * depth + tile : g * depth + tile + 2 * group, :].astype(jnp.float32)
            pieces.append(piece[:, upper])
        rope = query_ref[:, column_groups * depth :, :].astype(jnp.float32)
        rope = rope[:, upper, row // 2 * ROPE : (row // 2 + 1) * ROPE]
        swapped = jnp.concatenate([rope[:, :, ROPE // 2 :], rope[:, :, : ROPE // 2]], axis=-1)
        turned = rope * turns[row][0][None] + swapped * turns[row][1][None]
        query = jnp.concatenate([*pieces, turned, flags], axis=-1)
        queries.append(query.reshape(count, wide).astype(jnp.bfloat16))

    def score(row):
        copies[2 * row].wait()
        copies[2 * row + 1].wait()
        scores = jnp.dot(queries[row], keys_ref[row], preferred_element_type=jnp.float32)
        return scores

    sixteen = 2 * group
    at = column_groups * depth
    closed, packed = [], None
    lane = lax.broadcasted_iota(jnp.int32, (peers, group, LANES), 2)
    ahead = score(0)
    for row in range(rows):
        scores = ahead
        if row + 1 < rows:
            ahead = score(row + 1)
        tops, totals, strips = [], [], []
        for first in range(0, count, STRIP):
            strip = scores[first : first + STRIP]
            tops.append(jnp.maximum(jnp.max(strip, axis=-1, keepdims=True), LEAST))
            strip = jnp.exp2((strip - tops[-1]) * POWER)
            totals.append(jnp.sum(strip, axis=-1, keepdims=True))
            strips.append(strip.astype(jnp.bfloat16))
        top, total = jnp.concatenate(tops, axis=0), jnp.concatenate(totals, axis=0)
        out = lax.dot_general(
            jnp.concatenate(strips, axis=0),
            keys_ref[row, :latent],
            (((1,), (1,)), ((), ())),
            preferred_element_type=jnp.float32,
        )
        seen = total > 0.0
        safe = jnp.where(seen, total, 1.0)
        out = out * (1.0 / safe)
        stat = jnp.where(seen, top * POWER + jnp.log2(safe), HIDDEN)
        stat = jnp.broadcast_to(stat, (count, LANES)).reshape(peers, group, LANES)
        closed.append(out.reshape(peers, group, latent))
        stat = split_stat(stat, lane)
        packed = stat if packed is None else jnp.where(lane < row * STAT_LANES, packed, stat)
        if row % 2 == 1:
            both = jnp.concatenate(closed[-2:], axis=1).astype(jnp.bfloat16)
            for g in range(column_groups):
                start = g * depth + row // 2 * sixteen
                out_ref[:, start : start + sixteen, :] = both[:, :, g * LANES : (g + 1) * LANES]
    out_ref[:, at:, :] = packed.astype(jnp.bfloat16)


def attend(lengths, positions, own, came, query, new_count):
    peers = query.shape[0]
    rows = own.shape[0] // 2
    full, context = own.shape[1:]
    latent = full - ROPE
    depth = query.shape[1] * LANES // full
    group = depth // rows
    rows_out = latent // LANES * depth + group
    count = peers * group
    smem, vmem, anywhere = (pl.BlockSpec(memory_space=s) for s in (pltpu.SMEM, pltpu.VMEM, pl.ANY))
    own = pltpu.with_memory_space_constraint(own, pltpu.HBM)
    return pl.pallas_call(
        functools.partial(attend_kernel, new_count=new_count),
        out_shape=pltpu.VMEM((peers, rows_out, LANES), jnp.bfloat16),
        in_specs=[smem, smem, anywhere, anywhere, vmem],
        out_specs=vmem,
        scratch_shapes=[
            pltpu.VMEM((rows, -(-full // LANES) * LANES, 2 * context), jnp.bfloat16),
            pltpu.SemaphoreType.DMA((2 * rows,)),
        ],
        compiler_params=pltpu.CompilerParams(vmem_limit_bytes=VMEM_LIMIT),
        cost_estimate=pl.CostEstimate(
            flops=4 * count * context * (full + latent) * rows,
            bytes_accessed=2 * rows * context * full * 2 + 2 * peers * rows_out * LANES,
            transcendentals=2 * rows * count * context,
        ),
        name="attend",
    )(lengths, positions, own, came, query)


def project_kernel(parts_ref, own_up_ref, came_up_ref, own_proj_ref, came_proj_ref, out_ref, proj_ref, arrived):
    sixteen = 16
    peers, rows_out, _ = parts_ref.shape
    heads, wide, _ = own_up_ref.shape
    groups = wide // LANES
    at = rows_out - rows_out % sixteen
    depth = at // groups
    width = out_ref.shape[2]
    step = 4
    copies = []
    for piece, first in enumerate(range(0, peers, step)):
        columns = pl.ds(first * width, step * width)
        for side, ref in enumerate((own_proj_ref, came_proj_ref)):
            target = proj_ref.at[side, :, columns]
            copies.append(pltpu.make_async_copy(ref.at[:, columns], target, arrived.at[piece, side]))
    for copy in copies:
        copy.start()
    core = lax.axis_index("core")
    flats = []
    for side, up_ref in enumerate((own_up_ref, came_up_ref)):
        member = core if side == 0 else 1 - core
        blocks = []
        stat_tiles = [parts_ref[2 * k + member, at:, :].astype(jnp.float32) for k in range(peers // 2)]
        for pair in range(2):
            stats = [
                jnp.concatenate([join_stat(tile, 2 * pair), join_stat(tile, 2 * pair + 1)], axis=0)
                for tile in stat_tiles
            ]
            top = functools.reduce(jnp.maximum, stats)
            weights = [jnp.exp2(stat - top) for stat in stats]
            scale = 1.0 / functools.reduce(jnp.add, weights)
            sums = []
            for g in range(groups):
                start = g * depth + pair * sixteen
                terms = [
                    parts_ref[2 * k + member, start : start + sixteen, :].astype(jnp.float32) * weight
                    for k, weight in enumerate(weights)
                ]
                sums.append(functools.reduce(jnp.add, terms) * scale)
            blocks.append(jnp.concatenate(sums, axis=-1))
        latent = jnp.concatenate(blocks, axis=0).astype(jnp.bfloat16)
        count = latent.shape[0]
        out_row = lax.broadcasted_iota(jnp.int32, (count // heads, count), 0)
        in_row = lax.broadcasted_iota(jnp.int32, (count // heads, count), 1)
        values = []
        for head in range(heads):
            pick = jnp.where(in_row == out_row * heads + head, 1.0, 0.0).astype(jnp.bfloat16)
            chosen = jnp.dot(pick, latent, preferred_element_type=jnp.float32).astype(jnp.bfloat16)
            values.append(jnp.dot(chosen, up_ref[head], preferred_element_type=jnp.float32).astype(jnp.bfloat16))
        flats.append(jnp.concatenate(values, axis=-1))
    for piece, first in enumerate(range(0, peers, step)):
        columns = slice(first * width, (first + step) * width)
        terms = None
        for side in range(2):
            copies[2 * piece + side].wait()
            term = jnp.dot(flats[side], proj_ref[side, :, columns], preferred_element_type=jnp.float32)
            terms = term if terms is None else terms + term
        for k in range(step):
            out_ref[first + k] = terms[:, k * width : (k + 1) * width].astype(jnp.bfloat16)


def project(parts, own_up, came_up, own_proj, came_proj):
    peers, rows_out, _ = parts.shape
    heads, latent, _ = own_up.shape
    depth, columns = own_proj.shape
    tokens = rows_out // 16 * 16 // (latent // LANES) // heads
    vmem, anywhere = pl.BlockSpec(memory_space=pltpu.VMEM), pl.BlockSpec(memory_space=pl.ANY)
    return pl.pallas_call(
        project_kernel,
        out_shape=pltpu.VMEM((peers, tokens, columns // peers), jnp.bfloat16),
        in_specs=[vmem] * 3 + [anywhere] * 2,
        out_specs=vmem,
        scratch_shapes=[
            pltpu.VMEM((2, depth, columns), jnp.bfloat16),
            pltpu.SemaphoreType.DMA((peers // 4, 2)),
        ],
        compiler_params=pltpu.CompilerParams(vmem_limit_bytes=24 * 1024 * 1024),
        name="project",
    )(parts, own_up, came_up, own_proj, came_proj)


def total_kernel(terms_ref, out_ref):
    rows, new_count, _ = out_ref.shape
    half = rows // 2
    for core in range(2):
        terms = [terms_ref[k].astype(jnp.float32) for k in range(core, terms_ref.shape[0], 2)]
        result = functools.reduce(jnp.add, terms).astype(jnp.bfloat16)
        for row in range(half):
            out_ref[core * half + row] = result[row * new_count : (row + 1) * new_count]


def total(terms, rows, new_count):
    vmem = pl.BlockSpec(memory_space=pltpu.VMEM)
    return pl.pallas_call(
        total_kernel,
        out_shape=jax.ShapeDtypeStruct((rows, new_count, terms.shape[2]), jnp.bfloat16),
        in_specs=[vmem],
        out_specs=vmem,
        compiler_params=pltpu.CompilerParams(vmem_limit_bytes=8 * 1024 * 1024),
        name="total",
    )(terms)


def body(latent_cache, queries, lengths, positions, value_up, out_proj):
    row_count, new_count = queries.shape[:2]
    peers = lax.axis_size("chip") * 2
    swap = [(0, 1), (1, 0)]
    came_queries = lax.ppermute(queries, "core", swap)
    came_queries, latent_cache = lax.optimization_barrier((came_queries, latent_cache))
    cache = jnp.swapaxes(latent_cache, 1, 2)
    came = lax.ppermute(cache, "core", swap)
    query = lax.all_to_all(spread(queries, came_queries, peers), "chip", 0, 0, tiled=True)
    query, value_up, out_proj = lax.optimization_barrier((query, value_up, out_proj))
    came_up = lax.ppermute(value_up, "core", swap)
    came_proj = lax.ppermute(out_proj, "core", swap)
    mine = attend(lengths, positions, cache, came, query, new_count)
    mine, came_up, came_proj = lax.optimization_barrier((mine, came_up, came_proj))
    parts = lax.all_to_all(mine, "chip", 0, 0, tiled=True)
    terms = project(parts, value_up, came_up, out_proj, came_proj)
    terms = lax.all_to_all(terms, ("chip", "core"), 0, 0, tiled=True)
    return total(terms, row_count, new_count)


def solution(mesh):
    batch, ctx = mesh.devices.shape
    mesh = Mesh(mesh.devices.reshape(batch, ctx // 2, 2), ("batch", "chip", "core"))
    ctx = ("chip", "core")
    in_specs = (
        P("batch", ctx, None),
        P("batch", None, ctx, None),
        P("batch"),
        P("batch"),
        P(ctx, None, None),
        P(ctx, None),
    )
    out_specs = P("batch", None, ctx)
    return jax.shard_map(body, mesh=mesh, in_specs=in_specs, out_specs=out_specs, check_vma=False)
```

```python
import functools
import math

import jax
import jax.numpy as jnp
import numpy as np
from jax import lax
from jax.experimental import pallas as pl
from jax.experimental.pallas import tpu as pltpu
from jax.sharding import Mesh
from jax.sharding import PartitionSpec as P

ROPE = 64
NOPE = 128
LANES = 128
STAT_LANES = 32
POWER = math.log2(math.e) / math.sqrt(NOPE + ROPE)
HIDDEN = -1e30
STRIP = 16
VMEM_LIMIT = 24 * 1024 * 1024
LEAST = -1e29


def angles(positions, new_count, repeats):
    half_rope = ROPE // 2
    shape = (new_count * repeats, ROPE)
    lane = lax.broadcasted_iota(jnp.int32, shape, 1)
    frequency = jnp.zeros(shape, jnp.float32)
    for i in range(half_rope):
        value = float(np.float32(50000.0 ** (-2.0 * i / ROPE)))
        frequency = jnp.where(lane % half_rope == i, value, frequency)
    token = lax.broadcasted_iota(jnp.int32, shape, 0) // repeats
    terms = []
    for position in positions:
        angle = (position + token).astype(jnp.float32) * frequency
        sine = jnp.sin(angle)
        terms.append((jnp.cos(angle), jnp.where(lane < half_rope, -sine, sine)))
    return terms


def split_stat(value, lane):
    high = value.astype(jnp.bfloat16).astype(jnp.float32)
    rest = value - high
    middle = rest.astype(jnp.bfloat16).astype(jnp.float32)
    low = rest - middle
    spot = lane % STAT_LANES
    return jnp.where(spot == 0, high, jnp.where(spot == 1, middle, low))


def join_stat(tile, row):
    at = row * STAT_LANES
    return tile[..., at : at + 1] + tile[..., at + 1 : at + 2] + tile[..., at + 2 : at + 3]


def spread_kernel(query_ref, out_ref, flat_ref):
    rows, new_count, heads, full = query_ref.shape
    latent = full - ROPE
    for row in range(rows):
        for token in range(new_count):
            at = (row * new_count + token) * heads
            flat_ref[at : at + heads, :] = query_ref[row, token].astype(jnp.float32)
    flat = flat_ref[...]
    depth = flat.shape[0] // 2
    for half in range(2):
        mine = flat[half * depth : (half + 1) * depth]
        pieces = [mine[:, g : g + LANES] for g in range(0, latent, LANES)]
        pieces.append(jnp.concatenate([mine[: depth // 2, latent:], mine[depth // 2 :, latent:]], axis=-1))
        block = jnp.concatenate(pieces, axis=0).astype(jnp.bfloat16)
        for peer in range(half, out_ref.shape[0], 2):
            out_ref[peer] = block


def spread(queries, peers):
    rows, new_count, heads, full = queries.shape
    count = rows * new_count * heads
    vmem = pl.BlockSpec(memory_space=pltpu.VMEM)
    return pl.pallas_call(
        spread_kernel,
        out_shape=pltpu.VMEM((peers, count // 2 * full // LANES, LANES), jnp.bfloat16),
        in_specs=[vmem],
        out_specs=vmem,
        scratch_shapes=[pltpu.VMEM((count, full), jnp.float32)],
        compiler_params=pltpu.CompilerParams(vmem_limit_bytes=8 * 1024 * 1024),
        name="spread",
    )(queries)


def attend_kernel(lengths_ref, positions_ref, own_ref, came_ref, query_ref, out_ref, keys_ref, arrived, *, new_count):
    peers = query_ref.shape[0]
    full = own_ref.shape[1]
    rows, wide, context = keys_ref.shape
    span = context // 2
    latent = full - ROPE
    column_groups = latent // LANES
    depth = query_ref.shape[1] * LANES // full
    group = depth // rows
    heads = group // new_count
    count = peers * group
    core = lax.axis_index("core")
    base = core * rows
    starts = [(lax.axis_index("chip") * 2 + place) * span for place in (core, 1 - core)]
    copies = []
    for row in range(rows):
        for side, ref in enumerate((own_ref, came_ref)):
            target = keys_ref.at[row, pl.ds(0, full), pl.ds(side * span, span)]
            copies.append(pltpu.make_async_copy(ref.at[base + row], target, arrived.at[row * 2 + side]))
    for copy in copies:
        copy.start()
    spare = wide - full
    column = lax.broadcasted_iota(jnp.int32, (peers, group, spare), 2)
    member = lax.broadcasted_iota(jnp.int32, (peers, group, spare), 1)
    flags = jnp.where(column == member // heads, 1.0, 0.0)
    place = lax.broadcasted_iota(jnp.int32, (spare, span), 1)
    token = lax.broadcasted_iota(jnp.int32, (spare, span), 0)
    turns = angles([positions_ref[base + row] for row in range(rows)], new_count, heads)
    queries = []
    for row in range(rows):
        for side in range(2):
            limit = lengths_ref[base + row] - new_count + 1 - starts[side]
            hidden = (token < new_count) & (place >= limit + token)
            keys_ref[row, full:, side * span : (side + 1) * span] = jnp.where(hidden, HIDDEN, 0.0).astype(jnp.bfloat16)
        tile, upper = row // 2 * 2 * group, slice(row % 2 * group, (row % 2 + 1) * group)
        pieces = []
        for g in range(column_groups):
            piece = query_ref[:, g * depth + tile : g * depth + tile + 2 * group, :].astype(jnp.float32)
            pieces.append(piece[:, upper])
        rope = query_ref[:, column_groups * depth :, :].astype(jnp.float32)
        rope = rope[:, upper, row // 2 * ROPE : (row // 2 + 1) * ROPE]
        swapped = jnp.concatenate([rope[:, :, ROPE // 2 :], rope[:, :, : ROPE // 2]], axis=-1)
        turned = rope * turns[row][0][None] + swapped * turns[row][1][None]
        query = jnp.concatenate([*pieces, turned, flags], axis=-1)
        queries.append(query.reshape(count, wide).astype(jnp.bfloat16))

    def score(row):
        copies[2 * row].wait()
        copies[2 * row + 1].wait()
        scores = jnp.dot(queries[row], keys_ref[row], preferred_element_type=jnp.float32)
        return scores

    sixteen = 2 * group
    at = column_groups * depth
    closed, packed = [], None
    lane = lax.broadcasted_iota(jnp.int32, (peers, group, LANES), 2)
    ahead = score(0)
    for row in range(rows):
        scores = ahead
        if row + 1 < rows:
            ahead = score(row + 1)
        tops, totals, strips = [], [], []
        for first in range(0, count, STRIP):
            strip = scores[first : first + STRIP]
            tops.append(jnp.maximum(jnp.max(strip, axis=-1, keepdims=True), LEAST))
            strip = jnp.exp2((strip - tops[-1]) * POWER)
            totals.append(jnp.sum(strip, axis=-1, keepdims=True))
            strips.append(strip.astype(jnp.bfloat16))
        top, total = jnp.concatenate(tops, axis=0), jnp.concatenate(totals, axis=0)
        out = lax.dot_general(
            jnp.concatenate(strips, axis=0),
            keys_ref[row, :latent],
            (((1,), (1,)), ((), ())),
            preferred_element_type=jnp.float32,
        )
        seen = total > 0.0
        safe = jnp.where(seen, total, 1.0)
        out = out * (1.0 / safe)
        stat = jnp.where(seen, top * POWER + jnp.log2(safe), HIDDEN)
        stat = jnp.broadcast_to(stat, (count, LANES)).reshape(peers, group, LANES)
        closed.append(out.reshape(peers, group, latent))
        stat = split_stat(stat, lane)
        packed = stat if packed is None else jnp.where(lane < row * STAT_LANES, packed, stat)
        if row % 2 == 1:
            both = jnp.concatenate(closed[-2:], axis=1).astype(jnp.bfloat16)
            for g in range(column_groups):
                start = g * depth + row // 2 * sixteen
                out_ref[:, start : start + sixteen, :] = both[:, :, g * LANES : (g + 1) * LANES]
    out_ref[:, at:, :] = packed.astype(jnp.bfloat16)


def attend(lengths, positions, own, came, query, new_count):
    peers = query.shape[0]
    rows = own.shape[0] // 2
    full, context = own.shape[1:]
    latent = full - ROPE
    depth = query.shape[1] * LANES // full
    group = depth // rows
    rows_out = latent // LANES * depth + group
    count = peers * group
    smem, vmem, anywhere = (pl.BlockSpec(memory_space=s) for s in (pltpu.SMEM, pltpu.VMEM, pl.ANY))
    own = pltpu.with_memory_space_constraint(own, pltpu.HBM)
    return pl.pallas_call(
        functools.partial(attend_kernel, new_count=new_count),
        out_shape=pltpu.VMEM((peers, rows_out, LANES), jnp.bfloat16),
        in_specs=[smem, smem, anywhere, anywhere, vmem],
        out_specs=vmem,
        scratch_shapes=[
            pltpu.VMEM((rows, -(-full // LANES) * LANES, 2 * context), jnp.bfloat16),
            pltpu.SemaphoreType.DMA((2 * rows,)),
        ],
        compiler_params=pltpu.CompilerParams(vmem_limit_bytes=VMEM_LIMIT),
        cost_estimate=pl.CostEstimate(
            flops=4 * count * context * (full + latent) * rows,
            bytes_accessed=2 * rows * context * full * 2 + 2 * peers * rows_out * LANES,
            transcendentals=2 * rows * count * context,
        ),
        name="attend",
    )(lengths, positions, own, came, query)


def project_kernel(parts_ref, own_up_ref, came_up_ref, own_proj_ref, came_proj_ref, out_ref):
    sixteen = 16
    peers, rows_out, _ = parts_ref.shape
    heads, wide, _ = own_up_ref.shape
    groups = wide // LANES
    at = rows_out - rows_out % sixteen
    depth = at // groups
    width = out_ref.shape[2]
    step = 4
    core = lax.axis_index("core")
    flats = []
    for side, up_ref in enumerate((own_up_ref, came_up_ref)):
        member = core if side == 0 else 1 - core
        blocks = []
        stat_tiles = [parts_ref[2 * k + member, at:, :].astype(jnp.float32) for k in range(peers // 2)]
        for pair in range(2):
            stats = [
                jnp.concatenate([join_stat(tile, 2 * pair), join_stat(tile, 2 * pair + 1)], axis=0)
                for tile in stat_tiles
            ]
            top = functools.reduce(jnp.maximum, stats)
            weights = [jnp.exp2(stat - top) for stat in stats]
            scale = 1.0 / functools.reduce(jnp.add, weights)
            sums = []
            for g in range(groups):
                start = g * depth + pair * sixteen
                terms = [
                    parts_ref[2 * k + member, start : start + sixteen, :].astype(jnp.float32) * weight
                    for k, weight in enumerate(weights)
                ]
                sums.append(functools.reduce(jnp.add, terms) * scale)
            blocks.append(jnp.concatenate(sums, axis=-1))
        latent = jnp.concatenate(blocks, axis=0).astype(jnp.bfloat16)
        count = latent.shape[0]
        out_row = lax.broadcasted_iota(jnp.int32, (count // heads, count), 0)
        in_row = lax.broadcasted_iota(jnp.int32, (count // heads, count), 1)
        values = []
        for head in range(heads):
            pick = jnp.where(in_row == out_row * heads + head, 1.0, 0.0).astype(jnp.bfloat16)
            chosen = jnp.dot(pick, latent, preferred_element_type=jnp.float32).astype(jnp.bfloat16)
            values.append(jnp.dot(chosen, up_ref[head], preferred_element_type=jnp.float32).astype(jnp.bfloat16))
        flats.append(jnp.concatenate(values, axis=-1))
    for first in range(0, peers, step):
        columns = slice(first * width, (first + step) * width)
        terms = jnp.dot(flats[0], own_proj_ref[:, columns], preferred_element_type=jnp.float32)
        terms += jnp.dot(flats[1], came_proj_ref[:, columns], preferred_element_type=jnp.float32)
        for k in range(step):
            out_ref[first + k] = terms[:, k * width : (k + 1) * width].astype(jnp.bfloat16)


def project(parts, own_up, came_up, own_proj, came_proj):
    peers, rows_out, _ = parts.shape
    heads, latent, _ = own_up.shape
    columns = own_proj.shape[1]
    tokens = rows_out // 16 * 16 // (latent // LANES) // heads
    vmem = pl.BlockSpec(memory_space=pltpu.VMEM)
    return pl.pallas_call(
        project_kernel,
        out_shape=pltpu.VMEM((peers, tokens, columns // peers), jnp.bfloat16),
        in_specs=[vmem] * 5,
        out_specs=vmem,
        compiler_params=pltpu.CompilerParams(vmem_limit_bytes=16 * 1024 * 1024),
        name="project",
    )(parts, own_up, came_up, own_proj, came_proj)


def total_kernel(terms_ref, out_ref):
    rows, new_count, _ = out_ref.shape
    half = rows // 2
    for core in range(2):
        terms = [terms_ref[k].astype(jnp.float32) for k in range(core, terms_ref.shape[0], 2)]
        result = functools.reduce(jnp.add, terms).astype(jnp.bfloat16)
        for row in range(half):
            out_ref[core * half + row] = result[row * new_count : (row + 1) * new_count]


def total(terms, rows, new_count):
    vmem = pl.BlockSpec(memory_space=pltpu.VMEM)
    return pl.pallas_call(
        total_kernel,
        out_shape=jax.ShapeDtypeStruct((rows, new_count, terms.shape[2]), jnp.bfloat16),
        in_specs=[vmem],
        out_specs=vmem,
        compiler_params=pltpu.CompilerParams(vmem_limit_bytes=8 * 1024 * 1024),
        name="total",
    )(terms)


def body(latent_cache, queries, lengths, positions, value_up, out_proj):
    row_count, new_count = queries.shape[:2]
    peers = lax.axis_size("chip") * 2
    swap = [(0, 1), (1, 0)]
    cache = jnp.swapaxes(latent_cache, 1, 2)
    came = lax.ppermute(cache, "core", swap)
    query = lax.all_to_all(spread(queries, peers), ("chip", "core"), 0, 0, tiled=True)
    query, value_up, out_proj = lax.optimization_barrier((query, value_up, out_proj))
    came_up = lax.ppermute(value_up, "core", swap)
    came_proj = lax.ppermute(out_proj, "core", swap)
    mine = attend(lengths, positions, cache, came, query, new_count)
    mine, came_up, came_proj = lax.optimization_barrier((mine, came_up, came_proj))
    parts = lax.all_to_all(mine, "chip", 0, 0, tiled=True)
    terms = project(parts, value_up, came_up, out_proj, came_proj)
    terms = lax.all_to_all(terms, ("chip", "core"), 0, 0, tiled=True)
    return total(terms, row_count, new_count)


def solution(mesh):
    batch, ctx = mesh.devices.shape
    mesh = Mesh(mesh.devices.reshape(batch, ctx // 2, 2), ("batch", "chip", "core"))
    ctx = ("chip", "core")
    in_specs = (
        P("batch", ctx, None),
        P("batch", None, ctx, None),
        P("batch"),
        P("batch"),
        P(ctx, None, None),
        P(ctx, None),
    )
    out_specs = P("batch", None, ctx)
    return jax.shard_map(body, mesh=mesh, in_specs=in_specs, out_specs=out_specs, check_vma=False)
```

```python
import functools
import math

import jax
import jax.numpy as jnp
import numpy as np
from jax import lax
from jax.experimental import pallas as pl
from jax.experimental.pallas import tpu as pltpu
from jax.sharding import Mesh
from jax.sharding import PartitionSpec as P

ROPE = 64
NOPE = 128
LANES = 128
STAT_LANES = 32
POWER = math.log2(math.e) / math.sqrt(NOPE + ROPE)
HIDDEN = -1e30
STRIP = 16
VMEM_LIMIT = 24 * 1024 * 1024
LEAST = -1e29


def angles(positions, new_count, repeats):
    half_rope = ROPE // 2
    shape = (new_count * repeats, ROPE)
    lane = lax.broadcasted_iota(jnp.int32, shape, 1)
    frequency = jnp.zeros(shape, jnp.float32)
    for i in range(half_rope):
        value = float(np.float32(50000.0 ** (-2.0 * i / ROPE)))
        frequency = jnp.where(lane % half_rope == i, value, frequency)
    token = lax.broadcasted_iota(jnp.int32, shape, 0) // repeats
    terms = []
    for position in positions:
        angle = (position + token).astype(jnp.float32) * frequency
        sine = jnp.sin(angle)
        terms.append((jnp.cos(angle), jnp.where(lane < half_rope, -sine, sine)))
    return terms


def split_stat(value, lane):
    high = value.astype(jnp.bfloat16).astype(jnp.float32)
    rest = value - high
    middle = rest.astype(jnp.bfloat16).astype(jnp.float32)
    low = rest - middle
    spot = lane % STAT_LANES
    return jnp.where(spot == 0, high, jnp.where(spot == 1, middle, low))


def join_stat(tile, row):
    at = row * STAT_LANES
    return tile[..., at : at + 1] + tile[..., at + 1 : at + 2] + tile[..., at + 2 : at + 3]


def spread_kernel(query_ref, out_ref, flat_ref):
    rows, new_count, heads, full = query_ref.shape
    latent = full - ROPE
    for row in range(rows):
        for token in range(new_count):
            at = (row * new_count + token) * heads
            flat_ref[at : at + heads, :] = query_ref[row, token].astype(jnp.float32)
    flat = flat_ref[...]
    depth = flat.shape[0] // 2
    for half in range(2):
        mine = flat[half * depth : (half + 1) * depth]
        pieces = [mine[:, g : g + LANES] for g in range(0, latent, LANES)]
        pieces.append(jnp.concatenate([mine[: depth // 2, latent:], mine[depth // 2 :, latent:]], axis=-1))
        block = jnp.concatenate(pieces, axis=0).astype(jnp.bfloat16)
        for peer in range(half, out_ref.shape[0], 2):
            out_ref[peer] = block


def spread(queries, peers):
    rows, new_count, heads, full = queries.shape
    count = rows * new_count * heads
    vmem = pl.BlockSpec(memory_space=pltpu.VMEM)
    return pl.pallas_call(
        spread_kernel,
        out_shape=pltpu.VMEM((peers, count // 2 * full // LANES, LANES), jnp.bfloat16),
        in_specs=[vmem],
        out_specs=vmem,
        scratch_shapes=[pltpu.VMEM((count, full), jnp.float32)],
        compiler_params=pltpu.CompilerParams(vmem_limit_bytes=8 * 1024 * 1024),
        name="spread",
    )(queries)


def attend_kernel(
    far_lengths_ref, far_positions_ref, own_ref, came_ref, query_ref, out_ref, keys_ref, lengths_ref, positions_ref, arrived, told, *, new_count
):
    peers = query_ref.shape[0]
    full = own_ref.shape[1]
    rows, wide, context = keys_ref.shape
    span = context // 2
    latent = full - ROPE
    column_groups = latent // LANES
    depth = query_ref.shape[1] * LANES // full
    group = depth // rows
    heads = group // new_count
    count = peers * group
    core = lax.axis_index("core")
    base = core * rows
    starts = [(lax.axis_index("chip") * 2 + place) * span for place in (core, 1 - core)]
    scalars = [
        pltpu.make_async_copy(far_lengths_ref, lengths_ref, told.at[0]),
        pltpu.make_async_copy(far_positions_ref, positions_ref, told.at[1]),
    ]
    for copy in scalars:
        copy.start()
    copies = []
    for row in range(rows):
        for side, ref in enumerate((own_ref, came_ref)):
            target = keys_ref.at[row, pl.ds(0, full), pl.ds(side * span, span)]
            copies.append(pltpu.make_async_copy(ref.at[base + row], target, arrived.at[row * 2 + side]))
    for copy in copies:
        copy.start()
    spare = wide - full
    column = lax.broadcasted_iota(jnp.int32, (peers, group, spare), 2)
    member = lax.broadcasted_iota(jnp.int32, (peers, group, spare), 1)
    flags = jnp.where(column == member // heads, 1.0, 0.0)
    place = lax.broadcasted_iota(jnp.int32, (spare, span), 1)
    token = lax.broadcasted_iota(jnp.int32, (spare, span), 0)
    latents, ropes = [], []
    for row in range(rows):
        tile, upper = row // 2 * 2 * group, slice(row % 2 * group, (row % 2 + 1) * group)
        for g in range(column_groups):
            piece = query_ref[:, g * depth + tile : g * depth + tile + 2 * group, :].astype(jnp.float32)
            latents.append(piece[:, upper])
        rope = query_ref[:, column_groups * depth :, :].astype(jnp.float32)
        ropes.append(rope[:, upper, row // 2 * ROPE : (row // 2 + 1) * ROPE])
    for copy in scalars:
        copy.wait()
    turns = angles([positions_ref[base + row] for row in range(rows)], new_count, heads)
    queries = []
    for row in range(rows):
        for side in range(2):
            limit = lengths_ref[base + row] - new_count + 1 - starts[side]
            hidden = (token < new_count) & (place >= limit + token)
            keys_ref[row, full:, side * span : (side + 1) * span] = jnp.where(hidden, HIDDEN, 0.0).astype(jnp.bfloat16)
        rope = ropes[row]
        swapped = jnp.concatenate([rope[:, :, ROPE // 2 :], rope[:, :, : ROPE // 2]], axis=-1)
        turned = rope * turns[row][0][None] + swapped * turns[row][1][None]
        pieces = latents[row * column_groups : (row + 1) * column_groups]
        query = jnp.concatenate([*pieces, turned, flags], axis=-1)
        queries.append(query.reshape(count, wide).astype(jnp.bfloat16))

    def score(row):
        copies[2 * row].wait()
        copies[2 * row + 1].wait()
        scores = jnp.dot(queries[row], keys_ref[row], preferred_element_type=jnp.float32)
        return scores

    sixteen = 2 * group
    at = column_groups * depth
    closed, packed = [], None
    lane = lax.broadcasted_iota(jnp.int32, (peers, group, LANES), 2)
    ahead = score(0)
    for row in range(rows):
        scores = ahead
        if row + 1 < rows:
            ahead = score(row + 1)
        tops, totals, strips = [], [], []
        for first in range(0, count, STRIP):
            strip = scores[first : first + STRIP]
            tops.append(jnp.maximum(jnp.max(strip, axis=-1, keepdims=True), LEAST))
            strip = jnp.exp2((strip - tops[-1]) * POWER)
            totals.append(jnp.sum(strip, axis=-1, keepdims=True))
            strips.append(strip.astype(jnp.bfloat16))
        top, total = jnp.concatenate(tops, axis=0), jnp.concatenate(totals, axis=0)
        out = lax.dot_general(
            jnp.concatenate(strips, axis=0),
            keys_ref[row, :latent],
            (((1,), (1,)), ((), ())),
            preferred_element_type=jnp.float32,
        )
        seen = total > 0.0
        safe = jnp.where(seen, total, 1.0)
        out = out * (1.0 / safe)
        stat = jnp.where(seen, top * POWER + jnp.log2(safe), HIDDEN)
        stat = jnp.broadcast_to(stat, (count, LANES)).reshape(peers, group, LANES)
        closed.append(out.reshape(peers, group, latent))
        stat = split_stat(stat, lane)
        packed = stat if packed is None else jnp.where(lane < row * STAT_LANES, packed, stat)
        if row % 2 == 1:
            both = jnp.concatenate(closed[-2:], axis=1).astype(jnp.bfloat16)
            for g in range(column_groups):
                start = g * depth + row // 2 * sixteen
                out_ref[:, start : start + sixteen, :] = both[:, :, g * LANES : (g + 1) * LANES]
    out_ref[:, at:, :] = packed.astype(jnp.bfloat16)


def attend(lengths, positions, own, came, query, new_count):
    peers = query.shape[0]
    rows = own.shape[0] // 2
    full, context = own.shape[1:]
    latent = full - ROPE
    depth = query.shape[1] * LANES // full
    group = depth // rows
    rows_out = latent // LANES * depth + group
    count = peers * group
    vmem, anywhere = (pl.BlockSpec(memory_space=space) for space in (pltpu.VMEM, pl.ANY))
    own, lengths, positions = (
        pltpu.with_memory_space_constraint(array, pltpu.HBM) for array in (own, lengths, positions)
    )
    return pl.pallas_call(
        functools.partial(attend_kernel, new_count=new_count),
        out_shape=pltpu.VMEM((peers, rows_out, LANES), jnp.bfloat16),
        in_specs=[anywhere] * 4 + [vmem],
        out_specs=vmem,
        scratch_shapes=[
            pltpu.VMEM((rows, -(-full // LANES) * LANES, 2 * context), jnp.bfloat16),
            pltpu.SMEM(lengths.shape, jnp.int32),
            pltpu.SMEM(positions.shape, jnp.int32),
            pltpu.SemaphoreType.DMA((2 * rows,)),
            pltpu.SemaphoreType.DMA((2,)),
        ],
        compiler_params=pltpu.CompilerParams(vmem_limit_bytes=VMEM_LIMIT),
        cost_estimate=pl.CostEstimate(
            flops=4 * count * context * (full + latent) * rows,
            bytes_accessed=2 * rows * context * full * 2 + 2 * peers * rows_out * LANES,
            transcendentals=2 * rows * count * context,
        ),
        name="attend",
    )(lengths, positions, own, came, query)


def project_kernel(parts_ref, own_up_ref, came_up_ref, own_proj_ref, came_proj_ref, out_ref):
    sixteen = 16
    peers, rows_out, _ = parts_ref.shape
    heads, wide, _ = own_up_ref.shape
    groups = wide // LANES
    at = rows_out - rows_out % sixteen
    depth = at // groups
    width = out_ref.shape[2]
    step = 4
    core = lax.axis_index("core")
    flats = []
    for side, up_ref in enumerate((own_up_ref, came_up_ref)):
        member = core if side == 0 else 1 - core
        blocks = []
        stat_tiles = [parts_ref[2 * k + member, at:, :].astype(jnp.float32) for k in range(peers // 2)]
        for pair in range(2):
            stats = [
                jnp.concatenate([join_stat(tile, 2 * pair), join_stat(tile, 2 * pair + 1)], axis=0)
                for tile in stat_tiles
            ]
            top = functools.reduce(jnp.maximum, stats)
            weights = [jnp.exp2(stat - top) for stat in stats]
            scale = 1.0 / functools.reduce(jnp.add, weights)
            sums = []
            for g in range(groups):
                start = g * depth + pair * sixteen
                terms = [
                    parts_ref[2 * k + member, start : start + sixteen, :].astype(jnp.float32) * weight
                    for k, weight in enumerate(weights)
                ]
                sums.append(functools.reduce(jnp.add, terms) * scale)
            blocks.append(jnp.concatenate(sums, axis=-1))
        latent = jnp.concatenate(blocks, axis=0).astype(jnp.bfloat16)
        count = latent.shape[0]
        out_row = lax.broadcasted_iota(jnp.int32, (count // heads, count), 0)
        in_row = lax.broadcasted_iota(jnp.int32, (count // heads, count), 1)
        values = []
        for head in range(heads):
            pick = jnp.where(in_row == out_row * heads + head, 1.0, 0.0).astype(jnp.bfloat16)
            chosen = jnp.dot(pick, latent, preferred_element_type=jnp.float32).astype(jnp.bfloat16)
            values.append(jnp.dot(chosen, up_ref[head], preferred_element_type=jnp.float32).astype(jnp.bfloat16))
        flats.append(jnp.concatenate(values, axis=-1))
    for first in range(0, peers, step):
        columns = slice(first * width, (first + step) * width)
        terms = jnp.dot(flats[0], own_proj_ref[:, columns], preferred_element_type=jnp.float32)
        terms += jnp.dot(flats[1], came_proj_ref[:, columns], preferred_element_type=jnp.float32)
        for k in range(step):
            out_ref[first + k] = terms[:, k * width : (k + 1) * width].astype(jnp.bfloat16)


def project(parts, own_up, came_up, own_proj, came_proj):
    peers, rows_out, _ = parts.shape
    heads, latent, _ = own_up.shape
    columns = own_proj.shape[1]
    tokens = rows_out // 16 * 16 // (latent // LANES) // heads
    vmem = pl.BlockSpec(memory_space=pltpu.VMEM)
    return pl.pallas_call(
        project_kernel,
        out_shape=pltpu.VMEM((peers, tokens, columns // peers), jnp.bfloat16),
        in_specs=[vmem] * 5,
        out_specs=vmem,
        compiler_params=pltpu.CompilerParams(vmem_limit_bytes=16 * 1024 * 1024),
        name="project",
    )(parts, own_up, came_up, own_proj, came_proj)


def total_kernel(terms_ref, out_ref):
    rows, new_count, _ = out_ref.shape
    half = rows // 2
    for core in range(2):
        terms = [terms_ref[k].astype(jnp.float32) for k in range(core, terms_ref.shape[0], 2)]
        result = functools.reduce(jnp.add, terms).astype(jnp.bfloat16)
        for row in range(half):
            out_ref[core * half + row] = result[row * new_count : (row + 1) * new_count]


def total(terms, rows, new_count):
    vmem = pl.BlockSpec(memory_space=pltpu.VMEM)
    return pl.pallas_call(
        total_kernel,
        out_shape=jax.ShapeDtypeStruct((rows, new_count, terms.shape[2]), jnp.bfloat16),
        in_specs=[vmem],
        out_specs=vmem,
        compiler_params=pltpu.CompilerParams(vmem_limit_bytes=8 * 1024 * 1024),
        name="total",
    )(terms)


def body(latent_cache, queries, lengths, positions, value_up, out_proj):
    row_count, new_count = queries.shape[:2]
    peers = lax.axis_size("chip") * 2
    swap = [(0, 1), (1, 0)]
    cache = jnp.swapaxes(latent_cache, 1, 2)
    came = lax.ppermute(cache, "core", swap)
    query = lax.all_to_all(spread(queries, peers), ("chip", "core"), 0, 0, tiled=True)
    query, value_up, out_proj = lax.optimization_barrier((query, value_up, out_proj))
    came_up = lax.ppermute(value_up, "core", swap)
    came_proj = lax.ppermute(out_proj, "core", swap)
    mine = attend(lengths, positions, cache, came, query, new_count)
    mine, came_up, came_proj = lax.optimization_barrier((mine, came_up, came_proj))
    parts = lax.all_to_all(mine, "chip", 0, 0, tiled=True)
    terms = project(parts, value_up, came_up, out_proj, came_proj)
    terms = lax.all_to_all(terms, ("chip", "core"), 0, 0, tiled=True)
    return total(terms, row_count, new_count)


def solution(mesh):
    batch, ctx = mesh.devices.shape
    mesh = Mesh(mesh.devices.reshape(batch, ctx // 2, 2), ("batch", "chip", "core"))
    ctx = ("chip", "core")
    in_specs = (
        P("batch", ctx, None),
        P("batch", None, ctx, None),
        P("batch"),
        P("batch"),
        P(ctx, None, None),
        P(ctx, None),
    )
    out_specs = P("batch", None, ctx)
    return jax.shard_map(body, mesh=mesh, in_specs=in_specs, out_specs=out_specs, check_vma=False)
```

```python
import functools
import math

import jax
import jax.numpy as jnp
import numpy as np
from jax import lax
from jax.experimental import pallas as pl
from jax.experimental.pallas import tpu as pltpu
from jax.sharding import Mesh
from jax.sharding import PartitionSpec as P

ROPE = 64
NOPE = 128
LANES = 128
STAT_LANES = 32
POWER = math.log2(math.e) / math.sqrt(NOPE + ROPE)
HIDDEN = -1e30
STRIP = 16
VMEM_LIMIT = 24 * 1024 * 1024
LEAST = -1e29


def angles(positions, new_count, repeats):
    half_rope = ROPE // 2
    shape = (new_count * repeats, ROPE)
    lane = lax.broadcasted_iota(jnp.int32, shape, 1)
    frequency = jnp.zeros(shape, jnp.float32)
    for i in range(half_rope):
        value = float(np.float32(50000.0 ** (-2.0 * i / ROPE)))
        frequency = jnp.where(lane % half_rope == i, value, frequency)
    token = lax.broadcasted_iota(jnp.int32, shape, 0) // repeats
    terms = []
    for position in positions:
        angle = (position + token).astype(jnp.float32) * frequency
        sine = jnp.sin(angle)
        terms.append((jnp.cos(angle), jnp.where(lane < half_rope, -sine, sine)))
    return terms


def split_stat(value, lane):
    high = value.astype(jnp.bfloat16).astype(jnp.float32)
    rest = value - high
    middle = rest.astype(jnp.bfloat16).astype(jnp.float32)
    low = rest - middle
    spot = lane % STAT_LANES
    return jnp.where(spot == 0, high, jnp.where(spot == 1, middle, low))


def join_stat(tile, row):
    at = row * STAT_LANES
    return tile[..., at : at + 1] + tile[..., at + 1 : at + 2] + tile[..., at + 2 : at + 3]


def spread_kernel(query_ref, out_ref, flat_ref):
    rows, new_count, heads, full = query_ref.shape
    latent = full - ROPE
    for row in range(rows):
        for token in range(new_count):
            at = (row * new_count + token) * heads
            flat_ref[at : at + heads, :] = query_ref[row, token].astype(jnp.float32)
    flat = flat_ref[...]
    depth = flat.shape[0] // 2
    for half in range(2):
        mine = flat[half * depth : (half + 1) * depth]
        pieces = [mine[:, g : g + LANES] for g in range(0, latent, LANES)]
        pieces.append(jnp.concatenate([mine[: depth // 2, latent:], mine[depth // 2 :, latent:]], axis=-1))
        block = jnp.concatenate(pieces, axis=0).astype(jnp.bfloat16)
        for peer in range(half, out_ref.shape[0], 2):
            out_ref[peer] = block


def spread(queries, peers):
    rows, new_count, heads, full = queries.shape
    count = rows * new_count * heads
    vmem = pl.BlockSpec(memory_space=pltpu.VMEM)
    return pl.pallas_call(
        spread_kernel,
        out_shape=pltpu.VMEM((peers, count // 2 * full // LANES, LANES), jnp.bfloat16),
        in_specs=[vmem],
        out_specs=vmem,
        scratch_shapes=[pltpu.VMEM((count, full), jnp.float32)],
        compiler_params=pltpu.CompilerParams(vmem_limit_bytes=8 * 1024 * 1024),
        name="spread",
    )(queries)


def attend_kernel(
    far_lengths_ref, far_positions_ref, own_ref, came_ref, query_ref, out_ref, keys_ref, lengths_ref, positions_ref, arrived, told, *, new_count
):
    peers = query_ref.shape[0]
    full = own_ref.shape[1]
    rows, wide, context = keys_ref.shape
    span = context // 2
    latent = full - ROPE
    column_groups = latent // LANES
    depth = query_ref.shape[1] * LANES // full
    group = depth // rows
    heads = group // new_count
    count = peers * group
    core = lax.axis_index("core")
    base = core * rows
    starts = [(lax.axis_index("chip") * 2 + place) * span for place in (core, 1 - core)]
    scalars = [
        pltpu.make_async_copy(far_lengths_ref, lengths_ref, told.at[0]),
        pltpu.make_async_copy(far_positions_ref, positions_ref, told.at[1]),
    ]
    for copy in scalars:
        copy.start()
    copies = []
    for row in range(rows):
        for side, ref in enumerate((own_ref, came_ref)):
            target = keys_ref.at[row, pl.ds(0, full), pl.ds(side * span, span)]
            copies.append(pltpu.make_async_copy(ref.at[base + row], target, arrived.at[row * 2 + side]))
    for copy in copies:
        copy.start()
    spare = wide - full
    column = lax.broadcasted_iota(jnp.int32, (peers, group, spare), 2)
    member = lax.broadcasted_iota(jnp.int32, (peers, group, spare), 1)
    flags = jnp.where(column == member // heads, 1.0, 0.0)
    place = lax.broadcasted_iota(jnp.int32, (spare, span), 1)
    token = lax.broadcasted_iota(jnp.int32, (spare, span), 0)
    latents, ropes = [], []
    for row in range(rows):
        tile, upper = row // 2 * 2 * group, slice(row % 2 * group, (row % 2 + 1) * group)
        for g in range(column_groups):
            piece = query_ref[:, g * depth + tile : g * depth + tile + 2 * group, :].astype(jnp.float32)
            latents.append(piece[:, upper])
        rope = query_ref[:, column_groups * depth :, :].astype(jnp.float32)
        ropes.append(rope[:, upper, row // 2 * ROPE : (row // 2 + 1) * ROPE])
    for copy in scalars:
        copy.wait()
    turns = angles([positions_ref[base + row] for row in range(rows)], new_count, heads)
    queries = []
    for row in range(rows):
        for side in range(2):
            limit = lengths_ref[base + row] - new_count + 1 - starts[side]
            hidden = (token < new_count) & (place >= limit + token)
            keys_ref[row, full:, side * span : (side + 1) * span] = jnp.where(hidden, HIDDEN, 0.0).astype(jnp.bfloat16)
        rope = ropes[row]
        swapped = jnp.concatenate([rope[:, :, ROPE // 2 :], rope[:, :, : ROPE // 2]], axis=-1)
        turned = rope * turns[row][0][None] + swapped * turns[row][1][None]
        pieces = latents[row * column_groups : (row + 1) * column_groups]
        query = jnp.concatenate([*pieces, turned, flags], axis=-1)
        queries.append(query.reshape(count, wide).astype(jnp.bfloat16))

    def score(row):
        copies[2 * row].wait()
        copies[2 * row + 1].wait()
        scores = jnp.dot(queries[row], keys_ref[row], preferred_element_type=jnp.float32)
        return scores

    sixteen = 2 * group
    at = column_groups * depth
    closed, packed = [], None
    lane = lax.broadcasted_iota(jnp.int32, (peers, group, LANES), 2)
    ahead = score(0)
    for row in range(rows):
        scores = ahead
        if row + 1 < rows:
            ahead = score(row + 1)
        tops, totals, strips = [], [], []
        for first in range(0, count, STRIP):
            strip = scores[first : first + STRIP]
            tops.append(jnp.maximum(jnp.max(strip, axis=-1, keepdims=True), LEAST))
            strip = jnp.exp2((strip - tops[-1]) * POWER)
            totals.append(jnp.sum(strip, axis=-1, keepdims=True))
            strips.append(strip.astype(jnp.bfloat16))
        top, total = jnp.concatenate(tops, axis=0), jnp.concatenate(totals, axis=0)
        out = lax.dot_general(
            jnp.concatenate(strips, axis=0),
            keys_ref[row, :latent],
            (((1,), (1,)), ((), ())),
            preferred_element_type=jnp.float32,
        )
        seen = total > 0.0
        safe = jnp.where(seen, total, 1.0)
        out = out * (1.0 / safe)
        stat = jnp.where(seen, top * POWER + jnp.log2(safe), HIDDEN)
        stat = jnp.broadcast_to(stat, (count, LANES)).reshape(peers, group, LANES)
        closed.append(out.reshape(peers, group, latent))
        stat = split_stat(stat, lane)
        packed = stat if packed is None else jnp.where(lane < row * STAT_LANES, packed, stat)
        if row % 2 == 1:
            both = jnp.concatenate(closed[-2:], axis=1).reshape(peers // 2, 2, sixteen, latent).astype(jnp.bfloat16)
            for member in range(2):
                for g in range(column_groups):
                    start = member * at + g * depth + row // 2 * sixteen
                    out_ref[:, start : start + sixteen, :] = both[:, member, :, g * LANES : (g + 1) * LANES]
    out_ref[:, 2 * at :, :] = packed.reshape(peers // 2, 2 * group, LANES).astype(jnp.bfloat16)


def attend(lengths, positions, own, came, query, new_count):
    peers = query.shape[0]
    rows = own.shape[0] // 2
    full, context = own.shape[1:]
    latent = full - ROPE
    depth = query.shape[1] * LANES // full
    group = depth // rows
    rows_out = 2 * (latent // LANES * depth + group)
    count = peers * group
    vmem, anywhere = (pl.BlockSpec(memory_space=space) for space in (pltpu.VMEM, pl.ANY))
    own, lengths, positions = (
        pltpu.with_memory_space_constraint(array, pltpu.HBM) for array in (own, lengths, positions)
    )
    return pl.pallas_call(
        functools.partial(attend_kernel, new_count=new_count),
        out_shape=pltpu.VMEM((peers // 2, rows_out, LANES), jnp.bfloat16),
        in_specs=[anywhere] * 4 + [vmem],
        out_specs=vmem,
        scratch_shapes=[
            pltpu.VMEM((rows, -(-full // LANES) * LANES, 2 * context), jnp.bfloat16),
            pltpu.SMEM(lengths.shape, jnp.int32),
            pltpu.SMEM(positions.shape, jnp.int32),
            pltpu.SemaphoreType.DMA((2 * rows,)),
            pltpu.SemaphoreType.DMA((2,)),
        ],
        compiler_params=pltpu.CompilerParams(vmem_limit_bytes=VMEM_LIMIT),
        cost_estimate=pl.CostEstimate(
            flops=4 * count * context * (full + latent) * rows,
            bytes_accessed=2 * rows * context * full * 2 + peers * rows_out * LANES,
            transcendentals=2 * rows * count * context,
        ),
        name="attend",
    )(lengths, positions, own, came, query)


def project_kernel(parts_ref, own_up_ref, came_up_ref, own_proj_ref, came_proj_ref, out_ref):
    sixteen = 16
    chips, rows_out, _ = parts_ref.shape
    peers = out_ref.shape[0]
    heads, wide, _ = own_up_ref.shape
    groups = wide // LANES
    at = rows_out - sixteen
    depth = at // 2 // groups
    width = out_ref.shape[2]
    step = 4
    core = lax.axis_index("core")
    flats = []
    for side, up_ref in enumerate((own_up_ref, came_up_ref)):
        member = core if side == 0 else 1 - core
        blocks = []
        stat_tiles = [parts_ref[k, at:, :].astype(jnp.float32) for k in range(chips)]
        stat_tiles = [jnp.where(member == 0, tile[: sixteen // 2], tile[sixteen // 2 :]) for tile in stat_tiles]
        for pair in range(2):
            stats = [
                jnp.concatenate([join_stat(tile, 2 * pair), join_stat(tile, 2 * pair + 1)], axis=0)
                for tile in stat_tiles
            ]
            top = functools.reduce(jnp.maximum, stats)
            weights = [jnp.exp2(stat - top) for stat in stats]
            scale = 1.0 / functools.reduce(jnp.add, weights)
            sums = []
            for g in range(groups):
                start = pl.multiple_of(member * (at // 2) + g * depth + pair * sixteen, sixteen)
                terms = [
                    parts_ref[k, pl.ds(start, sixteen), :].astype(jnp.float32) * weight
                    for k, weight in enumerate(weights)
                ]
                sums.append(functools.reduce(jnp.add, terms) * scale)
            blocks.append(jnp.concatenate(sums, axis=-1))
        latent = jnp.concatenate(blocks, axis=0).astype(jnp.bfloat16)
        count = latent.shape[0]
        out_row = lax.broadcasted_iota(jnp.int32, (count // heads, count), 0)
        in_row = lax.broadcasted_iota(jnp.int32, (count // heads, count), 1)
        values = []
        for head in range(heads):
            pick = jnp.where(in_row == out_row * heads + head, 1.0, 0.0).astype(jnp.bfloat16)
            chosen = jnp.dot(pick, latent, preferred_element_type=jnp.float32).astype(jnp.bfloat16)
            values.append(jnp.dot(chosen, up_ref[head], preferred_element_type=jnp.float32).astype(jnp.bfloat16))
        flats.append(jnp.concatenate(values, axis=-1))
    for first in range(0, peers, step):
        columns = slice(first * width, (first + step) * width)
        terms = jnp.dot(flats[0], own_proj_ref[:, columns], preferred_element_type=jnp.float32)
        terms += jnp.dot(flats[1], came_proj_ref[:, columns], preferred_element_type=jnp.float32)
        for k in range(step):
            out_ref[first + k] = terms[:, k * width : (k + 1) * width].astype(jnp.bfloat16)


def project(parts, own_up, came_up, own_proj, came_proj):
    chips, rows_out, _ = parts.shape
    peers = chips * 2
    heads, latent, _ = own_up.shape
    columns = own_proj.shape[1]
    tokens = (rows_out - 16) // 2 // (latent // LANES) // heads
    vmem = pl.BlockSpec(memory_space=pltpu.VMEM)
    return pl.pallas_call(
        project_kernel,
        out_shape=pltpu.VMEM((peers, tokens, columns // peers), jnp.bfloat16),
        in_specs=[vmem] * 5,
        out_specs=vmem,
        compiler_params=pltpu.CompilerParams(vmem_limit_bytes=16 * 1024 * 1024),
        name="project",
    )(parts, own_up, came_up, own_proj, came_proj)


def total_kernel(terms_ref, out_ref):
    rows, new_count, _ = out_ref.shape
    half = rows // 2
    for core in range(2):
        terms = [terms_ref[k].astype(jnp.float32) for k in range(core, terms_ref.shape[0], 2)]
        result = functools.reduce(jnp.add, terms).astype(jnp.bfloat16)
        for row in range(half):
            out_ref[core * half + row] = result[row * new_count : (row + 1) * new_count]


def total(terms, rows, new_count):
    vmem = pl.BlockSpec(memory_space=pltpu.VMEM)
    return pl.pallas_call(
        total_kernel,
        out_shape=jax.ShapeDtypeStruct((rows, new_count, terms.shape[2]), jnp.bfloat16),
        in_specs=[vmem],
        out_specs=vmem,
        compiler_params=pltpu.CompilerParams(vmem_limit_bytes=8 * 1024 * 1024),
        name="total",
    )(terms)


def body(latent_cache, queries, lengths, positions, value_up, out_proj):
    row_count, new_count = queries.shape[:2]
    peers = lax.axis_size("chip") * 2
    swap = [(0, 1), (1, 0)]
    cache = jnp.swapaxes(latent_cache, 1, 2)
    came = lax.ppermute(cache, "core", swap)
    query = lax.all_to_all(spread(queries, peers), ("chip", "core"), 0, 0, tiled=True)
    query, value_up, out_proj = lax.optimization_barrier((query, value_up, out_proj))
    came_up = lax.ppermute(value_up, "core", swap)
    came_proj = lax.ppermute(out_proj, "core", swap)
    mine = attend(lengths, positions, cache, came, query, new_count)
    mine, came_up, came_proj = lax.optimization_barrier((mine, came_up, came_proj))
    parts = lax.all_to_all(mine, "chip", 0, 0, tiled=True)
    terms = project(parts, value_up, came_up, out_proj, came_proj)
    terms = lax.all_to_all(terms, ("chip", "core"), 0, 0, tiled=True)
    return total(terms, row_count, new_count)


def solution(mesh):
    batch, ctx = mesh.devices.shape
    mesh = Mesh(mesh.devices.reshape(batch, ctx // 2, 2), ("batch", "chip", "core"))
    ctx = ("chip", "core")
    in_specs = (
        P("batch", ctx, None),
        P("batch", None, ctx, None),
        P("batch"),
        P("batch"),
        P(ctx, None, None),
        P(ctx, None),
    )
    out_specs = P("batch", None, ctx)
    return jax.shard_map(body, mesh=mesh, in_specs=in_specs, out_specs=out_specs, check_vma=False)
```

```python
import functools
import math

import jax
import jax.numpy as jnp
import numpy as np
from jax import lax
from jax.experimental import pallas as pl
from jax.experimental.pallas import tpu as pltpu
from jax.sharding import Mesh
from jax.sharding import PartitionSpec as P

ROPE = 64
NOPE = 128
LANES = 128
STAT_LANES = 32
POWER = math.log2(math.e) / math.sqrt(NOPE + ROPE)
HIDDEN = -1e30
STRIP = 16
VMEM_LIMIT = 24 * 1024 * 1024
LEAST = -1e29


def angles(positions, new_count, repeats):
    half_rope = ROPE // 2
    shape = (new_count * repeats, ROPE)
    lane = lax.broadcasted_iota(jnp.int32, shape, 1)
    frequency = jnp.zeros(shape, jnp.float32)
    for i in range(half_rope):
        value = float(np.float32(50000.0 ** (-2.0 * i / ROPE)))
        frequency = jnp.where(lane % half_rope == i, value, frequency)
    token = lax.broadcasted_iota(jnp.int32, shape, 0) // repeats
    terms = []
    for position in positions:
        angle = (position + token).astype(jnp.float32) * frequency
        sine = jnp.sin(angle)
        terms.append((jnp.cos(angle), jnp.where(lane < half_rope, -sine, sine)))
    return terms


def split_stat(value, lane):
    high = value.astype(jnp.bfloat16).astype(jnp.float32)
    rest = value - high
    middle = rest.astype(jnp.bfloat16).astype(jnp.float32)
    low = rest - middle
    spot = lane % STAT_LANES
    return jnp.where(spot == 0, high, jnp.where(spot == 1, middle, low))


def join_stat(tile, row):
    at = row * STAT_LANES
    return tile[..., at : at + 1] + tile[..., at + 1 : at + 2] + tile[..., at + 2 : at + 3]


def spread_kernel(query_ref, out_ref, flat_ref):
    rows, new_count, heads, full = query_ref.shape
    latent = full - ROPE
    for row in range(rows):
        for token in range(new_count):
            at = (row * new_count + token) * heads
            flat_ref[at : at + heads, :] = query_ref[row, token].astype(jnp.float32)
    flat = flat_ref[...]
    depth = flat.shape[0] // 2
    for half in range(2):
        mine = flat[half * depth : (half + 1) * depth]
        pieces = [mine[:, g : g + LANES] for g in range(0, latent, LANES)]
        pieces.append(jnp.concatenate([mine[: depth // 2, latent:], mine[depth // 2 :, latent:]], axis=-1))
        block = jnp.concatenate(pieces, axis=0).astype(jnp.bfloat16)
        for peer in range(half, out_ref.shape[0], 2):
            out_ref[peer] = block


def spread(queries, peers):
    rows, new_count, heads, full = queries.shape
    count = rows * new_count * heads
    vmem = pl.BlockSpec(memory_space=pltpu.VMEM)
    return pl.pallas_call(
        spread_kernel,
        out_shape=pltpu.VMEM((peers, count // 2 * full // LANES, LANES), jnp.bfloat16),
        in_specs=[vmem],
        out_specs=vmem,
        scratch_shapes=[pltpu.VMEM((count, full), jnp.float32)],
        compiler_params=pltpu.CompilerParams(vmem_limit_bytes=8 * 1024 * 1024),
        name="spread",
    )(queries)


def attend_kernel(
    far_lengths_ref, far_positions_ref, own_ref, came_ref, query_ref, out_ref, keys_ref, lengths_ref, positions_ref, arrived, told, *, new_count
):
    peers = query_ref.shape[0]
    full = own_ref.shape[1]
    rows, wide, context = keys_ref.shape
    span = context // 2
    latent = full - ROPE
    column_groups = latent // LANES
    depth = query_ref.shape[1] * LANES // full
    group = depth // rows
    heads = group // new_count
    count = peers * group
    core = lax.axis_index("core")
    base = core * rows
    starts = [(lax.axis_index("chip") * 2 + place) * span for place in (core, 1 - core)]
    scalars = [
        pltpu.make_async_copy(far_lengths_ref, lengths_ref, told.at[0]),
        pltpu.make_async_copy(far_positions_ref, positions_ref, told.at[1]),
    ]
    for copy in scalars:
        copy.start()
    copies = []
    for row in range(rows):
        for side, ref in enumerate((own_ref, came_ref)):
            target = keys_ref.at[row, pl.ds(0, full), pl.ds(side * span, span)]
            copies.append(pltpu.make_async_copy(ref.at[base + row], target, arrived.at[row * 2 + side]))
    for copy in copies:
        copy.start()
    spare = wide - full
    column = lax.broadcasted_iota(jnp.int32, (peers, group, spare), 2)
    member = lax.broadcasted_iota(jnp.int32, (peers, group, spare), 1)
    flags = jnp.where(column == member // heads, 1.0, 0.0)
    place = lax.broadcasted_iota(jnp.int32, (spare, span), 1)
    token = lax.broadcasted_iota(jnp.int32, (spare, span), 0)
    latents, ropes = [], []
    for row in range(rows):
        tile, upper = row // 2 * 2 * group, slice(row % 2 * group, (row % 2 + 1) * group)
        for g in range(column_groups):
            piece = query_ref[:, g * depth + tile : g * depth + tile + 2 * group, :].astype(jnp.float32)
            latents.append(piece[:, upper])
        rope = query_ref[:, column_groups * depth :, :].astype(jnp.float32)
        ropes.append(rope[:, upper, row // 2 * ROPE : (row // 2 + 1) * ROPE])
    for copy in scalars:
        copy.wait()
    turns = angles([positions_ref[base + row] for row in range(rows)], new_count, heads)
    queries = []
    for row in range(rows):
        for side in range(2):
            limit = lengths_ref[base + row] - new_count + 1 - starts[side]
            hidden = (token < new_count) & (place >= limit + token)
            keys_ref[row, full:, side * span : (side + 1) * span] = jnp.where(hidden, HIDDEN, 0.0).astype(jnp.bfloat16)
        rope = ropes[row]
        swapped = jnp.concatenate([rope[:, :, ROPE // 2 :], rope[:, :, : ROPE // 2]], axis=-1)
        turned = rope * turns[row][0][None] + swapped * turns[row][1][None]
        pieces = latents[row * column_groups : (row + 1) * column_groups]
        query = jnp.concatenate([*pieces, turned, flags], axis=-1)
        queries.append(query.reshape(count, wide).astype(jnp.bfloat16))

    def score(row):
        if row > 0:
            copies[2 * row].wait()
            copies[2 * row + 1].wait()
            return jnp.dot(queries[row], keys_ref[row], preferred_element_type=jnp.float32)
        halves = []
        for side in range(2):
            copies[side].wait()
            keys = keys_ref[row, :, side * span : (side + 1) * span]
            halves.append(jnp.dot(queries[row], keys, preferred_element_type=jnp.float32))
        return jnp.concatenate(halves, axis=-1)

    sixteen = 2 * group
    at = column_groups * depth
    closed, packed = [], None
    lane = lax.broadcasted_iota(jnp.int32, (peers, group, LANES), 2)
    ahead = score(0)
    for row in range(rows):
        scores = ahead
        if row + 1 < rows:
            ahead = score(row + 1)
        tops, totals, strips = [], [], []
        for first in range(0, count, STRIP):
            strip = scores[first : first + STRIP]
            tops.append(jnp.maximum(jnp.max(strip, axis=-1, keepdims=True), LEAST))
            strip = jnp.exp2((strip - tops[-1]) * POWER)
            totals.append(jnp.sum(strip, axis=-1, keepdims=True))
            strips.append(strip.astype(jnp.bfloat16))
        top, total = jnp.concatenate(tops, axis=0), jnp.concatenate(totals, axis=0)
        out = lax.dot_general(
            jnp.concatenate(strips, axis=0),
            keys_ref[row, :latent],
            (((1,), (1,)), ((), ())),
            preferred_element_type=jnp.float32,
        )
        seen = total > 0.0
        safe = jnp.where(seen, total, 1.0)
        out = out * (1.0 / safe)
        stat = jnp.where(seen, top * POWER + jnp.log2(safe), HIDDEN)
        stat = jnp.broadcast_to(stat, (count, LANES)).reshape(peers, group, LANES)
        closed.append(out.reshape(peers, group, latent))
        stat = split_stat(stat, lane)
        packed = stat if packed is None else jnp.where(lane < row * STAT_LANES, packed, stat)
        if row % 2 == 1:
            both = jnp.concatenate(closed[-2:], axis=1).reshape(peers // 2, 2, sixteen, latent).astype(jnp.bfloat16)
            for member in range(2):
                for g in range(column_groups):
                    start = member * at + g * depth + row // 2 * sixteen
                    out_ref[:, start : start + sixteen, :] = both[:, member, :, g * LANES : (g + 1) * LANES]
    out_ref[:, 2 * at :, :] = packed.reshape(peers // 2, 2 * group, LANES).astype(jnp.bfloat16)


def attend(lengths, positions, own, came, query, new_count):
    peers = query.shape[0]
    rows = own.shape[0] // 2
    full, context = own.shape[1:]
    latent = full - ROPE
    depth = query.shape[1] * LANES // full
    group = depth // rows
    rows_out = 2 * (latent // LANES * depth + group)
    count = peers * group
    vmem, anywhere = (pl.BlockSpec(memory_space=space) for space in (pltpu.VMEM, pl.ANY))
    own, lengths, positions = (
        pltpu.with_memory_space_constraint(array, pltpu.HBM) for array in (own, lengths, positions)
    )
    return pl.pallas_call(
        functools.partial(attend_kernel, new_count=new_count),
        out_shape=pltpu.VMEM((peers // 2, rows_out, LANES), jnp.bfloat16),
        in_specs=[anywhere] * 4 + [vmem],
        out_specs=vmem,
        scratch_shapes=[
            pltpu.VMEM((rows, -(-full // LANES) * LANES, 2 * context), jnp.bfloat16),
            pltpu.SMEM(lengths.shape, jnp.int32),
            pltpu.SMEM(positions.shape, jnp.int32),
            pltpu.SemaphoreType.DMA((2 * rows,)),
            pltpu.SemaphoreType.DMA((2,)),
        ],
        compiler_params=pltpu.CompilerParams(vmem_limit_bytes=VMEM_LIMIT),
        cost_estimate=pl.CostEstimate(
            flops=4 * count * context * (full + latent) * rows,
            bytes_accessed=2 * rows * context * full * 2 + peers * rows_out * LANES,
            transcendentals=2 * rows * count * context,
        ),
        name="attend",
    )(lengths, positions, own, came, query)


def project_kernel(parts_ref, own_up_ref, came_up_ref, own_proj_ref, came_proj_ref, out_ref):
    sixteen = 16
    chips, rows_out, _ = parts_ref.shape
    peers = out_ref.shape[0]
    heads, wide, _ = own_up_ref.shape
    groups = wide // LANES
    at = rows_out - sixteen
    depth = at // 2 // groups
    width = out_ref.shape[2]
    step = 4
    core = lax.axis_index("core")
    flats = []
    for side, up_ref in enumerate((own_up_ref, came_up_ref)):
        member = core if side == 0 else 1 - core
        blocks = []
        stat_tiles = [parts_ref[k, at:, :].astype(jnp.float32) for k in range(chips)]
        stat_tiles = [jnp.where(member == 0, tile[: sixteen // 2], tile[sixteen // 2 :]) for tile in stat_tiles]
        for pair in range(2):
            stats = [
                jnp.concatenate([join_stat(tile, 2 * pair), join_stat(tile, 2 * pair + 1)], axis=0)
                for tile in stat_tiles
            ]
            top = functools.reduce(jnp.maximum, stats)
            weights = [jnp.exp2(stat - top) for stat in stats]
            scale = 1.0 / functools.reduce(jnp.add, weights)
            sums = []
            for g in range(groups):
                start = pl.multiple_of(member * (at // 2) + g * depth + pair * sixteen, sixteen)
                terms = [
                    parts_ref[k, pl.ds(start, sixteen), :].astype(jnp.float32) * weight
                    for k, weight in enumerate(weights)
                ]
                sums.append(functools.reduce(jnp.add, terms) * scale)
            blocks.append(jnp.concatenate(sums, axis=-1))
        latent = jnp.concatenate(blocks, axis=0).astype(jnp.bfloat16)
        count = latent.shape[0]
        out_row = lax.broadcasted_iota(jnp.int32, (count // heads, count), 0)
        in_row = lax.broadcasted_iota(jnp.int32, (count // heads, count), 1)
        values = []
        for head in range(heads):
            pick = jnp.where(in_row == out_row * heads + head, 1.0, 0.0).astype(jnp.bfloat16)
            chosen = jnp.dot(pick, latent, preferred_element_type=jnp.float32).astype(jnp.bfloat16)
            values.append(jnp.dot(chosen, up_ref[head], preferred_element_type=jnp.float32).astype(jnp.bfloat16))
        flats.append(jnp.concatenate(values, axis=-1))
    for first in range(0, peers, step):
        columns = slice(first * width, (first + step) * width)
        terms = jnp.dot(flats[0], own_proj_ref[:, columns], preferred_element_type=jnp.float32)
        terms += jnp.dot(flats[1], came_proj_ref[:, columns], preferred_element_type=jnp.float32)
        for k in range(step):
            out_ref[first + k] = terms[:, k * width : (k + 1) * width].astype(jnp.bfloat16)


def project(parts, own_up, came_up, own_proj, came_proj):
    chips, rows_out, _ = parts.shape
    peers = chips * 2
    heads, latent, _ = own_up.shape
    columns = own_proj.shape[1]
    tokens = (rows_out - 16) // 2 // (latent // LANES) // heads
    vmem = pl.BlockSpec(memory_space=pltpu.VMEM)
    return pl.pallas_call(
        project_kernel,
        out_shape=pltpu.VMEM((peers, tokens, columns // peers), jnp.bfloat16),
        in_specs=[vmem] * 5,
        out_specs=vmem,
        compiler_params=pltpu.CompilerParams(vmem_limit_bytes=16 * 1024 * 1024),
        name="project",
    )(parts, own_up, came_up, own_proj, came_proj)


def total_kernel(terms_ref, out_ref):
    rows, new_count, _ = out_ref.shape
    half = rows // 2
    for core in range(2):
        terms = [terms_ref[k].astype(jnp.float32) for k in range(core, terms_ref.shape[0], 2)]
        result = functools.reduce(jnp.add, terms).astype(jnp.bfloat16)
        for row in range(half):
            out_ref[core * half + row] = result[row * new_count : (row + 1) * new_count]


def total(terms, rows, new_count):
    vmem = pl.BlockSpec(memory_space=pltpu.VMEM)
    return pl.pallas_call(
        total_kernel,
        out_shape=jax.ShapeDtypeStruct((rows, new_count, terms.shape[2]), jnp.bfloat16),
        in_specs=[vmem],
        out_specs=vmem,
        compiler_params=pltpu.CompilerParams(vmem_limit_bytes=8 * 1024 * 1024),
        name="total",
    )(terms)


def body(latent_cache, queries, lengths, positions, value_up, out_proj):
    row_count, new_count = queries.shape[:2]
    peers = lax.axis_size("chip") * 2
    swap = [(0, 1), (1, 0)]
    cache = jnp.swapaxes(latent_cache, 1, 2)
    came = lax.ppermute(cache, "core", swap)
    query = lax.all_to_all(spread(queries, peers), ("chip", "core"), 0, 0, tiled=True)
    query, value_up, out_proj = lax.optimization_barrier((query, value_up, out_proj))
    came_up = lax.ppermute(value_up, "core", swap)
    came_proj = lax.ppermute(out_proj, "core", swap)
    mine = attend(lengths, positions, cache, came, query, new_count)
    mine, came_up, came_proj = lax.optimization_barrier((mine, came_up, came_proj))
    parts = lax.all_to_all(mine, "chip", 0, 0, tiled=True)
    terms = project(parts, value_up, came_up, out_proj, came_proj)
    terms = lax.all_to_all(terms, ("chip", "core"), 0, 0, tiled=True)
    return total(terms, row_count, new_count)


def solution(mesh):
    batch, ctx = mesh.devices.shape
    mesh = Mesh(mesh.devices.reshape(batch, ctx // 2, 2), ("batch", "chip", "core"))
    ctx = ("chip", "core")
    in_specs = (
        P("batch", ctx, None),
        P("batch", None, ctx, None),
        P("batch"),
        P("batch"),
        P(ctx, None, None),
        P(ctx, None),
    )
    out_specs = P("batch", None, ctx)
    return jax.shard_map(body, mesh=mesh, in_specs=in_specs, out_specs=out_specs, check_vma=False)
```

```python
import functools
import math

import jax
import jax.numpy as jnp
import numpy as np
from jax import lax
from jax.experimental import pallas as pl
from jax.experimental.pallas import tpu as pltpu
from jax.sharding import Mesh
from jax.sharding import PartitionSpec as P

ROPE = 64
NOPE = 128
LANES = 128
STAT_LANES = 32
POWER = math.log2(math.e) / math.sqrt(NOPE + ROPE)
HIDDEN = -1e30
STRIP = 16
VMEM_LIMIT = 24 * 1024 * 1024
LEAST = -1e29


def angles(positions, new_count, repeats):
    half_rope = ROPE // 2
    shape = (new_count * repeats, ROPE)
    lane = lax.broadcasted_iota(jnp.int32, shape, 1)
    frequency = jnp.zeros(shape, jnp.float32)
    for i in range(half_rope):
        value = float(np.float32(50000.0 ** (-2.0 * i / ROPE)))
        frequency = jnp.where(lane % half_rope == i, value, frequency)
    token = lax.broadcasted_iota(jnp.int32, shape, 0) // repeats
    terms = []
    for position in positions:
        angle = (position + token).astype(jnp.float32) * frequency
        sine = jnp.sin(angle)
        terms.append((jnp.cos(angle), jnp.where(lane < half_rope, -sine, sine)))
    return terms


def split_stat(value, lane):
    high = value.astype(jnp.bfloat16).astype(jnp.float32)
    rest = value - high
    middle = rest.astype(jnp.bfloat16).astype(jnp.float32)
    low = rest - middle
    spot = lane % STAT_LANES
    return jnp.where(spot == 0, high, jnp.where(spot == 1, middle, low))


def join_stat(tile, row):
    at = row * STAT_LANES
    return tile[..., at : at + 1] + tile[..., at + 1 : at + 2] + tile[..., at + 2 : at + 3]


def spread_kernel(query_ref, out_ref, flat_ref):
    rows, new_count, heads, full = query_ref.shape
    latent = full - ROPE
    for row in range(rows):
        for token in range(new_count):
            at = (row * new_count + token) * heads
            flat_ref[at : at + heads, :] = query_ref[row, token].astype(jnp.float32)
    flat = flat_ref[...]
    depth = flat.shape[0] // 2
    for half in range(2):
        mine = flat[half * depth : (half + 1) * depth]
        pieces = [mine[:, g : g + LANES] for g in range(0, latent, LANES)]
        pieces.append(jnp.concatenate([mine[: depth // 2, latent:], mine[depth // 2 :, latent:]], axis=-1))
        block = jnp.concatenate(pieces, axis=0).astype(jnp.bfloat16)
        for peer in range(half, out_ref.shape[0], 2):
            out_ref[peer] = block


def spread(queries, peers):
    rows, new_count, heads, full = queries.shape
    count = rows * new_count * heads
    vmem = pl.BlockSpec(memory_space=pltpu.VMEM)
    return pl.pallas_call(
        spread_kernel,
        out_shape=pltpu.VMEM((peers, count // 2 * full // LANES, LANES), jnp.bfloat16),
        in_specs=[vmem],
        out_specs=vmem,
        scratch_shapes=[pltpu.VMEM((count, full), jnp.float32)],
        compiler_params=pltpu.CompilerParams(vmem_limit_bytes=8 * 1024 * 1024),
        name="spread",
    )(queries)


def attend_kernel(
    far_lengths_ref, far_positions_ref, own_ref, came_ref, query_ref, out_ref, keys_ref, lengths_ref, positions_ref, arrived, told, *, new_count
):
    peers = query_ref.shape[0]
    full = own_ref.shape[1]
    rows, wide, context = keys_ref.shape
    span = context // 2
    latent = full - ROPE
    column_groups = latent // LANES
    depth = query_ref.shape[1] * LANES // full
    group = depth // rows
    heads = group // new_count
    count = peers * group
    core = lax.axis_index("core")
    base = core * rows
    starts = [(lax.axis_index("chip") * 2 + place) * span for place in (core, 1 - core)]
    scalars = [
        pltpu.make_async_copy(far_lengths_ref, lengths_ref, told.at[0]),
        pltpu.make_async_copy(far_positions_ref, positions_ref, told.at[1]),
    ]
    for copy in scalars:
        copy.start()
    copies = []
    for row in range(rows):
        for side, ref in enumerate((own_ref, came_ref)):
            target = keys_ref.at[row, pl.ds(0, full), pl.ds(side * span, span)]
            copies.append(pltpu.make_async_copy(ref.at[base + row], target, arrived.at[row * 2 + side]))
    for copy in copies:
        copy.start()
    spare = wide - full
    column = lax.broadcasted_iota(jnp.int32, (peers, group, spare), 2)
    member = lax.broadcasted_iota(jnp.int32, (peers, group, spare), 1)
    flags = jnp.where(column == member // heads, 1.0, 0.0)
    place = lax.broadcasted_iota(jnp.int32, (spare, span), 1)
    token = lax.broadcasted_iota(jnp.int32, (spare, span), 0)
    latents, ropes = [], []
    for row in range(rows):
        tile, upper = row // 2 * 2 * group, slice(row % 2 * group, (row % 2 + 1) * group)
        for g in range(column_groups):
            piece = query_ref[:, g * depth + tile : g * depth + tile + 2 * group, :].astype(jnp.float32)
            latents.append(piece[:, upper])
        rope = query_ref[:, column_groups * depth :, :].astype(jnp.float32)
        ropes.append(rope[:, upper, row // 2 * ROPE : (row // 2 + 1) * ROPE])
    for copy in scalars:
        copy.wait()
    turns = angles([positions_ref[base + row] for row in range(rows)], new_count, heads)
    queries = []
    for row in range(rows):
        for side in range(2):
            limit = lengths_ref[base + row] - new_count + 1 - starts[side]
            hidden = (token < new_count) & (place >= limit + token)
            keys_ref[row, full:, side * span : (side + 1) * span] = jnp.where(hidden, HIDDEN, 0.0).astype(jnp.bfloat16)
        rope = ropes[row]
        swapped = jnp.concatenate([rope[:, :, ROPE // 2 :], rope[:, :, : ROPE // 2]], axis=-1)
        turned = rope * turns[row][0][None] + swapped * turns[row][1][None]
        pieces = latents[row * column_groups : (row + 1) * column_groups]
        query = jnp.concatenate([*pieces, turned, flags], axis=-1)
        queries.append(query.reshape(count, wide).astype(jnp.bfloat16))

    def score(row):
        copies[2 * row].wait()
        copies[2 * row + 1].wait()
        scores = jnp.dot(queries[row], keys_ref[row], preferred_element_type=jnp.float32)
        return scores

    sixteen = 2 * group
    at = column_groups * depth
    closed, packed = [], None
    lane = lax.broadcasted_iota(jnp.int32, (peers, group, LANES), 2)
    ahead = score(0)
    for row in range(rows):
        scores = ahead
        if row + 1 < rows:
            ahead = score(row + 1)
        tops, totals, strips = [], [], []
        for first in range(0, count, STRIP):
            strip = scores[first : first + STRIP]
            tops.append(jnp.maximum(jnp.max(strip, axis=-1, keepdims=True), LEAST))
            strip = jnp.exp2((strip - tops[-1]) * POWER)
            totals.append(jnp.sum(strip, axis=-1, keepdims=True))
            strips.append(strip.astype(jnp.bfloat16))
        top, total = jnp.concatenate(tops, axis=0), jnp.concatenate(totals, axis=0)
        out = lax.dot_general(
            jnp.concatenate(strips, axis=0),
            keys_ref[row, :latent],
            (((1,), (1,)), ((), ())),
            preferred_element_type=jnp.float32,
        )
        seen = total > 0.0
        safe = jnp.where(seen, total, 1.0)
        out = out * (1.0 / safe)
        stat = jnp.where(seen, top * POWER + jnp.log2(safe), HIDDEN)
        stat = jnp.broadcast_to(stat, (count, LANES)).reshape(peers, group, LANES)
        closed.append(out.reshape(peers, group, latent))
        stat = split_stat(stat, lane)
        packed = stat if packed is None else jnp.where(lane < row * STAT_LANES, packed, stat)
        if row % 2 == 1:
            both = jnp.concatenate(closed[-2:], axis=1).reshape(peers // 2, 2, sixteen, latent).astype(jnp.bfloat16)
            for member in range(2):
                for g in range(column_groups):
                    start = member * at + g * depth + row // 2 * sixteen
                    out_ref[:, start : start + sixteen, :] = both[:, member, :, g * LANES : (g + 1) * LANES]
    out_ref[:, 2 * at :, :] = packed.reshape(peers // 2, 2 * group, LANES).astype(jnp.bfloat16)


def attend(lengths, positions, own, came, query, new_count):
    peers = query.shape[0]
    rows = own.shape[0] // 2
    full, context = own.shape[1:]
    latent = full - ROPE
    depth = query.shape[1] * LANES // full
    group = depth // rows
    rows_out = 2 * (latent // LANES * depth + group)
    count = peers * group
    vmem, anywhere = (pl.BlockSpec(memory_space=space) for space in (pltpu.VMEM, pl.ANY))
    own, lengths, positions = (
        pltpu.with_memory_space_constraint(array, pltpu.HBM) for array in (own, lengths, positions)
    )
    return pl.pallas_call(
        functools.partial(attend_kernel, new_count=new_count),
        out_shape=pltpu.VMEM((peers // 2, rows_out, LANES), jnp.bfloat16),
        in_specs=[anywhere] * 4 + [vmem],
        out_specs=vmem,
        scratch_shapes=[
            pltpu.VMEM((rows, -(-full // LANES) * LANES, 2 * context), jnp.bfloat16),
            pltpu.SMEM(lengths.shape, jnp.int32),
            pltpu.SMEM(positions.shape, jnp.int32),
            pltpu.SemaphoreType.DMA((2 * rows,)),
            pltpu.SemaphoreType.DMA((2,)),
        ],
        compiler_params=pltpu.CompilerParams(vmem_limit_bytes=VMEM_LIMIT),
        cost_estimate=pl.CostEstimate(
            flops=4 * count * context * (full + latent) * rows,
            bytes_accessed=2 * rows * context * full * 2 + peers * rows_out * LANES,
            transcendentals=2 * rows * count * context,
        ),
        name="attend",
    )(lengths, positions, own, came, query)


def project_kernel(parts_ref, own_up_ref, came_up_ref, own_proj_ref, came_proj_ref, out_ref):
    sixteen = 16
    chips, rows_out, _ = parts_ref.shape
    peers = out_ref.shape[0]
    heads, wide, _ = own_up_ref.shape
    groups = wide // LANES
    at = rows_out - sixteen
    depth = at // 2 // groups
    width = out_ref.shape[2]
    step = 4
    core = lax.axis_index("core")
    flats = []
    for side, up_ref in enumerate((own_up_ref, came_up_ref)):
        member = core if side == 0 else 1 - core
        blocks = []
        stat_tiles = [parts_ref[k, at:, :].astype(jnp.float32) for k in range(chips)]
        stat_tiles = [jnp.where(member == 0, tile[: sixteen // 2], tile[sixteen // 2 :]) for tile in stat_tiles]
        for pair in range(2):
            stats = [
                jnp.concatenate([join_stat(tile, 2 * pair), join_stat(tile, 2 * pair + 1)], axis=0)
                for tile in stat_tiles
            ]
            top = functools.reduce(jnp.maximum, stats)
            weights = [jnp.exp2(stat - top) for stat in stats]
            scale = 1.0 / functools.reduce(jnp.add, weights)
            sums = []
            for g in range(groups):
                start = pl.multiple_of(member * (at // 2) + g * depth + pair * sixteen, sixteen)
                terms = [
                    parts_ref[k, pl.ds(start, sixteen), :].astype(jnp.float32) * weight
                    for k, weight in enumerate(weights)
                ]
                sums.append(functools.reduce(jnp.add, terms) * scale)
            blocks.append(jnp.concatenate(sums, axis=-1))
        latent = jnp.concatenate(blocks, axis=0).astype(jnp.bfloat16)
        count = latent.shape[0]
        out_row = lax.broadcasted_iota(jnp.int32, (count // heads, count), 0)
        in_row = lax.broadcasted_iota(jnp.int32, (count // heads, count), 1)
        values = []
        for head in range(heads):
            pick = jnp.where(in_row == out_row * heads + head, 1.0, 0.0).astype(jnp.bfloat16)
            chosen = jnp.dot(pick, latent, preferred_element_type=jnp.float32).astype(jnp.bfloat16)
            values.append(jnp.dot(chosen, up_ref[head], preferred_element_type=jnp.float32).astype(jnp.bfloat16))
        flats.append(jnp.concatenate(values, axis=-1))
    for first in range(0, peers, step):
        columns = slice(first * width, (first + step) * width)
        terms = jnp.dot(flats[0], own_proj_ref[:, columns], preferred_element_type=jnp.float32)
        terms += jnp.dot(flats[1], came_proj_ref[:, columns], preferred_element_type=jnp.float32)
        for k in range(step):
            out_ref[first + k] = terms[:, k * width : (k + 1) * width].astype(jnp.bfloat16)


def project(parts, own_up, came_up, own_proj, came_proj):
    chips, rows_out, _ = parts.shape
    peers = chips * 2
    heads, latent, _ = own_up.shape
    columns = own_proj.shape[1]
    tokens = (rows_out - 16) // 2 // (latent // LANES) // heads
    vmem = pl.BlockSpec(memory_space=pltpu.VMEM)
    return pl.pallas_call(
        project_kernel,
        out_shape=pltpu.VMEM((peers, tokens, columns // peers), jnp.bfloat16),
        in_specs=[vmem] * 5,
        out_specs=vmem,
        compiler_params=pltpu.CompilerParams(vmem_limit_bytes=16 * 1024 * 1024),
        name="project",
    )(parts, own_up, came_up, own_proj, came_proj)


def total_kernel(terms_ref, out_ref):
    rows, new_count, _ = out_ref.shape
    half = rows // 2
    for core in range(2):
        terms = [terms_ref[k].astype(jnp.float32) for k in range(core, terms_ref.shape[0], 2)]
        result = functools.reduce(jnp.add, terms).astype(jnp.bfloat16)
        for row in range(half):
            out_ref[core * half + row] = result[row * new_count : (row + 1) * new_count]


def total(terms, rows, new_count):
    vmem = pl.BlockSpec(memory_space=pltpu.VMEM)
    return pl.pallas_call(
        total_kernel,
        out_shape=jax.ShapeDtypeStruct((rows, new_count, terms.shape[2]), jnp.bfloat16),
        in_specs=[vmem],
        out_specs=vmem,
        compiler_params=pltpu.CompilerParams(vmem_limit_bytes=8 * 1024 * 1024),
        name="total",
    )(terms)


def body(latent_cache, queries, lengths, positions, value_up, out_proj):
    row_count, new_count = queries.shape[:2]
    peers = lax.axis_size("chip") * 2
    swap = [(0, 1), (1, 0)]
    cache = jnp.swapaxes(latent_cache, 1, 2)
    came = lax.ppermute(cache, "core", swap)
    query = lax.all_to_all(spread(queries, peers), ("chip", "core"), 0, 0, tiled=True)
    mine = attend(lengths, positions, cache, came, query, new_count)
    mine, value_up, out_proj = lax.optimization_barrier((mine, value_up, out_proj))
    came_up = lax.ppermute(value_up, "core", swap)
    came_proj = lax.ppermute(out_proj, "core", swap)
    parts = lax.all_to_all(mine, "chip", 0, 0, tiled=True)
    terms = project(parts, value_up, came_up, out_proj, came_proj)
    terms = lax.all_to_all(terms, ("chip", "core"), 0, 0, tiled=True)
    return total(terms, row_count, new_count)


def solution(mesh):
    batch, ctx = mesh.devices.shape
    mesh = Mesh(mesh.devices.reshape(batch, ctx // 2, 2), ("batch", "chip", "core"))
    ctx = ("chip", "core")
    in_specs = (
        P("batch", ctx, None),
        P("batch", None, ctx, None),
        P("batch"),
        P("batch"),
        P(ctx, None, None),
        P(ctx, None),
    )
    out_specs = P("batch", None, ctx)
    return jax.shard_map(body, mesh=mesh, in_specs=in_specs, out_specs=out_specs, check_vma=False)
```
